32 devices in a mesh: dp: 8 (over y, x, core), tensor: 4 (over z).
Axes of the slice: x: 2, y: 2, z: 4, core: 2. Of those that a mesh axis runs over, the one named last changes fastest.
Arguments:
- hidden: bfloat16 [16384, 768], P(('dp', 'tensor')), may hold values from -6 to 6
- page_boxes: int32 [16384, 4], P(('dp', 'tensor')), may hold values from 0 to 1000
- lengths: int32 [32], P('dp'), may hold values from 128 to 512
- table_x: bfloat16 [1024, 768], replicated, may hold values from -3 to 3
- table_y: bfloat16 [1024, 768], replicated, may hold values from -3 to 3
- in_weight: bfloat16 [3, 768, 768], P(None, None, 'tensor'), may hold values from -0.21875 to 0.21875
- in_bias: float32 [2, 768], P(None, 'tensor'), may hold values from -0.6 to 0.6
- out_weight: bfloat16 [768, 768], P('tensor'), may hold values from -1.25 to 1.25
- out_bias: float32 [768], replicated, may hold values from -1.5 to 1.5
- up_weight: bfloat16 [768, 3072], P(None, 'tensor'), may hold values from -0.21875 to 0.21875
- up_bias: float32 [3072], P('tensor'), may hold values from -1.5 to 1.5
- down_weight: bfloat16 [3072, 768], P('tensor'), may hold values from -0.109375 to 0.109375
- down_bias: float32 [768], replicated, may hold values from -1.5 to 1.5
- norm_gain: float32 [2, 768], replicated, may hold values from 0.25 to 1.75
- norm_bias: float32 [2, 768], replicated, may hold values from -1.5 to 1.5
- cotangent: bfloat16 [16384, 768], P(('dp', 'tensor')), may hold values from -6 to 6
Outputs:
- layer_out: bfloat16 [16384, 768], P(('dp', 'tensor'))
- grad_hidden: float32 [16384, 768], P(('dp', 'tensor'))
- grad_table_x: float32 [1024, 768], replicated
- grad_table_y: float32 [1024, 768], replicated
- grad_in_weight: float32 [3, 768, 768], P(None, None, 'tensor')
- grad_in_bias: float32 [2, 768], P(None, 'tensor')
- grad_out_weight: float32 [768, 768], P('tensor')
- grad_out_bias: float32 [768], replicated
- grad_up_weight: float32 [768, 3072], P(None, 'tensor')
- grad_up_bias: float32 [3072], P('tensor')
- grad_down_weight: float32 [3072, 768], P('tensor')
- grad_down_bias: float32 [768], replicated
- grad_norm_gain: float32 [2, 768], replicated
- grad_norm_bias: float32 [2, 768], replicated
The draws below stay inside these ranges and needn't reach their ends.
All inputs are finite; a program needn't handle non-finite values.
Results may differ from the reference program's by a relative error of at most 0.02.
The reference program's roundings to bfloat16 on the way count: a program that leaves them out, or rounds other values in their place, can miss the bound.
Values may be sent and summed in bfloat16 or wider, within the bound.
A program may use at most 128 MiB of HBM per device.

```python
from functools import partial
import jax
import jax.numpy as jnp
from jax import lax

D = 768
HEADS = 12
HEAD = 64
FF = 3072
GRID = 1024
PAGE = 512
PAGES_DEV = 4
PAGES = 32
TOKENS = 16384


def place_ends(values, rng, least, largest):
    place = [jax.random.randint(jax.random.fold_in(rng, axis), (), 0, length) for axis, length in enumerate(values.shape)]
    longest = values.shape.index(max(values.shape))
    beside = place[:longest] + [(place[longest] + 1) % values.shape[longest]] + place[longest + 1:]
    return values.at[tuple(place)].set(least).at[tuple(beside)].set(largest)


def steps_of(key, extent, split, smallest, top_value):
    level, own = 1.0, jax.random.fold_in(key, 6)
    for position, parts in split:
        steps = jnp.exp(jax.random.uniform(jax.random.fold_in(own, position), (parts,), jnp.float32, smallest / len(split), top_value / len(split)))
        level = level * jnp.repeat(steps, extent[position] // parts).reshape([-1 if axis == position else 1 for axis in range(len(extent))])
    return level


def centred(key, dims, scale, reach, shards=(), kind=jnp.bfloat16):
    gain = steps_of(key, dims, shards, -0.22, 0.18) if shards else 1.0
    values = jax.random.normal(key, dims, jnp.float32) * scale * gain
    return jnp.minimum(jnp.maximum(values, -reach), reach).astype(kind)


def setup_inputs(seed: int = 0) -> dict:
    key_of = jax.random.split(jax.random.key(seed), 17)
    hidden = centred(key_of[0], (TOKENS, D), 1.0, 6.0, ((0, 32),))
    page_boxes = place_ends(jax.random.randint(key_of[1], (TOKENS, 4), 0, min(1001, GRID)), jax.random.fold_in(key_of[1], 1), 0, (min(1001, GRID)) - 1).astype(jnp.int32)
    lengths = place_ends(jax.random.randint(key_of[2], (PAGES,), PAGE // 4, PAGE + 1), jax.random.fold_in(key_of[2], 1), PAGE // 4, PAGE).astype(jnp.int32)
    table_x = centred(key_of[3], (GRID, D), 0.5, 3.0)
    table_y = centred(key_of[4], (GRID, D), 0.5, 3.0)
    in_weight = centred(key_of[5], (3, D, D), D ** -0.5, 0.21875, ((2, 4),))
    in_bias = centred(key_of[6], (2, D), 0.1, 0.6, ((1, 4),), jnp.float32)
    out_weight = centred(key_of[7], (D, D), (D * 16 // PAGE) ** -0.5, 1.25, ((0, 4),))
    out_bias = centred(key_of[8], (D,), 0.3, 1.5, (), jnp.float32)
    up_weight = centred(key_of[9], (D, FF), D ** -0.5, 0.21875, ((1, 4),))
    up_bias = centred(key_of[10], (FF,), 0.3, 1.5, ((0, 4),), jnp.float32)
    down_weight = centred(key_of[11], (FF, D), FF ** -0.5, 0.109375, ((0, 4),))
    down_bias = centred(key_of[12], (D,), 0.3, 1.5, (), jnp.float32)
    norm_gain = jnp.clip(1.0 + 0.15 * jax.random.normal(key_of[13], (2, D), jnp.float32), 0.25, 1.75)
    norm_bias = centred(key_of[14], (2, D), 0.3, 1.5, (), jnp.float32)
    cotangent = centred(key_of[15], (TOKENS, D), 1.0, 6.0, ((0, 32),))
    return dict(hidden=hidden, page_boxes=page_boxes, lengths=lengths, table_x=table_x, table_y=table_y, in_weight=in_weight, in_bias=in_bias, out_weight=out_weight, out_bias=out_bias, up_weight=up_weight, up_bias=up_bias, down_weight=down_weight, down_bias=down_bias, norm_gain=norm_gain, norm_bias=norm_bias, cotangent=cotangent)


@jax.custom_vjp
def low(v):
    return lax.optimization_barrier(v.astype(jnp.bfloat16)).astype(jnp.float32)

@jax.custom_vjp
def low_back(v):
    return v

def low_keep(v):
    return (low(v), None)

def low_pass(kept, grad):
    return (grad,)

def back_keep(v):
    return (v, None)

def back_low(kept, grad):
    return (low(grad),)
low.defvjp(low_keep, low_pass)
low_back.defvjp(back_keep, back_low)
highest = lax.Precision.HIGHEST
eps = 1e-12

def rounded_both(value):
    return low(low_back(value))

def matmul(left, right):
    return jnp.dot(left, right, precision=highest)

def normalize(value, gain_row, bias_row):
    average = lax.optimization_barrier(jnp.mean(value, axis=-1, keepdims=True))
    centered = value - average
    variance = lax.optimization_barrier(jnp.mean(centered * centered, axis=-1, keepdims=True))
    return centered * lax.rsqrt(variance + eps) * gain_row + bias_row

def group_layer(params, group_item):
    page_rows, group_boxes, group_lengths = group_item
    table_x, table_y, in_weight, in_bias, out_weight, out_bias, up_weight, up_bias, down_weight, down_bias, norm_gain, norm_bias = params
    embedded = jnp.take(table_x, group_boxes[:, 0], axis=0) + jnp.take(table_x, group_boxes[:, 2], axis=0) + jnp.take(table_y, group_boxes[:, 1], axis=0) + jnp.take(table_y, group_boxes[:, 3], axis=0)
    residual = page_rows + low_back(embedded)
    residual_b = low(residual)
    queries = rounded_both(matmul(residual_b, in_weight[0]) + in_bias[0])
    key_rows = rounded_both(matmul(residual_b, in_weight[1]))
    value_rows = rounded_both(matmul(residual_b, in_weight[2]) + in_bias[1])
    page_count = group_lengths.shape[0]

    def to_pages(tensor_in):
        return tensor_in.reshape(page_count, PAGE, HEADS, HEAD)
    scores = jnp.einsum('pqhd,pkhd->phqk', to_pages(queries), to_pages(key_rows), precision=highest)
    scores = low_back(scores * HEAD ** (-0.5))
    visible = jnp.arange(PAGE, dtype=jnp.int32)[None, None, None, :] < group_lengths[:, None, None, None]
    scores = jnp.where(visible, scores, -1e+30)
    attend = low(jax.nn.softmax(scores, axis=-1))
    context = jnp.einsum('phqk,pkhd->pqhd', attend, to_pages(value_rows), precision=highest)
    context = rounded_both(context.reshape(-1, HEADS * HEAD))
    attention = low_back(matmul(context, out_weight) + out_bias)
    middle = normalize(residual + attention, norm_gain[0], norm_bias[0])
    hidden_pre = low_back(matmul(low(middle), up_weight) + up_bias)
    activated = rounded_both(jax.nn.gelu(hidden_pre, approximate=False))
    branch = low_back(matmul(activated, down_weight) + down_bias)
    return normalize(middle + branch, norm_gain[1], norm_bias[1])

def reference(hidden, page_boxes, lengths, table_x, table_y, in_weight, in_bias, out_weight, out_bias, up_weight, up_bias, down_weight, down_bias, norm_gain, norm_bias, cotangent):
    floats = tuple((a.astype(jnp.float32) for a in (hidden, table_x, table_y, in_weight, in_bias, out_weight, out_bias, up_weight, up_bias, down_weight, down_bias, norm_gain, norm_bias)))
    group_count = lengths.shape[0] // PAGES_DEV
    box_groups = page_boxes.reshape(group_count, -1, 4)
    length_groups = lengths.reshape(group_count, PAGES_DEV)

    def forward(hidden_in, *params):
        one_group = jax.checkpoint(partial(group_layer, params))
        result = lax.map(one_group, (hidden_in.reshape(group_count, -1, hidden_in.shape[1]), box_groups, length_groups))
        return result.reshape(hidden_in.shape)
    result, pull = jax.vjp(forward, *floats)
    grads = pull(cotangent.astype(jnp.float32))
    return (result.astype(jnp.bfloat16), grads[0], grads[1], grads[2], grads[3], grads[4], grads[5], grads[6], grads[7], grads[8], grads[9], grads[10], grads[11], grads[12])
```

```python
from functools import partial

import jax
import jax.numpy as jnp
from jax import lax
from jax.experimental import pallas as pl
from jax.experimental.pallas import tpu as pltpu
from jax.sharding import PartitionSpec as P

HEAD = 64
EPS = 1e-12
MESH = pl.DeviceIdType.MESH
f32 = jnp.float32
bf16 = jnp.bfloat16

R = 48
RT = 32
FR = 32
XR = R - FR


def dot(a, b, ca, cb):
    return lax.dot_general(a, b, (((ca,), (cb,)), ((), ())), preferred_element_type=f32)


def kernel(
    dp,
    hidden,
    boxes,
    lengths,
    tables_x,
    tables_y,
    in_w,
    in_b,
    out_w,
    out_b,
    up_w,
    up_b,
    down_w,
    down_b,
    gain,
    nbias,
    cotangent,
    layer_out,
    grad_hidden,
    G,
    GT,
    W,
    G2,
    pre,
    act,
    gp,
    qkv,
    ctx,
    lse,
    resb,
    midb,
    bgrad,
    hid,
    res,
    total,
    n1,
    r1,
    bias,
    vec,
    core_land,
    lands0,
    lands1,
    lands2,
    lands_t,
    lands_f,
    zl0,
    zl1,
    zl2,
    zlt,
    zlf,
    extra,
    extra_t,
    loc,
    bs,
    br,
    gzs,
    gzr,
    xs,
    xr,
    cs,
    cr,
    ks,
    kr,
    credit,
    rs,
    rr,
    zs,
    zr,
    es,
    er,
):
    d = lax.axis_index("dp")
    t = lax.axis_index("tensor")
    c = d % 2
    x = (d // 2) % 2
    y = (d // 4) % 2
    X = (d + 2 - 4 * x, t)
    Y = (d + 4 - 8 * y, t)
    C = (d + 1 - 2 * c, t)
    extras = []
    step = 8
    while step < dp:
        extras.append((d + step - 2 * step * ((d // step) % 2), t))
        step *= 2

    def remote(src, dst, send, recv, dev):
        return pltpu.make_async_remote_copy(
            src_ref=src, dst_ref=dst, send_sem=send, recv_sem=recv, device_id=dev, device_id_type=MESH
        )

    def wait_recv(ref, sem):
        remote(ref, ref, sem, sem, C).wait_recv()

    def wait_send(ref, sem):
        remote(ref, ref, sem, sem, C).wait_send()

    barrier = pltpu.get_barrier_semaphore()
    zpeers = [(d, (t + j) % 4) for j in range(1, 4)]
    peers = [X, Y, C] + zpeers + extras
    for peer in peers:
        pl.semaphore_signal(barrier, inc=1, device_id=peer, device_id_type=MESH)

    local = [
        pltpu.make_async_copy(in_w.at[pl.ds(0, 2)], W.at[0, t, 0], loc.at[0]),
        pltpu.make_async_copy(tables_x, pre.at[pl.ds(0, 1024)], loc.at[1]),
        pltpu.make_async_copy(tables_y, pre.at[pl.ds(1024, 1024)], loc.at[2]),
        pltpu.make_async_copy(hidden, hid, loc.at[3]),
        pltpu.make_async_copy(out_w, W.at[0, t, 1, 1], loc.at[4]),
        pltpu.make_async_copy(up_w, W.at[1, t], loc.at[5]),
        pltpu.make_async_copy(down_w, W.at[2, t], loc.at[6]),
        pltpu.make_async_copy(in_w.at[2], W.at[0, t, 1, 0], loc.at[7]),
    ]
    for i in (0, 7, 4, 1, 2, 3, 5, 6):
        local[i].start()
    bias[t] = jnp.zeros((8, 768), f32)
    bias[t, 0:1, :] = up_b[...].reshape(1, 768)
    bias[t, 1:2, 0:192] = in_b[0:1, :]
    bias[t, 1:2, 384:576] = in_b[1:2, :]
    local[0].wait()
    local[4].wait()
    local[7].wait()
    pl.semaphore_wait(barrier, len(peers))

    half = t // 2
    near = t * (1 - half) + (3 - t) * half

    def other(j):
        base = j + 1 - near * ((3 - j) // 3)
        return base * (1 - half) + (3 - base) * half

    def z_own(src, dst, ss, rsem):
        @pl.when(t > 0)
        def _():
            remote(src, dst, ss(0), rsem, (d, t - 1)).start()

        @pl.when(t < 3)
        def _():
            remote(src, dst, ss(1), rsem, (d, t + 1)).start()

    def z_arrive(ref, tp, send, recv):
        wait_recv(ref, recv)

        @pl.when(jnp.logical_and(tp < t, t < 3))
        def _():
            remote(ref, ref, send, recv, (d, t + 1)).start()

        @pl.when(jnp.logical_and(tp > t, t > 0))
        def _():
            remote(ref, ref, send, recv, (d, t - 1)).start()

    def z_drain(ref, ss):
        @pl.when(t > 0)
        def _():
            wait_send(ref, ss(0))

        @pl.when(t < 3)
        def _():
            wait_send(ref, ss(1))

    def z_arrive_drain(ref, tp, send):
        @pl.when(jnp.logical_or(jnp.logical_and(tp < t, t < 3), jnp.logical_and(tp > t, t > 0)))
        def _():
            wait_send(ref, send)

    def xy_own(src, dst, i):
        a, b = src.at[0], src.at[1]
        da, db = dst.at[c, y, x, 0], dst.at[c, y, x, 1]
        remote(a, da, xs.at[i, 0], xr.at[i, 0], X).start()
        remote(b, db, xs.at[i, 2], xr.at[i, 2], Y).start()
        remote(a, da, xs.at[i, 1], xr.at[i, 1], Y).start()
        remote(b, db, xs.at[i, 3], xr.at[i, 3], X).start()

    def xy_relay(ref, i):
        a, b = ref.at[c, y, 1 - x, 0], ref.at[c, 1 - y, x, 1]
        wait_recv(a, xr.at[i, 0])
        remote(a, a, xs.at[i, 4], xr.at[i, 4], Y).start()
        wait_recv(b, xr.at[i, 2])
        remote(b, b, xs.at[i, 5], xr.at[i, 5], X).start()

    def xy_finish(ref, i):
        wait_recv(ref.at[c, 1 - y, x, 0], xr.at[i, 1])
        wait_recv(ref.at[c, y, 1 - x, 1], xr.at[i, 3])
        wait_recv(ref.at[c, 1 - y, 1 - x, 0], xr.at[i, 4])
        wait_recv(ref.at[c, 1 - y, 1 - x, 1], xr.at[i, 5])
        remote(ref.at[c], ref.at[c], cs.at[i], cr.at[i], C).start()

    def xy_done(ref, i):
        wait_recv(ref.at[1 - c], cr.at[i])

    def xy_drain(ref, i):
        for k in range(6):
            wait_send(ref.at[c, 0, 0, 0], xs.at[i, k])
        wait_send(ref.at[c], cs.at[i])

    def gz_own(b):
        ref = W.at[b, t, c, y, x]
        z_own(ref, ref, lambda k: gzs.at[b, k], gzr.at[b, t])

    def e1(i):
        b, j = i // 3, i % 3
        tp = other(j)
        ref = W.at[b, tp, c, y, x]
        z_arrive(ref, tp, gzs.at[b, 2 + j], gzr.at[b, tp])
        xy_own(ref, W.at[b, tp], i)

    def e2(i):
        xy_relay(W.at[i // 3, other(i % 3)], i)

    def e3(i):
        xy_finish(W.at[i // 3, other(i % 3)], i)

    def e4(i):
        xy_done(W.at[i // 3, other(i % 3)], i)

    gz_own(0)
    for j in range(3):
        remote(bias.at[t], bias.at[t], bs.at[j], br.at[2 - j], zpeers[j]).start()

    def one_hot(first, second, levels):
        return ((first == levels).astype(f32) + (second == levels).astype(f32)).astype(bf16)

    levels = lax.broadcasted_iota(jnp.int32, (1024, 1), 0)

    def embed():
        for i in (1, 2, 3):
            local[i].wait()
        horizontal = one_hot(boxes[0:1], boxes[2:3], levels)
        vertical = one_hot(boxes[1:2], boxes[3:4], levels)
        residual = (
            hid[...].astype(f32)
            + dot(horizontal, pre[0:1024, :], 0, 0)
            + dot(vertical, pre[1024:2048, :], 0, 0)
        )
        res[...] = residual
        resb[...] = residual.astype(bf16)
        total[...] = jnp.zeros_like(total)

    embed()
    cot_copy = pltpu.make_async_copy(cotangent, hid, loc.at[3])
    cot_copy.start()

    local[5].wait()
    local[6].wait()
    for j in range(3):
        tz = (t + 3 - j) % 4
        wait_recv(bias.at[tz], br.at[2 - j])

    length = lengths[t]
    visible = lax.broadcasted_iota(jnp.int32, (512, 1), 0) < length
    scaling = HEAD**-0.5

    def project(tp):
        weight = W[0, tp].reshape(768, 768)
        qkv[tp] = (dot(resb[...], weight[0:576], 1, 1) + bias[tp, 1:2, 0:576]).astype(bf16)

    def heads(tp):
        for j in range(3):
            q = qkv[tp, :, j * 64 : (j + 1) * 64]
            k = qkv[tp, :, 192 + j * 64 : 192 + (j + 1) * 64]
            v = qkv[tp, :, 384 + j * 64 : 384 + (j + 1) * 64]
            scores = jnp.where(visible, dot(k, q, 1, 1) * scaling, -1e30)
            top = jnp.max(scores, axis=0, keepdims=True)
            exponent = jnp.exp(scores - top)
            sums = jnp.sum(exponent, axis=0, keepdims=True)
            attend = (exponent * (1.0 / sums)).astype(bf16)
            ctx[tp, :, j * 64 : (j + 1) * 64] = dot(attend, v, 0, 0).astype(bf16)
            lse[tp, j : j + 1, :] = top + jnp.log(sums)
        total[...] += dot(ctx[tp], W[0, tp, 1, 1].reshape(192, 768), 1, 0)

    def up(tp):
        hidden_pre = dot(midb[...], W[1, tp].reshape(768, 768), 1, 0) + bias[tp, 0:1, :]
        cdf = 0.5 * (1.0 + lax.erf(hidden_pre * 0.7071067811865476))
        act[tp] = (hidden_pre * cdf).astype(bf16).reshape(2, 2, 2, 2, RT, 768)
        slope = cdf + hidden_pre * jnp.exp(-0.5 * hidden_pre * hidden_pre) * 0.3989422804014327
        gp[tp] = slope.astype(bf16)

    def down(tp):
        total[...] += dot(act[tp].reshape(512, 768), W[2, tp].reshape(768, 768), 1, 0)

    def normalize(value):
        average = jnp.mean(value, axis=-1, keepdims=True)
        centered = value - average
        inverse = lax.rsqrt(jnp.mean(centered * centered, axis=-1, keepdims=True) + EPS)
        return centered * inverse, inverse

    def normalize_back(gradient, normed, inverse, gain_row):
        scaled = gradient * gain_row
        inner = (
            scaled
            - jnp.mean(scaled, axis=-1, keepdims=True)
            - normed * jnp.mean(scaled * normed, axis=-1, keepdims=True)
        )
        return inverse * inner

    def row_sum(value):
        return jnp.sum(value, axis=0, keepdims=True)

    def out_norm():
        normed, inverse = normalize(res[...] + total[...] + out_b[...].reshape(1, 768))
        n1[...] = normed
        r1[...] = inverse
        middle = normed * gain[0:1] + nbias[0:1]
        res[...] = middle
        midb[...] = middle.astype(bf16)
        total[...] = jnp.zeros_like(total)

    def drain_item(i):
        xy_drain(W.at[0, 0], i)

    def drain_z(b):
        z_drain(W.at[0, 0, 0, 0, 0], lambda k: gzs.at[b, k])
        for j in range(3):
            z_arrive_drain(W.at[0, 0, 0, 0, 0], other(j), gzs.at[b, 2 + j])

    e1(0)
    e1(1)
    e2(0)
    e1(2)
    gz_own(1)
    e2(1)
    project(t)
    e3(0)
    e2(2)
    heads(t)
    e1(3)
    e3(1)
    e4(0)
    project(other(0))
    e1(4)
    heads(other(0))
    e3(2)
    e1(5)
    gz_own(2)
    e2(3)
    e4(1)
    project(other(1))
    e2(4)
    heads(other(1))
    e1(6)
    e2(5)
    e3(3)
    e4(2)
    project(other(2))
    e1(7)
    heads(other(2))
    e3(4)
    e1(8)
    out_norm()
    e2(6)
    up(t)
    e3(5)
    e4(3)
    up(other(0))
    e2(7)
    e4(4)
    up(other(1))
    e3(6)
    e2(8)
    e4(5)
    up(other(2))
    e3(7)
    down(t)
    for i in range(6):
        drain_item(i)
    for b in range(3):
        drain_z(b)
    e4(6)
    down(other(0))
    e3(8)
    e4(7)
    down(other(1))
    e4(8)
    down(other(2))

    normed, inverse = normalize(res[...] + total[...] + down_b[...].reshape(1, 768))
    pre[1536:2048, :] = (normed * gain[1:2] + nbias[1:2]).astype(bf16)
    out_copy = pltpu.make_async_copy(pre.at[pl.ds(1536, 512)], layer_out, loc.at[8])
    out_copy.start()
    cot_copy.wait()
    gradient = hid[...].astype(f32)
    final_grad = normalize_back(gradient, normed, inverse, gain[1:2])
    res[...] = final_grad
    bgrad[...] = final_grad.astype(bf16)
    vec[...] = jnp.zeros_like(vec)
    vec[1:2, :] = row_sum(bgrad[...].astype(f32))
    vec[3:4, :] = row_sum(gradient * normed)
    vec[5:6, :] = row_sum(gradient)

    def core_send(ref, n, tp, rows=R):
        @pl.when(n >= 4)
        def _():
            pl.semaphore_wait(credit, 1)

        land = core_land.at[n % 4, :, :, :, pl.ds(0, rows)]
        remote(ref.at[tp, 1 - c], land, ks.at[n], kr.at[n], C).start()

    def core_add(ref, n, tp, rows=R):
        wait_recv(core_land.at[n % 4, :, :, :, pl.ds(0, rows)], kr.at[n])
        ref[tp, c] = ref[tp, c] + core_land[n % 4, :, :, :, 0:rows]

        @pl.when(n < 12)
        def _():
            pl.semaphore_signal(credit, inc=1, device_id=C, device_id_type=MESH)

    def xy1_send(ref, part, rows, lands, lp, g):
        a = ref.at[part, c, :, 1 - x, 0, rows]
        b = ref.at[part, c, 1 - y, :, 1, rows]
        remote(a, lands[0].at[lp], rs.at[g, 0], rr.at[g, 0], X).start()
        remote(b, lands[1].at[lp], rs.at[g, 1], rr.at[g, 1], Y).start()

    def xy1_add(ref, part, rows, lands, lp, g):
        wait_recv(lands[0].at[lp], rr.at[g, 0])
        ref[part, c, :, x, 0, rows] = ref[part, c, :, x, 0, rows] + lands[0][lp]
        remote(ref.at[part, c, 1 - y, x, 0, rows], lands[3].at[lp], rs.at[g, 3], rr.at[g, 3], Y).start()
        wait_recv(lands[1].at[lp], rr.at[g, 1])
        ref[part, c, y, :, 1, rows] = ref[part, c, y, :, 1, rows] + lands[1][lp]
        remote(ref.at[part, c, y, 1 - x, 1, rows], lands[2].at[lp], rs.at[g, 2], rr.at[g, 2], X).start()

    def xy2_add(ref, part, rows, lands, lp, g):
        wait_recv(lands[3].at[lp], rr.at[g, 3])
        ref[part, c, y, x, 0, rows] = ref[part, c, y, x, 0, rows] + lands[3][lp]
        wait_recv(lands[2].at[lp], rr.at[g, 2])
        ref[part, c, y, x, 1, rows] = ref[part, c, y, x, 1, rows] + lands[2][lp]

    def xy_rs_drain(lands, lp, g):
        for k in range(4):
            wait_send(lands[k].at[lp], rs.at[g, k])

    def z_send(ref, rows, land, g):
        for j in range(1, 4):
            k = (t + j) % 4
            remote(ref.at[k, c, y, x, :, rows], land.at[j - 1], zs.at[g, j - 1], zr.at[g, j - 1], (d, k)).start()

    def z_sum(ref, rows, land, g):
        for j in range(3):
            wait_recv(land.at[j], zr.at[g, j])
        value = ref[t, c, y, x, :, rows].astype(f32)
        for j in range(3):
            value = value + land[j].astype(f32)
        ref[t, c, y, x, :, rows] = value.astype(bf16)

    def z_drain_sum(land, g):
        for j in range(3):
            wait_send(land.at[j], zs.at[g, j])

    def zf_send(k):
        @pl.when(t != k)
        def _():
            slot = (k - t + 3) % 4
            remote(G2.at[k, c, :, :, :, rows_f], zlf.at[slot], zs.at[4, slot], zr.at[4, slot], (d, k)).start()

    def zf_sum():
        for j in range(3):
            wait_recv(zlf.at[j], zr.at[4, j])
        value = G2[t, c, :, :, :, rows_f].astype(f32)
        for j in range(3):
            value = value + zlf[j].astype(f32)
        G2[t, c, :, :, :, rows_f] = value.astype(bf16)

    def across(ref, land, g):
        for i, peer in enumerate(extras):
            copy = remote(ref, land.at[i], es.at[g, i], er.at[g, i], peer)
            copy.start()
            copy.wait()
            ref[...] = ref[...] + land[i]

    g1 = W.at[2]
    g0 = W.at[1]
    low, high, every = pl.ds(0, 2), pl.ds(2, 2), pl.ds(0, 4)
    rows_x, rows_f, rows, rows_t = pl.ds(0, XR), pl.ds(XR, FR), pl.ds(0, R), pl.ds(0, RT)
    b2_low, b2_high = (G2, low, rows_x, lands2, low, 0), (G2, high, rows_x, lands2, high, 1)
    b1_low, b1_high = (g1, low, rows, lands1, low, 2), (g1, high, rows, lands1, high, 3)
    b0_low, b0_high = (g0, low, rows, lands0, low, 4), (g0, high, rows, lands0, high, 5)
    table, f2 = (act, every, rows_t, lands_t, every, 6), (G2, t, rows_f, lands_f, 0, 7)
    z0, z1, z2, zt = (g0, rows, zl0, 0), (g1, rows, zl1, 1), (G2, rows_x, zl2, 2), (act, rows_t, zlt, 3)

    def down_grad(i):
        G2[i] = dot(act[i].reshape(512, 768), bgrad[...], 0, 0).astype(bf16).reshape(2, 2, 2, 2, R, 768)
        core_send(G2, i, i)

    def down_act(i):
        grad = dot(bgrad[...], W[2, i].reshape(768, 768), 1, 1).astype(bf16)
        pre_grad = (grad.astype(f32) * gp[i].astype(f32)).astype(bf16)
        pre[i * 512 : (i + 1) * 512, :] = pre_grad
        vec[6 + i : 7 + i, :] = row_sum(pre_grad.astype(f32))

    def down_add(i):
        core_add(G2, i, i)
        zf_send(i)

    def up_grad(i):
        grads = pre[i * 512 : (i + 1) * 512, :]
        g1[i] = dot(midb[...], grads, 0, 0).astype(bf16).reshape(2, 2, 2, 2, R, 768)
        core_send(g1, 4 + i, i)

    def up_act(i):
        res[...] += dot(pre[i * 512 : (i + 1) * 512, :], W[1, i].reshape(768, 768), 1, 1)

    def up_add(i):
        core_add(g1, 4 + i, i)

    def norm_back():
        normed = n1[...]
        gradient = res[...]
        residual_grad = normalize_back(gradient, normed, r1[...], gain[0:1])
        res[...] = residual_grad
        bgrad[...] = residual_grad.astype(bf16)
        vec[0:1, :] = row_sum(bgrad[...].astype(f32))
        vec[2:3, :] = row_sum(gradient * normed)
        vec[4:5, :] = row_sum(gradient)

    def heads_back(i):
        context_grad = dot(bgrad[...], W[0, i, 1, 1].reshape(192, 768), 1, 1).astype(bf16)
        for j in range(3):
            q = qkv[i, :, j * 64 : (j + 1) * 64]
            k = qkv[i, :, 192 + j * 64 : 192 + (j + 1) * 64]
            v = qkv[i, :, 384 + j * 64 : 384 + (j + 1) * 64]
            dc = context_grad[:, j * 64 : (j + 1) * 64]
            scores = jnp.where(visible, dot(k, q, 1, 1) * scaling, -1e30)
            attend = jnp.exp(scores - lse[i, j : j + 1, :])
            prob_grad = dot(v, dc, 1, 1)
            inner = jnp.sum(prob_grad * attend, axis=0, keepdims=True)
            score_grad = (attend * (prob_grad - inner)).astype(bf16)
            value_grad = dot(attend.astype(bf16), dc, 1, 0)
            key_grad = dot(score_grad, q, 1, 0) * scaling
            query_grad = dot(score_grad, k, 0, 0) * scaling
            qkv[i, :, j * 64 : (j + 1) * 64] = query_grad.astype(bf16)
            qkv[i, :, 192 + j * 64 : 192 + (j + 1) * 64] = key_grad.astype(bf16)
            qkv[i, :, 384 + j * 64 : 384 + (j + 1) * 64] = value_grad.astype(bf16)
        grads = qkv[i]
        res[...] += dot(grads, W[0, i].reshape(768, 768)[0:576], 1, 0)
        vec[10 + i : 11 + i, 0:576] = row_sum(grads.astype(f32))

    def in_grad(i):
        made = dot(qkv[i], resb[...], 0, 0).astype(bf16)
        g0[i, 0] = made[0:384].reshape(2, 2, 2, R, 768)
        g0[i, 1, 0] = made[384:576].reshape(2, 2, R, 768)
        g0[i, 1, 1] = dot(ctx[i], bgrad[...], 0, 0).astype(bf16).reshape(2, 2, R, 768)
        core_send(g0, 12 + i, i)

    def in_add(i):
        core_add(g0, 12 + i, i)

    def table_grad():
        hid[...] = res[...].astype(bf16)
        horizontal = one_hot(boxes[0:1], boxes[2:3], levels)
        act[0:2] = dot(horizontal, hid[...], 1, 0).astype(bf16).reshape(2, 2, 2, 2, 2, RT, 768)
        act[1, 1, 1, 1, 1, 16:32, :] = vec[...].astype(bf16)
        core_send(act, 8, 0, RT)
        core_send(act, 9, 1, RT)
        vertical = one_hot(boxes[1:2], boxes[3:4], levels)
        act[2:4] = dot(vertical, hid[...], 1, 0).astype(bf16).reshape(2, 2, 2, 2, 2, RT, 768)
        core_send(act, 10, 2, RT)
        core_send(act, 11, 3, RT)

    def table_add():
        for i in range(4):
            core_add(act, 8 + i, i, RT)

    F = [g0.at[t, c, y, x], g1.at[t, c, y, x], G2.at[t, c, y, x], act.at[t, c, y, x]]
    back = [G.at[0], G.at[1], G.at[2], GT.at[t]]
    kept = [pltpu.make_async_copy(F[b], back[b].at[c, y, x], loc.at[10 + b]) for b in range(4)]

    def ag_own(b):
        across(F[b], extra_t if b == 3 else extra, b)
        kept[b].start()
        xy_own(F[b], back[b], 9 + b)

    def ag_relay(b):
        xy_relay(back[b], 9 + b)

    def ag_finish(b):
        kept[b].wait()
        xy_finish(back[b], 9 + b)

    def table_out():
        ag_own(3)
        for j in range(1, 4):
            remote(F[3], GT.at[t, c, y, x], zs.at[5, j - 1], zr.at[5, j - 1], (d, (t + j) % 4)).start()

    def table_in(j):
        tp = (t + 4 - j) % 4
        wait_recv(GT.at[tp, c, y, x], zr.at[5, j - 1])
        xy_own(GT.at[tp, c, y, x], GT.at[tp], 12 + j)

    def table_relay(j):
        xy_relay(GT.at[(t + 4 - j) % 4], 12 + j)

    def table_finish(j):
        xy_finish(GT.at[(t + 4 - j) % 4], 12 + j)

    down_grad(0)
    down_act(0)
    down_grad(1)
    down_act(1)
    down_add(0)
    down_grad(2)
    down_add(1)
    xy1_send(*b2_low)
    down_act(2)
    down_grad(3)
    down_add(2)
    out_copy.wait()
    down_act(3)
    down_add(3)
    xy1_send(*b2_high)
    for i in range(6, 9):
        drain_item(i)
    up_grad(0)
    up_act(0)
    up_grad(1)
    up_act(1)
    up_add(0)
    xy1_add(*b2_low)
    up_grad(2)
    up_add(1)
    xy1_send(*b1_low)
    up_act(2)
    up_grad(3)
    up_add(2)
    xy1_add(*b2_high)
    up_act(3)
    up_add(3)
    xy1_send(*b1_high)
    norm_back()
    xy2_add(*b2_low)
    heads_back(0)
    xy2_add(*b2_high)
    z_send(*z2)
    xy1_add(*b1_low)
    heads_back(1)
    xy1_add(*b1_high)
    xy2_add(*b1_low)
    heads_back(2)
    xy2_add(*b1_high)
    z_send(*z1)
    heads_back(3)
    hidden_copy = pltpu.make_async_copy(res, grad_hidden, loc.at[9])
    hidden_copy.start()
    table_grad()
    table_add()
    xy1_send(*table)
    in_grad(0)
    in_grad(1)
    in_add(0)
    in_grad(2)
    in_add(1)
    xy1_send(*b0_low)
    in_grad(3)
    in_add(2)
    in_add(3)
    xy1_send(*b0_high)
    xy1_add(*table)
    zf_sum()
    xy1_send(*f2)
    z_sum(*z2)
    z_sum(*z1)
    ag_own(1)
    xy2_add(*table)
    z_send(*zt)
    xy1_add(*f2)
    xy1_add(*b0_low)
    xy2_add(*f2)
    ag_own(2)
    xy1_add(*b0_high)
    ag_relay(1)
    xy2_add(*b0_low)
    z_sum(*zt)
    table_out()
    xy2_add(*b0_high)
    z_send(*z0)
    ag_relay(2)
    ag_finish(1)
    table_in(1)
    ag_relay(3)
    table_in(2)
    table_in(3)
    table_relay(1)
    ag_finish(2)
    z_sum(*z0)
    ag_own(0)
    ag_finish(3)
    table_relay(2)
    table_relay(3)
    table_finish(1)
    ag_relay(0)
    table_finish(2)
    table_finish(3)
    ag_finish(0)

    hidden_copy.wait()
    for j in range(3):
        wait_send(bias.at[0], bs.at[j])
    for n in range(16):
        land = core_land.at[0, :, :, :, pl.ds(0, RT if 8 <= n < 12 else R)]
        wait_send(land, ks.at[n])
    for group in (b2_low, b2_high, b1_low, b1_high, b0_low, b0_high, table, f2):
        xy_rs_drain(*group[3:])
    for group in (z0, z1, z2, zt):
        z_drain_sum(*group[2:])
    z_drain_sum(zlf, 4)
    z_drain_sum(zlt, 5)
    for b in range(3):
        xy_drain(back[b], 9 + b)
        xy_done(back[b], 9 + b)
    for j in range(4):
        xy_drain(GT.at[(t + 4 - j) % 4], 12 + j)
        xy_done(GT.at[(t + 4 - j) % 4], 12 + j)


def finish(
    G,
    GT,
    made_out,
    made_hidden,
    layer_out,
    grad_hidden,
    table_x,
    table_y,
    in_w,
    out_w,
    up_w,
    down_w,
    in_b,
    out_b,
    up_b,
    down_b,
    gain,
    nbias,
    wide_w,
    wide_t,
    full_w,
    full_t,
    sem_in,
    sem_out,
    sem_pass,
):
    t = lax.axis_index("tensor")
    passed = [
        pltpu.make_async_copy(made_hidden, grad_hidden, sem_pass.at[0]),
        pltpu.make_async_copy(made_out, layer_out, sem_pass.at[1]),
    ]
    places = [in_w.at[0], in_w.at[1], in_w.at[2], out_w]
    places += [ref.at[pl.ds(192 * i, 192)] for ref in (up_w, down_w) for i in range(4)]
    tables = [ref.at[pl.ds(256 * i, 256)] for ref in (table_x, table_y) for i in range(4)]
    ins = [pltpu.make_async_copy(GT.at[i], wide_t.at[i], sem_in.at[12 + i]) for i in range(8)]
    ins = [pltpu.make_async_copy(G.at[i], wide_w.at[i], sem_in.at[i]) for i in range(12)] + ins
    outs = [pltpu.make_async_copy(full_w.at[i], places[i], sem_out.at[i]) for i in range(12)]
    outs += [pltpu.make_async_copy(full_t.at[i], tables[i], sem_out.at[12 + i]) for i in range(8)]
    for copy in ins + passed:
        copy.start()
    for i in range(12):
        ins[i].wait()
        full_w[i] = wide_w[i].astype(f32)
        outs[i].start()
    for i in range(8):
        ins[12 + i].wait()
        full_t[i] = wide_t[i].astype(f32)
        if i == 3:
            small = wide_t[3, 240:256].astype(f32)
            full_t[3, 240:256, :] = jnp.zeros((16, 768), f32)
            gain[...] = small[2:4]
            nbias[...] = small[4:6]
            out_b[...] = small[0]
            down_b[...] = small[1]
            level = lax.broadcasted_iota(jnp.int32, (16, 1), 0)
            up_b[...] = jnp.sum(jnp.where(level == 6 + t, small, 0.0), axis=0)
            row = jnp.sum(jnp.where(level == 10 + t, small, 0.0), axis=0, keepdims=True)
            in_b[0:1, :] = row[:, 0:192]
            in_b[1:2, :] = row[:, 384:576]
        outs[12 + i].start()
    for copy in outs + passed:
        copy.wait()


def on_device(
    dp,
    hidden,
    page_boxes,
    lengths,
    table_x,
    table_y,
    in_weight,
    in_bias,
    out_weight,
    out_bias,
    up_weight,
    up_bias,
    down_weight,
    down_bias,
    norm_gain,
    norm_bias,
    cotangent,
):
    blocks = (2, 2, 2, 2)
    vmem = pl.BlockSpec(memory_space=pltpu.VMEM)
    anywhere = pl.BlockSpec(memory_space=pl.ANY)
    dma = pltpu.SemaphoreType.DMA
    count = max(1, (dp // 8).bit_length() - 1)
    V = pltpu.VMEM

    def lands(quarters, rows):
        first, second = V((quarters, 2, rows, 768), bf16), V((quarters, rows, 768), bf16)
        return [first, first, second, second]

    scratch = [
        V((3, 4, *blocks, R, 768), bf16),
        V((4, *blocks, R, 768), bf16),
        V((2048, 768), bf16),
        V((4, *blocks, RT, 768), bf16),
        V((4, 512, 768), bf16),
        V((4, 512, 576), bf16),
        V((4, 512, 192), bf16),
        V((4, 8, 512), f32),
        V((512, 768), bf16),
        V((512, 768), bf16),
        V((512, 768), bf16),
        V((512, 768), bf16),
        V((512, 768), f32),
        V((512, 768), f32),
        V((512, 768), f32),
        V((512, 1), f32),
        V((4, 8, 768), f32),
        V((16, 768), f32),
        V((4, 2, 2, 2, R, 768), bf16),
        lands(4, R),
        lands(4, R),
        lands(4, XR),
        lands(4, RT),
        lands(1, FR),
        V((3, 2, R, 768), bf16),
        V((3, 2, R, 768), bf16),
        V((3, 2, XR, 768), bf16),
        V((3, 2, RT, 768), bf16),
        V((3, 2, 2, 2, FR, 768), bf16),
        V((count, 2, R, 768) if dp > 8 else (8, 128), bf16),
        V((count, 2, RT, 768) if dp > 8 else (8, 128), bf16),
        dma((14,)),
        dma((3,)),
        dma((3,)),
        dma((3, 5)),
        dma((3, 4)),
        dma((16, 6)),
        dma((16, 6)),
        dma((16,)),
        dma((16,)),
        dma((16,)),
        dma((16,)),
        pltpu.SemaphoreType.REGULAR,
        dma((8, 4)),
        dma((8, 4)),
        dma((6, 3)),
        dma((6, 3)),
        dma((4, count)),
        dma((4, count)),
    ]
    shape = jax.ShapeDtypeStruct
    made_out, made_hidden, G, GT = pl.pallas_call(
        partial(kernel, dp),
        out_shape=(
            shape((512, 768), bf16),
            shape((512, 768), f32),
            shape((3, *blocks, R, 768), bf16),
            shape((4, *blocks, RT, 768), bf16),
        ),
        in_specs=[
            anywhere,
            vmem,
            pl.BlockSpec(memory_space=pltpu.SMEM),
            anywhere,
            anywhere,
            anywhere,
            vmem,
            anywhere,
            vmem,
            anywhere,
            vmem,
            anywhere,
            vmem,
            vmem,
            vmem,
            anywhere,
        ],
        out_specs=(anywhere,) * 4,
        scratch_shapes=scratch,
        compiler_params=pltpu.CompilerParams(
            collective_id=0, has_side_effects=True, vmem_limit_bytes=58 * 2**20
        ),
    )(
        hidden,
        page_boxes.T,
        lengths,
        table_x,
        table_y,
        in_weight.transpose(0, 2, 1).reshape(3, 2, 2, R, 768),
        in_bias,
        out_weight.reshape(2, 2, R, 768),
        out_bias,
        up_weight.reshape(*blocks, R, 768),
        up_bias,
        down_weight.reshape(*blocks, R, 768),
        down_bias,
        norm_gain,
        norm_bias,
        cotangent,
    )
    outs = pl.pallas_call(
        finish,
        out_shape=(
            shape((512, 768), bf16),
            shape((512, 768), f32),
            shape((1024, 768), f32),
            shape((1024, 768), f32),
            shape((3, 192, 768), f32),
            shape((192, 768), f32),
            shape((768, 768), f32),
            shape((768, 768), f32),
            shape((2, 192), f32),
            shape((768,), f32),
            shape((768,), f32),
            shape((768,), f32),
            shape((2, 768), f32),
            shape((2, 768), f32),
        ),
        in_specs=[anywhere] * 4,
        out_specs=(anywhere,) * 8 + (vmem,) * 6,
        scratch_shapes=[
            V((12, 192, 768), bf16),
            V((8, 256, 768), bf16),
            V((12, 192, 768), f32),
            V((8, 256, 768), f32),
            dma((20,)),
            dma((20,)),
            dma((2,)),
        ],
        compiler_params=pltpu.CompilerParams(vmem_limit_bytes=40 * 2**20),
    )(G.reshape(12, 192, 768), GT.reshape(8, 256, 768), made_out, made_hidden)
    out, hidden_grad, tx, ty, in_w, out_w, up_w, down_w, in_b, out_b, up_b, down_b, gains, biases = outs
    in_w = in_w.transpose(0, 2, 1)
    return out, hidden_grad, tx, ty, in_w, in_b, out_w, out_b, up_w, up_b, down_w, down_b, gains, biases


def solution(mesh):
    both = ("dp", "tensor")
    in_specs = (
        P(both, None),
        P(both, None),
        P("dp"),
        P(),
        P(),
        P(None, None, "tensor"),
        P(None, "tensor"),
        P("tensor", None),
        P(),
        P(None, "tensor"),
        P("tensor"),
        P("tensor", None),
        P(),
        P(),
        P(),
        P(both, None),
    )
    out_specs = (
        P(both, None),
        P(both, None),
        P(),
        P(),
        P(None, None, "tensor"),
        P(None, "tensor"),
        P("tensor", None),
        P(),
        P(None, "tensor"),
        P("tensor"),
        P("tensor", None),
        P(),
        P(),
        P(),
    )
    return jax.shard_map(
        partial(on_device, mesh.shape["dp"]),
        mesh=mesh,
        in_specs=in_specs,
        out_specs=out_specs,
        check_vma=False,
    )
```

```python
from functools import partial

import jax
import jax.numpy as jnp
from jax import lax
from jax.experimental import pallas as pl
from jax.experimental.pallas import tpu as pltpu
from jax.sharding import PartitionSpec as P

HEAD = 64
EPS = 1e-12
MESH = pl.DeviceIdType.MESH
f32 = jnp.float32
bf16 = jnp.bfloat16

R = 48
RT = 16
FR = 16
XR = R - FR


def dot(a, b, ca, cb):
    return lax.dot_general(a, b, (((ca,), (cb,)), ((), ())), preferred_element_type=f32)


def kernel(
    dp,
    hidden,
    boxes,
    lengths,
    tables_x,
    tables_y,
    in_w,
    in_b,
    out_w,
    out_b,
    up_w,
    up_b,
    down_w,
    down_b,
    gain,
    nbias,
    cotangent,
    layer_out,
    grad_hidden,
    G,
    GT,
    W,
    G2,
    pre,
    act,
    gp,
    qkv,
    ctx,
    lse,
    resb,
    midb,
    bgrad,
    hid,
    res,
    total,
    n1,
    r1,
    bias,
    vec,
    core_land,
    core_land_t,
    lands0,
    lands1,
    lands2,
    lands_t,
    lands_f,
    lands_ft,
    zl0,
    zl1,
    zl2,
    zlt,
    zlf,
    zlft,
    extra,
    extra_t,
    loc,
    bs,
    br,
    gzs,
    gzr,
    xs,
    xr,
    cs,
    cr,
    ks,
    kr,
    credit,
    rs,
    rr,
    zs,
    zr,
    es,
    er,
):
    d = lax.axis_index("dp")
    t = lax.axis_index("tensor")
    c = d % 2
    x = (d // 2) % 2
    y = (d // 4) % 2
    X = (d + 2 - 4 * x, t)
    Y = (d + 4 - 8 * y, t)
    C = (d + 1 - 2 * c, t)
    extras = []
    step = 8
    while step < dp:
        extras.append((d + step - 2 * step * ((d // step) % 2), t))
        step *= 2

    def remote(src, dst, send, recv, dev):
        return pltpu.make_async_remote_copy(
            src_ref=src, dst_ref=dst, send_sem=send, recv_sem=recv, device_id=dev, device_id_type=MESH
        )

    def wait_recv(ref, sem):
        remote(ref, ref, sem, sem, C).wait_recv()

    def wait_send(ref, sem):
        remote(ref, ref, sem, sem, C).wait_send()

    barrier = pltpu.get_barrier_semaphore()
    zpeers = [(d, (t + j) % 4) for j in range(1, 4)]
    peers = [X, Y, C] + zpeers + extras
    for peer in peers:
        pl.semaphore_signal(barrier, inc=1, device_id=peer, device_id_type=MESH)

    local = [
        pltpu.make_async_copy(in_w.at[pl.ds(0, 2)], W.at[0, t, 0], loc.at[0]),
        pltpu.make_async_copy(tables_x, pre.at[pl.ds(0, 1024)], loc.at[1]),
        pltpu.make_async_copy(tables_y, pre.at[pl.ds(1024, 1024)], loc.at[2]),
        pltpu.make_async_copy(hidden, hid, loc.at[3]),
        pltpu.make_async_copy(out_w, W.at[0, t, 1, 1], loc.at[4]),
        pltpu.make_async_copy(up_w, W.at[1, t], loc.at[5]),
        pltpu.make_async_copy(down_w, W.at[2, t], loc.at[6]),
        pltpu.make_async_copy(in_w.at[2], W.at[0, t, 1, 0], loc.at[7]),
    ]
    for i in (0, 7, 4, 1, 2, 3, 5, 6):
        local[i].start()
    bias[t] = jnp.zeros((8, 768), f32)
    bias[t, 0:1, :] = up_b[...].reshape(1, 768)
    bias[t, 1:2, 0:192] = in_b[0:1, :]
    bias[t, 1:2, 384:576] = in_b[1:2, :]
    def entry_local():
        local[0].wait()
        local[4].wait()
        local[7].wait()

    def entry_barrier():
        pl.semaphore_wait(barrier, len(peers))

    entry_barrier()
    entry_local()

    half = t // 2
    near = t * (1 - half) + (3 - t) * half

    def other(j):
        base = j + 1 - near * ((3 - j) // 3)
        return base * (1 - half) + (3 - base) * half

    def z_own(src, dst, ss, rsem):
        @pl.when(t > 0)
        def _():
            remote(src, dst, ss(0), rsem, (d, t - 1)).start()

        @pl.when(t < 3)
        def _():
            remote(src, dst, ss(1), rsem, (d, t + 1)).start()

    def z_arrive(ref, tp, send, recv):
        wait_recv(ref, recv)

        @pl.when(jnp.logical_and(tp < t, t < 3))
        def _():
            remote(ref, ref, send, recv, (d, t + 1)).start()

        @pl.when(jnp.logical_and(tp > t, t > 0))
        def _():
            remote(ref, ref, send, recv, (d, t - 1)).start()

    def z_drain(ref, ss):
        @pl.when(t > 0)
        def _():
            wait_send(ref, ss(0))

        @pl.when(t < 3)
        def _():
            wait_send(ref, ss(1))

    def z_arrive_drain(ref, tp, send):
        @pl.when(jnp.logical_or(jnp.logical_and(tp < t, t < 3), jnp.logical_and(tp > t, t > 0)))
        def _():
            wait_send(ref, send)

    def xy_own(src, dst, i):
        a, b = src.at[0], src.at[1]
        da, db = dst.at[c, y, x, 0], dst.at[c, y, x, 1]
        remote(a, da, xs.at[i, 0], xr.at[i, 0], X).start()
        remote(b, db, xs.at[i, 2], xr.at[i, 2], Y).start()
        remote(a, da, xs.at[i, 1], xr.at[i, 1], Y).start()
        remote(b, db, xs.at[i, 3], xr.at[i, 3], X).start()

    def xy_relay(ref, i):
        a, b = ref.at[c, y, 1 - x, 0], ref.at[c, 1 - y, x, 1]
        wait_recv(a, xr.at[i, 0])
        remote(a, a, xs.at[i, 4], xr.at[i, 4], Y).start()
        wait_recv(b, xr.at[i, 2])
        remote(b, b, xs.at[i, 5], xr.at[i, 5], X).start()

    def xy_finish(ref, i):
        wait_recv(ref.at[c, 1 - y, x, 0], xr.at[i, 1])
        wait_recv(ref.at[c, y, 1 - x, 1], xr.at[i, 3])
        wait_recv(ref.at[c, 1 - y, 1 - x, 0], xr.at[i, 4])
        wait_recv(ref.at[c, 1 - y, 1 - x, 1], xr.at[i, 5])
        remote(ref.at[c], ref.at[c], cs.at[i], cr.at[i], C).start()

    def xy_done(ref, i):
        wait_recv(ref.at[1 - c], cr.at[i])

    def xy_drain(ref, i):
        for k in range(6):
            wait_send(ref.at[c, 0, 0, 0], xs.at[i, k])
        wait_send(ref.at[c], cs.at[i])

    def gz_own(b):
        for h in range(2):
            ref = W.at[b, t, c, y, x, h]
            z_own(ref, ref, lambda k: gzs.at[b, k, h], gzr.at[b, t, h])

    def gz_end(b):
        @pl.when(jnp.logical_or(t == 0, t == 3))
        def _():
            gz_own(b)

    def gz_middle(b):
        @pl.when(jnp.logical_and(t > 0, t < 3))
        def _():
            gz_own(b)

    def e1(i):
        b, j = i // 3, i % 3
        tp = other(j)
        for h in range(2):
            ref = W.at[b, tp, c, y, x, h]
            z_arrive(ref, tp, gzs.at[b, 2 + j, h], gzr.at[b, tp, h])
            for dev, k in ((X, 0), (Y, 1)) if h == 0 else ((Y, 2), (X, 3)):
                remote(ref, ref, xs.at[i, k], xr.at[i, k], dev).start()

    def e2(i):
        xy_relay(W.at[i // 3, other(i % 3)], i)

    def e3(i):
        xy_finish(W.at[i // 3, other(i % 3)], i)

    def e4(i):
        xy_done(W.at[i // 3, other(i % 3)], i)

    gz_own(0)
    for j in range(3):
        remote(bias.at[t], bias.at[t], bs.at[j], br.at[2 - j], zpeers[j]).start()

    def one_hot(first, second, levels):
        return ((first == levels).astype(f32) + (second == levels).astype(f32)).astype(bf16)

    levels = lax.broadcasted_iota(jnp.int32, (1024, 1), 0)

    def embed():
        for i in (1, 2, 3):
            local[i].wait()
        horizontal = one_hot(boxes[0:1], boxes[2:3], levels)
        vertical = one_hot(boxes[1:2], boxes[3:4], levels)
        residual = (
            hid[...].astype(f32)
            + dot(horizontal, pre[0:1024, :], 0, 0)
            + dot(vertical, pre[1024:2048, :], 0, 0)
        )
        res[...] = residual
        resb[...] = residual.astype(bf16)
        total[...] = jnp.zeros_like(total)

    embed()
    local[5].wait()
    local[6].wait()
    cot_copy = pltpu.make_async_copy(cotangent, hid, loc.at[3])
    cot_copy.start()

    def biases():
        for j in range(3):
            tz = (t + 3 - j) % 4
            wait_recv(bias.at[tz], br.at[2 - j])

    length = lengths[t]
    visible = lax.broadcasted_iota(jnp.int32, (512, 1), 0) < length
    scaling = HEAD**-0.5

    def project(tp):
        weight = W[0, tp].reshape(768, 768)
        qkv[tp] = (dot(resb[...], weight[0:576], 1, 1) + bias[tp, 1:2, 0:576]).astype(bf16)

    def heads(tp):
        for j in range(3):
            q = qkv[tp, :, j * 64 : (j + 1) * 64]
            k = qkv[tp, :, 192 + j * 64 : 192 + (j + 1) * 64]
            v = qkv[tp, :, 384 + j * 64 : 384 + (j + 1) * 64]
            scores = jnp.where(visible, dot(k, q, 1, 1) * scaling, -1e30)
            top = jnp.max(scores, axis=0, keepdims=True)
            exponent = jnp.exp(scores - top)
            sums = jnp.sum(exponent, axis=0, keepdims=True)
            attend = (exponent * (1.0 / sums)).astype(bf16)
            ctx[tp, :, j * 64 : (j + 1) * 64] = dot(attend, v, 0, 0).astype(bf16)
            lse[tp, j : j + 1, :] = top + jnp.log(sums)
        total[...] += dot(ctx[tp], W[0, tp, 1, 1].reshape(192, 768), 1, 0)

    def up(tp):
        hidden_pre = dot(midb[...], W[1, tp].reshape(768, 768), 1, 0) + bias[tp, 0:1, :]
        cdf = 0.5 * (1.0 + lax.erf(hidden_pre * 0.7071067811865476))
        act[pl.ds(2 * tp, 2)] = (hidden_pre * cdf).astype(bf16).reshape(2, 2, 2, 2, 2, RT, 768)
        slope = cdf + hidden_pre * jnp.exp(-0.5 * hidden_pre * hidden_pre) * 0.3989422804014327
        gp[tp] = slope.astype(bf16)

    def down(tp):
        total[...] += dot(act[pl.ds(2 * tp, 2)].reshape(512, 768), W[2, tp].reshape(768, 768), 1, 0)

    def normalize(value):
        average = jnp.mean(value, axis=-1, keepdims=True)
        centered = value - average
        inverse = lax.rsqrt(jnp.mean(centered * centered, axis=-1, keepdims=True) + EPS)
        return centered * inverse, inverse

    def normalize_back(gradient, normed, inverse, gain_row):
        scaled = gradient * gain_row
        inner = (
            scaled
            - jnp.mean(scaled, axis=-1, keepdims=True)
            - normed * jnp.mean(scaled * normed, axis=-1, keepdims=True)
        )
        return inverse * inner

    def row_sum(value):
        return jnp.sum(value, axis=0, keepdims=True)

    def out_norm():
        normed, inverse = normalize(res[...] + total[...] + out_b[...].reshape(1, 768))
        n1[...] = normed
        r1[...] = inverse
        middle = normed * gain[0:1] + nbias[0:1]
        res[...] = middle
        midb[...] = middle.astype(bf16)
        total[...] = jnp.zeros_like(total)

    def drain_item(i):
        xy_drain(W.at[0, 0], i)

    def drain_z(b):
        for h in range(2):
            z_drain(W.at[0, 0, 0, 0, 0, 0], lambda k: gzs.at[b, k, h])
            for j in range(3):
                z_arrive_drain(W.at[0, 0, 0, 0, 0, 0], other(j), gzs.at[b, 2 + j, h])

    e1(0)
    e1(1)
    gz_end(1)
    e2(0)
    e1(2)
    gz_middle(1)
    e2(1)
    biases()
    project(t)
    e2(2)
    heads(t)
    e3(0)
    e1(3)
    e4(0)
    project(other(0))
    e1(4)
    gz_end(2)
    e3(1)
    heads(other(0))
    e1(5)
    gz_middle(2)
    e2(3)
    e4(1)
    project(other(1))
    e3(2)
    heads(other(1))
    e2(4)
    e1(6)
    e4(2)
    project(other(2))
    e1(7)
    e2(5)
    e3(3)
    heads(other(2))
    e1(8)
    out_norm()
    e2(6)
    up(t)
    e3(4)
    e4(3)
    up(other(0))
    e2(7)
    e3(5)
    e4(4)
    up(other(1))
    e2(8)
    e3(6)
    e4(5)
    up(other(2))
    down(t)
    e3(7)
    for i in range(6):
        drain_item(i)
    for b in range(3):
        drain_z(b)
    e4(6)
    down(other(0))
    e3(8)
    e4(7)
    down(other(1))
    e4(8)
    down(other(2))

    normed, inverse = normalize(res[...] + total[...] + down_b[...].reshape(1, 768))
    pre[1536:2048, :] = (normed * gain[1:2] + nbias[1:2]).astype(bf16)
    out_copy = pltpu.make_async_copy(pre.at[pl.ds(1536, 512)], layer_out, loc.at[8])
    out_copy.start()
    cot_copy.wait()
    gradient = hid[...].astype(f32)
    final_grad = normalize_back(gradient, normed, inverse, gain[1:2])
    res[...] = final_grad
    bgrad[...] = final_grad.astype(bf16)
    vec[...] = jnp.zeros_like(vec)
    vec[1:2, :] = row_sum(bgrad[...].astype(f32))
    vec[3:4, :] = row_sum(gradient * normed)
    vec[5:6, :] = row_sum(gradient)

    def core_send(ref, n, tp):
        if n >= 6:
            pl.semaphore_wait(credit, 1)

        remote(ref.at[tp, 1 - c], core_land.at[n % 6], ks.at[n], kr.at[n], C).start()

    def core_add(ref, n, tp):
        wait_recv(core_land.at[n % 6], kr.at[n])
        ref[tp, c] = ref[tp, c] + core_land[n % 6]

        if n < 6:
            pl.semaphore_signal(credit, inc=1, device_id=C, device_id_type=MESH)

    def xy1_send(ref, part, rows, lands, lp, g):
        a = ref.at[part, c, :, 1 - x, 0, rows]
        b = ref.at[part, c, 1 - y, :, 1, rows]
        remote(a, lands[0].at[lp], rs.at[g, 0], rr.at[g, 0], X).start()
        remote(b, lands[1].at[lp], rs.at[g, 1], rr.at[g, 1], Y).start()

    def xy1_add(ref, part, rows, lands, lp, g):
        wait_recv(lands[0].at[lp], rr.at[g, 0])
        ref[part, c, :, x, 0, rows] = ref[part, c, :, x, 0, rows] + lands[0][lp]
        remote(ref.at[part, c, 1 - y, x, 0, rows], lands[3].at[lp], rs.at[g, 3], rr.at[g, 3], Y).start()
        wait_recv(lands[1].at[lp], rr.at[g, 1])
        ref[part, c, y, :, 1, rows] = ref[part, c, y, :, 1, rows] + lands[1][lp]
        remote(ref.at[part, c, y, 1 - x, 1, rows], lands[2].at[lp], rs.at[g, 2], rr.at[g, 2], X).start()

    def xy2_add(ref, part, rows, lands, lp, g):
        wait_recv(lands[3].at[lp], rr.at[g, 3])
        ref[part, c, y, x, 0, rows] = ref[part, c, y, x, 0, rows] + lands[3][lp]
        wait_recv(lands[2].at[lp], rr.at[g, 2])
        ref[part, c, y, x, 1, rows] = ref[part, c, y, x, 1, rows] + lands[2][lp]

    def xy_rs_drain(lands, lp, g):
        for k in range(4):
            wait_send(lands[k].at[lp], rs.at[g, k])

    def z_send(ref, rows, land, g):
        for j in range(1, 4):
            k = (t + j) % 4
            remote(ref.at[k, c, y, x, :, rows], land.at[j - 1], zs.at[g, j - 1], zr.at[g, j - 1], (d, k)).start()

    def zk_send(ref, rows, land, g, k):
        @pl.when(t != k)
        def _():
            slot = (k - t + 3) % 4
            remote(ref.at[k, c, y, x, :, rows], land.at[slot], zs.at[g, slot], zr.at[g, slot], (d, k)).start()

    def z_sum(ref, rows, land, g):
        for j in range(3):
            wait_recv(land.at[j], zr.at[g, j])
        value = ref[t, c, y, x, :, rows].astype(f32)
        for j in range(3):
            value = value + land[j].astype(f32)
        ref[t, c, y, x, :, rows] = value.astype(bf16)

    def z_drain_sum(land, g):
        for j in range(3):
            wait_send(land.at[j], zs.at[g, j])

    def zf_send(ref, rows, land, g, k):
        @pl.when(t != k)
        def _():
            slot = (k - t + 3) % 4
            remote(ref.at[k, c, :, :, :, rows], land.at[slot], zs.at[g, slot], zr.at[g, slot], (d, k)).start()

    def zf_sum(ref, rows, land, g):
        for j in range(3):
            wait_recv(land.at[j], zr.at[g, j])
        value = ref[t, c, :, :, :, rows].astype(f32)
        for j in range(3):
            value = value + land[j].astype(f32)
        ref[t, c, :, :, :, rows] = value.astype(bf16)

    def across(ref, land, g):
        for i, peer in enumerate(extras):
            copy = remote(ref, land.at[i], es.at[g, i], er.at[g, i], peer)
            copy.start()
            copy.wait()
            ref[...] = ref[...] + land[i]

    g1 = W.at[2]
    g0 = W.at[1]
    low, high, every = pl.ds(0, 2), pl.ds(2, 2), pl.ds(0, 4)
    rows_x, rows_f, rows, rows_t = pl.ds(0, XR), pl.ds(XR, FR), pl.ds(0, R), pl.ds(0, RT)
    tables = [act.at[pl.ds(0, 4)], act.at[pl.ds(4, 4)]]
    b2_low, b2_high = (G2, low, rows_x, lands2, low, 0), (G2, high, rows_x, lands2, high, 1)
    b1_low, b1_high = (g1, low, rows, lands1, low, 2), (g1, high, rows, lands1, high, 3)
    b0_low = (g0, low, rows, lands0, low, 4)
    b0_q2, b0_q3 = (g0, pl.ds(2, 1), rows, lands0, pl.ds(2, 1), 5), (g0, pl.ds(3, 1), rows, lands0, pl.ds(3, 1), 6)
    table1 = (tables[1], every, rows_t, lands_t, every, 8)
    f2, ft = (G2, t, rows_f, lands_f, 0, 9), (tables[0], t, rows_t, lands_ft, 0, 7)
    z0, z1, z2 = (g0, rows, zl0, 0), (g1, rows, zl1, 1), (G2, rows_x, zl2, 2)
    zt1 = (tables[1], rows_t, zlt, 4)
    zf2, zft = (G2, rows_f, zlf, 7), (tables[0], rows_t, zlft, 3)

    def down_grad(i):
        G2[i] = dot(act[2 * i : 2 * i + 2].reshape(512, 768), bgrad[...], 0, 0).astype(bf16).reshape(2, 2, 2, 2, R, 768)
        core_send(G2, i, i)

    def down_act(i):
        grad = dot(bgrad[...], W[2, i].reshape(768, 768), 1, 1).astype(bf16)
        pre_grad = (grad.astype(f32) * gp[i].astype(f32)).astype(bf16)
        pre[i * 512 : (i + 1) * 512, :] = pre_grad
        vec[6 + i : 7 + i, :] = row_sum(pre_grad.astype(f32))

    def down_add(i):
        core_add(G2, i, i)
        zf_send(*zf2, i)

    def up_grad(i):
        grads = pre[i * 512 : (i + 1) * 512, :]
        g1[i] = dot(midb[...], grads, 0, 0).astype(bf16).reshape(2, 2, 2, 2, R, 768)
        core_send(g1, 4 + i, i)

    def up_act(i):
        res[...] += dot(pre[i * 512 : (i + 1) * 512, :], W[1, i].reshape(768, 768), 1, 1)

    def up_add(i):
        core_add(g1, 4 + i, i)

    def norm_back():
        normed = n1[...]
        gradient = res[...]
        residual_grad = normalize_back(gradient, normed, r1[...], gain[0:1])
        res[...] = residual_grad
        bgrad[...] = residual_grad.astype(bf16)
        vec[0:1, :] = row_sum(bgrad[...].astype(f32))
        vec[2:3, :] = row_sum(gradient * normed)
        vec[4:5, :] = row_sum(gradient)

    def heads_back(i):
        context_grad = dot(bgrad[...], W[0, i, 1, 1].reshape(192, 768), 1, 1).astype(bf16)
        for j in range(3):
            q = qkv[i, :, j * 64 : (j + 1) * 64]
            k = qkv[i, :, 192 + j * 64 : 192 + (j + 1) * 64]
            v = qkv[i, :, 384 + j * 64 : 384 + (j + 1) * 64]
            dc = context_grad[:, j * 64 : (j + 1) * 64]
            scores = jnp.where(visible, dot(k, q, 1, 1) * scaling, -1e30)
            attend = jnp.exp(scores - lse[i, j : j + 1, :])
            prob_grad = dot(v, dc, 1, 1)
            inner = jnp.sum(prob_grad * attend, axis=0, keepdims=True)
            score_grad = (attend * (prob_grad - inner)).astype(bf16)
            value_grad = dot(attend.astype(bf16), dc, 1, 0)
            key_grad = dot(score_grad, q, 1, 0) * scaling
            query_grad = dot(score_grad, k, 0, 0) * scaling
            qkv[i, :, j * 64 : (j + 1) * 64] = query_grad.astype(bf16)
            qkv[i, :, 192 + j * 64 : 192 + (j + 1) * 64] = key_grad.astype(bf16)
            qkv[i, :, 384 + j * 64 : 384 + (j + 1) * 64] = value_grad.astype(bf16)
        grads = qkv[i]
        res[...] += dot(grads, W[0, i].reshape(768, 768)[0:576], 1, 0)
        vec[10 + i : 11 + i, 0:576] = row_sum(grads.astype(f32))

    def in_grad(i):
        made = dot(qkv[i], resb[...], 0, 0).astype(bf16)
        g0[i, 0] = made[0:384].reshape(2, 2, 2, R, 768)
        g0[i, 1, 0] = made[384:576].reshape(2, 2, R, 768)
        g0[i, 1, 1] = dot(ctx[i], bgrad[...], 0, 0).astype(bf16).reshape(2, 2, R, 768)
        core_send(g0, 8 + i, i)

    def in_add(i):
        core_add(g0, 8 + i, i)

    def table_grad(h):
        if h == 0:
            hid[...] = res[...].astype(bf16)
        hot = one_hot(boxes[h : h + 1], boxes[h + 2 : h + 3], levels)
        made = dot(hot, hid[...], 1, 0).astype(bf16)
        act[4 * h : 4 * h + 4] = made.reshape(4, 2, 2, 2, 2, RT, 768)
        if h == 0:
            act[3, 1, 1, 1, 1] = vec[...].astype(bf16)
        remote(tables[h].at[:, 1 - c], core_land_t.at[h], ks.at[12 + h], kr.at[12 + h], C).start()

    def table_add(h):
        wait_recv(core_land_t.at[h], kr.at[12 + h])
        tables[h][:, c] = tables[h][:, c] + core_land_t[h]
        if h == 0:
            for k in range(4):
                zf_send(*zft, k)

    F = [g0.at[t, c, y, x], g1.at[t, c, y, x], G2.at[t, c, y, x]]
    F += [ref.at[t, c, y, x] for ref in tables]
    back = [G.at[0], G.at[1], G.at[2], GT.at[0, t], GT.at[1, t]]
    item = [9, 10, 11, 12, 16]
    kept = [pltpu.make_async_copy(F[b], back[b].at[c, y, x], loc.at[10 + b]) for b in range(5)]

    def ag_own(b):
        across(F[b], extra_t if b >= 3 else extra, b)
        kept[b].start()
        xy_own(F[b], back[b], item[b])

    def ag_relay(b):
        xy_relay(back[b], item[b])

    def ag_finish(b):
        kept[b].wait()
        xy_finish(back[b], item[b])

    def table_out(h):
        ag_own(3 + h)
        for j in range(1, 4):
            send, recv = zs.at[5 + h, j - 1], zr.at[5 + h, j - 1]
            remote(F[3 + h], GT.at[h, t, c, y, x], send, recv, (d, (t + j) % 4)).start()

    def table_in(h, j):
        ref = GT.at[h, (t + 4 - j) % 4]
        wait_recv(ref.at[c, y, x], zr.at[5 + h, j - 1])
        xy_own(ref.at[c, y, x], ref, 12 + 4 * h + j)

    def table_relay(h, j):
        xy_relay(GT.at[h, (t + 4 - j) % 4], 12 + 4 * h + j)

    def table_finish(h, j):
        if j == 0:
            kept[3 + h].wait()
        xy_finish(GT.at[h, (t + 4 - j) % 4], 12 + 4 * h + j)

    down_grad(0)
    down_grad(1)
    down_grad(2)
    down_add(0)
    down_grad(3)
    down_add(1)
    xy1_send(*b2_low)
    down_act(0)
    down_add(2)
    down_act(1)
    down_add(3)
    xy1_send(*b2_high)
    for i in range(6, 9):
        drain_item(i)
    up_grad(0)
    down_act(2)
    up_grad(1)
    up_add(0)
    out_copy.wait()
    down_act(3)
    xy1_add(*b2_low)
    up_add(1)
    xy1_send(*b1_low)
    up_grad(2)
    up_grad(3)
    up_act(0)
    xy1_add(*b2_high)
    up_add(2)
    up_act(1)
    up_add(3)
    xy2_add(*b2_low)
    up_act(2)
    up_act(3)
    xy1_send(*b1_high)
    norm_back()
    heads_back(0)
    xy1_add(*b1_low)
    xy2_add(*b2_high)
    z_send(*z2)
    in_grad(0)
    heads_back(1)
    in_add(0)
    in_grad(1)
    xy1_add(*b1_high)
    xy2_add(*b1_low)
    zk_send(*z1, 0)
    zk_send(*z1, 1)
    in_add(1)
    xy1_send(*b0_low)
    heads_back(2)
    xy2_add(*b1_high)
    zk_send(*z1, 2)
    zk_send(*z1, 3)
    zf_sum(*zf2)
    xy1_send(*f2)
    in_grad(2)
    heads_back(3)
    hidden_copy = pltpu.make_async_copy(res, grad_hidden, loc.at[9])
    hidden_copy.start()
    xy1_add(*b0_low)
    xy1_add(*f2)
    in_add(2)
    table_grad(0)
    table_grad(1)
    table_add(0)
    in_grad(3)
    table_add(1)
    xy1_send(*table1)
    xy2_add(*b0_low)
    xy2_add(*f2)
    in_add(3)
    xy1_send(*b0_q2)
    z_sum(*z2)
    ag_own(2)
    xy1_add(*table1)
    xy1_send(*b0_q3)
    z_sum(*z1)
    xy2_add(*table1)
    z_send(*zt1)
    xy1_add(*b0_q2)
    ag_own(1)
    zf_sum(*zft)
    xy1_send(*ft)
    zk_send(*z0, 0)
    zk_send(*z0, 1)
    ag_relay(2)
    xy1_add(*b0_q3)
    z_sum(*zt1)
    table_out(1)
    xy1_add(*ft)
    xy2_add(*b0_q2)
    zk_send(*z0, 2)
    xy2_add(*ft)
    table_out(0)
    ag_relay(1)
    xy2_add(*b0_q3)
    zk_send(*z0, 3)
    table_in(1, 1)
    table_relay(1, 0)
    table_in(1, 2)
    table_in(1, 3)
    table_relay(1, 1)
    ag_finish(2)
    table_in(0, 1)
    table_relay(0, 0)
    table_in(0, 2)
    table_in(0, 3)
    table_relay(1, 2)
    table_relay(1, 3)
    z_sum(*z0)
    ag_own(0)
    ag_finish(1)
    table_finish(1, 0)
    table_relay(0, 1)
    table_finish(1, 1)
    table_relay(0, 2)
    table_finish(1, 2)
    table_relay(0, 3)
    table_finish(1, 3)
    ag_relay(0)
    table_finish(0, 0)
    table_finish(0, 1)
    table_finish(0, 2)
    table_finish(0, 3)
    ag_finish(0)

    hidden_copy.wait()
    for j in range(3):
        wait_send(bias.at[0], bs.at[j])
    for n in range(12):
        wait_send(core_land.at[0], ks.at[n])
    for h in range(2):
        wait_send(core_land_t.at[h], ks.at[12 + h])
    for group in (b2_low, b2_high, b1_low, b1_high, b0_low, b0_q2, b0_q3, table1, f2, ft):
        xy_rs_drain(*group[3:])
    for group in (z0, z1, z2, zt1):
        z_drain_sum(*group[2:])
    z_drain_sum(zlf, 7)
    z_drain_sum(zlft, 3)
    z_drain_sum(zlt, 5)
    z_drain_sum(zlt, 6)
    for b in range(3):
        xy_drain(back[b], 9 + b)
        xy_done(back[b], 9 + b)
    for h in range(2):
        for j in range(4):
            ref = GT.at[h, (t + 4 - j) % 4]
            xy_drain(ref, 12 + 4 * h + j)
            xy_done(ref, 12 + 4 * h + j)


def finish(
    G,
    GT,
    table_x,
    table_y,
    in_w,
    out_w,
    up_w,
    down_w,
    in_b,
    out_b,
    up_b,
    down_b,
    gain,
    nbias,
    wide_w,
    wide_t,
    full_w,
    full_t,
    sem_in,
    sem_out,
):
    t = lax.axis_index("tensor")
    places = [in_w.at[0], in_w.at[1], in_w.at[2], out_w]
    places += [ref.at[pl.ds(192 * i, 192)] for ref in (up_w, down_w) for i in range(4)]
    tables = [ref.at[pl.ds(256 * i, 256)] for ref in (table_x, table_y) for i in range(4)]
    ins = [pltpu.make_async_copy(GT.at[i], wide_t.at[i], sem_in.at[12 + i]) for i in range(8)]
    ins = [pltpu.make_async_copy(G.at[i], wide_w.at[i], sem_in.at[i]) for i in range(12)] + ins
    outs = [pltpu.make_async_copy(full_w.at[i], places[i], sem_out.at[i]) for i in range(12)]
    outs += [pltpu.make_async_copy(full_t.at[i], tables[i], sem_out.at[12 + i]) for i in range(8)]
    for copy in ins:
        copy.start()
    for i in range(12):
        ins[i].wait()
        full_w[i] = wide_w[i].astype(f32)
        outs[i].start()
    for i in range(8):
        ins[12 + i].wait()
        full_t[i] = wide_t[i].astype(f32)
        if i == 3:
            small = wide_t[3, 240:256].astype(f32)
            full_t[3, 240:256, :] = jnp.zeros((16, 768), f32)
            gain[...] = small[2:4]
            nbias[...] = small[4:6]
            out_b[...] = small[0]
            down_b[...] = small[1]
            level = lax.broadcasted_iota(jnp.int32, (16, 1), 0)
            up_b[...] = jnp.sum(jnp.where(level == 6 + t, small, 0.0), axis=0)
            row = jnp.sum(jnp.where(level == 10 + t, small, 0.0), axis=0, keepdims=True)
            in_b[0:1, :] = row[:, 0:192]
            in_b[1:2, :] = row[:, 384:576]
        outs[12 + i].start()
    for copy in outs:
        copy.wait()


def on_device(
    dp,
    hidden,
    page_boxes,
    lengths,
    table_x,
    table_y,
    in_weight,
    in_bias,
    out_weight,
    out_bias,
    up_weight,
    up_bias,
    down_weight,
    down_bias,
    norm_gain,
    norm_bias,
    cotangent,
):
    blocks = (2, 2, 2, 2)
    vmem = pl.BlockSpec(memory_space=pltpu.VMEM)
    anywhere = pl.BlockSpec(memory_space=pl.ANY)
    dma = pltpu.SemaphoreType.DMA
    count = max(1, (dp // 8).bit_length() - 1)
    V = pltpu.VMEM

    def lands(quarters, rows):
        first, second = V((quarters, 2, rows, 768), bf16), V((quarters, rows, 768), bf16)
        return [first, first, second, second]

    scratch = [
        V((3, 4, *blocks, R, 768), bf16),
        V((4, *blocks, R, 768), bf16),
        V((2048, 768), bf16),
        V((8, *blocks, RT, 768), bf16),
        V((4, 512, 768), bf16),
        V((4, 512, 576), bf16),
        V((4, 512, 192), bf16),
        V((4, 8, 512), f32),
        V((512, 768), bf16),
        V((512, 768), bf16),
        V((512, 768), bf16),
        V((512, 768), bf16),
        V((512, 768), f32),
        V((512, 768), f32),
        V((512, 768), f32),
        V((512, 1), f32),
        V((4, 8, 768), f32),
        V((16, 768), f32),
        V((6, 2, 2, 2, R, 768), bf16),
        V((2, 4, 2, 2, 2, RT, 768), bf16),
        lands(4, R),
        lands(4, R),
        lands(4, XR),
        lands(4, RT),
        lands(1, FR),
        lands(1, RT),
        V((3, 2, R, 768), bf16),
        V((3, 2, R, 768), bf16),
        V((3, 2, XR, 768), bf16),
        V((3, 2, RT, 768), bf16),
        V((3, 2, 2, 2, FR, 768), bf16),
        V((3, 2, 2, 2, RT, 768), bf16),
        V((count, 2, R, 768) if dp > 8 else (8, 128), bf16),
        V((count, 2, RT, 768) if dp > 8 else (8, 128), bf16),
        dma((15,)),
        dma((3,)),
        dma((3,)),
        dma((3, 5, 2)),
        dma((3, 4, 2)),
        dma((20, 6)),
        dma((20, 6)),
        dma((20,)),
        dma((20,)),
        dma((14,)),
        dma((14,)),
        pltpu.SemaphoreType.REGULAR,
        dma((10, 4)),
        dma((10, 4)),
        dma((8, 3)),
        dma((8, 3)),
        dma((5, count)),
        dma((5, count)),
    ]
    shape = jax.ShapeDtypeStruct
    made_out, made_hidden, G, GT = pl.pallas_call(
        partial(kernel, dp),
        out_shape=(
            shape((512, 768), bf16),
            shape((512, 768), f32),
            shape((3, *blocks, R, 768), bf16),
            shape((2, 4, *blocks, RT, 768), bf16),
        ),
        in_specs=[
            anywhere,
            vmem,
            pl.BlockSpec(memory_space=pltpu.SMEM),
            anywhere,
            anywhere,
            anywhere,
            vmem,
            anywhere,
            vmem,
            anywhere,
            vmem,
            anywhere,
            vmem,
            vmem,
            vmem,
            anywhere,
        ],
        out_specs=(anywhere,) * 4,
        scratch_shapes=scratch,
        compiler_params=pltpu.CompilerParams(
            collective_id=0, has_side_effects=True, vmem_limit_bytes=58 * 2**20
        ),
    )(
        hidden,
        page_boxes.T,
        lengths,
        table_x,
        table_y,
        in_weight.transpose(0, 2, 1).reshape(3, 2, 2, R, 768),
        in_bias,
        out_weight.reshape(2, 2, R, 768),
        out_bias,
        up_weight.reshape(*blocks, R, 768),
        up_bias,
        down_weight.reshape(*blocks, R, 768),
        down_bias,
        norm_gain,
        norm_bias,
        cotangent,
    )
    outs = pl.pallas_call(
        finish,
        out_shape=(
            shape((1024, 768), f32),
            shape((1024, 768), f32),
            shape((3, 192, 768), f32),
            shape((192, 768), f32),
            shape((768, 768), f32),
            shape((768, 768), f32),
            shape((2, 192), f32),
            shape((768,), f32),
            shape((768,), f32),
            shape((768,), f32),
            shape((2, 768), f32),
            shape((2, 768), f32),
        ),
        in_specs=[pl.BlockSpec(memory_space=pltpu.HBM)] * 2,
        out_specs=(anywhere,) * 6 + (vmem,) * 6,
        scratch_shapes=[
            V((12, 192, 768), bf16),
            V((8, 256, 768), bf16),
            V((12, 192, 768), f32),
            V((8, 256, 768), f32),
            dma((20,)),
            dma((20,)),
        ],
        compiler_params=pltpu.CompilerParams(vmem_limit_bytes=62 * 2**20),
    )(G.reshape(12, 192, 768), GT.reshape(8, 256, 768))
    out, hidden_grad, outs = lax.optimization_barrier((made_out, made_hidden, outs))
    tx, ty, in_w, out_w, up_w, down_w, in_b, out_b, up_b, down_b, gains, biases = outs
    in_w = in_w.transpose(0, 2, 1)
    return out, hidden_grad, tx, ty, in_w, in_b, out_w, out_b, up_w, up_b, down_w, down_b, gains, biases


def solution(mesh):
    both = ("dp", "tensor")
    in_specs = (
        P(both, None),
        P(both, None),
        P("dp"),
        P(),
        P(),
        P(None, None, "tensor"),
        P(None, "tensor"),
        P("tensor", None),
        P(),
        P(None, "tensor"),
        P("tensor"),
        P("tensor", None),
        P(),
        P(),
        P(),
        P(both, None),
    )
    out_specs = (
        P(both, None),
        P(both, None),
        P(),
        P(),
        P(None, None, "tensor"),
        P(None, "tensor"),
        P("tensor", None),
        P(),
        P(None, "tensor"),
        P("tensor"),
        P("tensor", None),
        P(),
        P(),
        P(),
    )
    return jax.shard_map(
        partial(on_device, mesh.shape["dp"]),
        mesh=mesh,
        in_specs=in_specs,
        out_specs=out_specs,
        check_vma=False,
    )
```

```python
from functools import partial

import jax
import jax.numpy as jnp
from jax import lax
from jax.experimental import pallas as pl
from jax.experimental.pallas import tpu as pltpu
from jax.sharding import PartitionSpec as P

HEAD = 64
EPS = 1e-12
MESH = pl.DeviceIdType.MESH
f32 = jnp.float32
bf16 = jnp.bfloat16

R = 48
RT = 16
FR = 16
XR = R - FR
ZR = 16


def dot(a, b, ca, cb):
    return lax.dot_general(a, b, (((ca,), (cb,)), ((), ())), preferred_element_type=f32)


def kernel(
    dp,
    hidden,
    boxes,
    lengths,
    tables_x,
    tables_y,
    in_w,
    in_b,
    out_w,
    out_b,
    up_w,
    up_b,
    down_w,
    down_b,
    gain,
    nbias,
    cotangent,
    layer_out,
    grad_hidden,
    G,
    GT,
    W,
    G2,
    pre,
    act,
    gp,
    qkv,
    ctx,
    lse,
    resb,
    midb,
    bgrad,
    hid,
    res,
    total,
    n1,
    r1,
    bias,
    vec,
    core_land,
    core_land_t,
    lands0,
    lands1,
    lands2,
    lands_t,
    lands_f,
    lands_ft,
    zl0,
    zl1,
    zl2,
    zlt,
    zlf,
    zlft,
    extra,
    extra_t,
    loc,
    bs,
    br,
    gzs,
    gzr,
    gds,
    gdr,
    xs,
    xr,
    cs,
    cr,
    ks,
    kr,
    credit,
    rs,
    rr,
    zs,
    zr,
    es,
    er,
):
    d = lax.axis_index("dp")
    t = lax.axis_index("tensor")
    c = d % 2
    x = (d // 2) % 2
    y = (d // 4) % 2
    X = (d + 2 - 4 * x, t)
    Y = (d + 4 - 8 * y, t)
    C = (d + 1 - 2 * c, t)
    extras = []
    step = 8
    while step < dp:
        extras.append((d + step - 2 * step * ((d // step) % 2), t))
        step *= 2

    def remote(src, dst, send, recv, dev):
        return pltpu.make_async_remote_copy(
            src_ref=src, dst_ref=dst, send_sem=send, recv_sem=recv, device_id=dev, device_id_type=MESH
        )

    def wait_recv(ref, sem):
        remote(ref, ref, sem, sem, C).wait_recv()

    def wait_send(ref, sem):
        remote(ref, ref, sem, sem, C).wait_send()

    barrier = pltpu.get_barrier_semaphore()
    zpeers = [(d, (t + j) % 4) for j in range(1, 4)]
    peers = [X, Y, C] + zpeers + extras
    for peer in peers:
        pl.semaphore_signal(barrier, inc=1, device_id=peer, device_id_type=MESH)

    local = [
        pltpu.make_async_copy(in_w.at[pl.ds(0, 2)], W.at[0, t, 0], loc.at[0]),
        pltpu.make_async_copy(tables_x, pre.at[pl.ds(0, 1024)], loc.at[1]),
        pltpu.make_async_copy(tables_y, pre.at[pl.ds(1024, 1024)], loc.at[2]),
        pltpu.make_async_copy(hidden, hid, loc.at[3]),
        pltpu.make_async_copy(out_w, W.at[0, t, 1, 1], loc.at[4]),
        pltpu.make_async_copy(up_w, W.at[1, t], loc.at[5]),
        pltpu.make_async_copy(down_w, W.at[2, t], loc.at[6]),
        pltpu.make_async_copy(in_w.at[2], W.at[0, t, 1, 0], loc.at[7]),
    ]
    for i in (0, 7, 4, 1, 2, 3, 5, 6):
        local[i].start()
    bias[t] = jnp.zeros((8, 768), f32)
    bias[t, 0:1, :] = up_b[...].reshape(1, 768)
    bias[t, 1:2, 0:192] = in_b[0:1, :]
    bias[t, 1:2, 384:576] = in_b[1:2, :]
    def entry_local():
        local[0].wait()
        local[4].wait()
        local[7].wait()

    def entry_barrier():
        pl.semaphore_wait(barrier, len(peers))

    entry_barrier()
    entry_local()

    half = t // 2
    near = t * (1 - half) + (3 - t) * half

    def other(j):
        base = j + 1 - near * ((3 - j) // 3)
        return base * (1 - half) + (3 - base) * half

    def z_own(src, dst, ss, rsem):
        @pl.when(t > 0)
        def _():
            remote(src, dst, ss(0), rsem, (d, t - 1)).start()

        @pl.when(t < 3)
        def _():
            remote(src, dst, ss(1), rsem, (d, t + 1)).start()

    def z_arrive(ref, tp, send, recv):
        wait_recv(ref, recv)

        @pl.when(jnp.logical_and(tp < t, t < 3))
        def _():
            remote(ref, ref, send, recv, (d, t + 1)).start()

        @pl.when(jnp.logical_and(tp > t, t > 0))
        def _():
            remote(ref, ref, send, recv, (d, t - 1)).start()

    def z_drain(ref, ss):
        @pl.when(t > 0)
        def _():
            wait_send(ref, ss(0))

        @pl.when(t < 3)
        def _():
            wait_send(ref, ss(1))

    def z_arrive_drain(ref, tp, send):
        @pl.when(jnp.logical_or(jnp.logical_and(tp < t, t < 3), jnp.logical_and(tp > t, t > 0)))
        def _():
            wait_send(ref, send)

    def xy_own(src, dst, i):
        a, b = src.at[0], src.at[1]
        da, db = dst.at[c, y, x, 0], dst.at[c, y, x, 1]
        remote(a, da, xs.at[i, 0], xr.at[i, 0], X).start()
        remote(b, db, xs.at[i, 2], xr.at[i, 2], Y).start()
        remote(a, da, xs.at[i, 1], xr.at[i, 1], Y).start()
        remote(b, db, xs.at[i, 3], xr.at[i, 3], X).start()

    def xy_relay(ref, i, ra=slice(None), rb=slice(None)):
        a, b = ref.at[c, y, 1 - x, 0, ra], ref.at[c, 1 - y, x, 1, rb]
        wait_recv(a, xr.at[i, 0])
        remote(a, a, xs.at[i, 4], xr.at[i, 4], Y).start()
        wait_recv(b, xr.at[i, 2])
        remote(b, b, xs.at[i, 5], xr.at[i, 5], X).start()

    def xy_finish(ref, i, ra=slice(None), rb=slice(None)):
        wait_recv(ref.at[c, 1 - y, x, 0, ra], xr.at[i, 1])
        wait_recv(ref.at[c, y, 1 - x, 1, rb], xr.at[i, 3])
        wait_recv(ref.at[c, 1 - y, 1 - x, 0, ra], xr.at[i, 4])
        wait_recv(ref.at[c, 1 - y, 1 - x, 1, rb], xr.at[i, 5])
        remote(ref.at[c], ref.at[c], cs.at[i], cr.at[i], C).start()

    def xy_done(ref, i):
        wait_recv(ref.at[1 - c], cr.at[i])

    def xy_drain(ref, i, ra=slice(None), rb=slice(None)):
        for k in range(6):
            wait_send(ref.at[c, 0, 0, 0, ra if k in (0, 1, 4) else rb], xs.at[i, k])
        wait_send(ref.at[c], cs.at[i])

    def rows_of(b, h):
        return pl.ds(0, R - ZR) if b + h == 2 else pl.ds(0, R)

    def both(b):
        return rows_of(b, 0), rows_of(b, 1)

    def whole(b, tp):
        return W.at[b, tp, c, :, :, 2 - b, pl.ds(R - ZR, ZR)]

    def whole_own(b):
        z_own(whole(b, t), whole(b, t), lambda k: gds.at[b - 1, k], gdr.at[b - 1, t])

    def whole_in(i):
        b, j = i // 3, i % 3
        z_arrive(whole(b, other(j)), other(j), gds.at[b - 1, 2 + j], gdr.at[b - 1, other(j)])

    def gz_own(b):
        for h in range(2):
            ref = W.at[b, t, c, y, x, h, rows_of(b, h)]
            z_own(ref, ref, lambda k: gzs.at[b, k, h], gzr.at[b, t, h])

    def gz_end(b):
        @pl.when(jnp.logical_or(t == 0, t == 3))
        def _():
            gz_own(b)

    def gz_middle(b):
        @pl.when(jnp.logical_and(t > 0, t < 3))
        def _():
            gz_own(b)

    def e1(i):
        b, j = i // 3, i % 3
        tp = other(j)
        for h in range(2):
            ref = W.at[b, tp, c, y, x, h, rows_of(b, h)]
            z_arrive(ref, tp, gzs.at[b, 2 + j, h], gzr.at[b, tp, h])
            for dev, k in ((X, 0), (Y, 1)) if h == 0 else ((Y, 2), (X, 3)):
                remote(ref, ref, xs.at[i, k], xr.at[i, k], dev).start()

    def e2(i):
        xy_relay(W.at[i // 3, other(i % 3)], i, *both(i // 3))

    def e3(i):
        xy_finish(W.at[i // 3, other(i % 3)], i, *both(i // 3))

    def e4(i):
        xy_done(W.at[i // 3, other(i % 3)], i)

    gz_own(0)
    for j in range(3):
        remote(bias.at[t], bias.at[t], bs.at[j], br.at[2 - j], zpeers[j]).start()

    def one_hot(first, second, levels):
        return ((first == levels).astype(f32) + (second == levels).astype(f32)).astype(bf16)

    levels = lax.broadcasted_iota(jnp.int32, (1024, 1), 0)

    def embed():
        for i in (1, 2, 3):
            local[i].wait()
        horizontal = one_hot(boxes[0:1], boxes[2:3], levels)
        vertical = one_hot(boxes[1:2], boxes[3:4], levels)
        residual = (
            hid[...].astype(f32)
            + dot(horizontal, pre[0:1024, :], 0, 0)
            + dot(vertical, pre[1024:2048, :], 0, 0)
        )
        res[...] = residual
        resb[...] = residual.astype(bf16)
        total[...] = jnp.zeros_like(total)

    embed()
    local[5].wait()
    local[6].wait()
    cot_copy = pltpu.make_async_copy(cotangent, hid, loc.at[3])
    cot_copy.start()

    def biases():
        for j in range(3):
            tz = (t + 3 - j) % 4
            wait_recv(bias.at[tz], br.at[2 - j])

    length = lengths[t]
    visible = lax.broadcasted_iota(jnp.int32, (512, 1), 0) < length
    scaling = HEAD**-0.5

    def project(tp):
        weight = W[0, tp].reshape(768, 768)
        qkv[tp] = (dot(resb[...], weight[0:576], 1, 1) + bias[tp, 1:2, 0:576]).astype(bf16)

    def heads(tp):
        for j in range(3):
            q = qkv[tp, :, j * 64 : (j + 1) * 64]
            k = qkv[tp, :, 192 + j * 64 : 192 + (j + 1) * 64]
            v = qkv[tp, :, 384 + j * 64 : 384 + (j + 1) * 64]
            scores = jnp.where(visible, dot(k, q, 1, 1) * scaling, -1e30)
            top = jnp.max(scores, axis=0, keepdims=True)
            exponent = jnp.exp(scores - top)
            sums = jnp.sum(exponent, axis=0, keepdims=True)
            attend = (exponent * (1.0 / sums)).astype(bf16)
            ctx[tp, :, j * 64 : (j + 1) * 64] = dot(attend, v, 0, 0).astype(bf16)
            lse[tp, j : j + 1, :] = top + jnp.log(sums)
        total[...] += dot(ctx[tp], W[0, tp, 1, 1].reshape(192, 768), 1, 0)

    def up(tp):
        hidden_pre = dot(midb[...], W[1, tp].reshape(768, 768), 1, 0) + bias[tp, 0:1, :]
        cdf = 0.5 * (1.0 + lax.erf(hidden_pre * 0.7071067811865476))
        act[pl.ds(2 * tp, 2)] = (hidden_pre * cdf).astype(bf16).reshape(2, 2, 2, 2, 2, RT, 768)
        slope = cdf + hidden_pre * jnp.exp(-0.5 * hidden_pre * hidden_pre) * 0.3989422804014327
        gp[tp] = slope.astype(bf16)

    def down(tp):
        total[...] += dot(act[pl.ds(2 * tp, 2)].reshape(512, 768), W[2, tp].reshape(768, 768), 1, 0)

    def normalize(value):
        average = jnp.mean(value, axis=-1, keepdims=True)
        centered = value - average
        inverse = lax.rsqrt(jnp.mean(centered * centered, axis=-1, keepdims=True) + EPS)
        return centered * inverse, inverse

    def normalize_back(gradient, normed, inverse, gain_row):
        scaled = gradient * gain_row
        inner = (
            scaled
            - jnp.mean(scaled, axis=-1, keepdims=True)
            - normed * jnp.mean(scaled * normed, axis=-1, keepdims=True)
        )
        return inverse * inner

    def row_sum(value):
        return jnp.sum(value, axis=0, keepdims=True)

    def out_norm():
        normed, inverse = normalize(res[...] + total[...] + out_b[...].reshape(1, 768))
        n1[...] = normed
        r1[...] = inverse
        middle = normed * gain[0:1] + nbias[0:1]
        res[...] = middle
        midb[...] = middle.astype(bf16)
        total[...] = jnp.zeros_like(total)

    def drain_items(b):
        def one(j, _):
            xy_drain(W.at[0, 0], 3 * b + j, *both(b))
            return 0

        lax.fori_loop(0, 3, one, 0)

    def drain_z(b):
        for h in range(2):
            ref = W.at[0, 0, 0, 0, 0, 0, rows_of(b, h)]
            z_drain(ref, lambda k: gzs.at[b, k, h])
            for j in range(3):
                z_arrive_drain(ref, other(j), gzs.at[b, 2 + j, h])

    def drain_whole(b):
        z_drain(whole(b, 0), lambda k: gds.at[b - 1, k])
        for j in range(3):
            z_arrive_drain(whole(b, 0), other(j), gds.at[b - 1, 2 + j])

    def events(k, *turns):
        for turn, calls in enumerate(turns):
            if calls:

                @pl.when(k == turn)
                def _(calls=calls):
                    for call, *given in calls:
                        call(*given)

    def quarter(k):
        own = (3 - k) // 3
        return own * t + (1 - own) * other(k - 1)

    e1(0)
    e1(1)
    gz_end(1)
    e2(0)
    e1(2)
    gz_middle(1)
    e2(1)
    biases()

    def attend(k, _):
        tp = quarter(k)
        project(tp)
        events(
            k,
            [(e2, 2)],
            [(e1, 4), (whole_own, 1), (gz_end, 2), (e3, 1)],
            [(e3, 2)],
            [(e1, 7), (e2, 5), (whole_in, 3)],
        )
        heads(tp)
        events(
            k,
            [(e3, 0), (e1, 3), (e4, 0)],
            [(e1, 5), (gz_middle, 2), (e2, 3), (e4, 1)],
            [(e2, 4), (e1, 6), (e4, 2)],
            [(e1, 8), (whole_own, 2), (e3, 3)],
        )
        return 0

    def widen(k, _):
        up(quarter(k))
        events(
            k,
            [(e4, 3), (whole_in, 4), (e3, 4)],
            [(e2, 7), (whole_in, 5), (e3, 5), (e4, 4), (whole_in, 6)],
            [(e2, 8), (whole_in, 7), (e3, 6), (e4, 5)],
        )
        return 0

    def drain_early():
        drain_items(0)
        drain_items(1)
        for b in range(3):
            drain_z(b)
        drain_whole(1)

    def drain_late():
        drain_items(2)
        drain_whole(2)

    def narrow(k, _):
        down(quarter(k))
        events(k, [(e3, 7), (whole_in, 8), (drain_early,), (e4, 6)], [(e3, 8), (e4, 7)], [(e4, 8)])
        return 0

    lax.fori_loop(0, 4, attend, 0)
    out_norm()
    e2(6)
    lax.fori_loop(0, 4, widen, 0)
    lax.fori_loop(0, 4, narrow, 0)

    normed, inverse = normalize(res[...] + total[...] + down_b[...].reshape(1, 768))
    pre[1536:2048, :] = (normed * gain[1:2] + nbias[1:2]).astype(bf16)
    out_copy = pltpu.make_async_copy(pre.at[pl.ds(1536, 512)], layer_out, loc.at[8])
    out_copy.start()
    cot_copy.wait()
    gradient = hid[...].astype(f32)
    final_grad = normalize_back(gradient, normed, inverse, gain[1:2])
    res[...] = final_grad
    bgrad[...] = final_grad.astype(bf16)
    vec[...] = jnp.zeros_like(vec)
    vec[1:2, :] = row_sum(bgrad[...].astype(f32))
    vec[3:4, :] = row_sum(gradient * normed)
    vec[5:6, :] = row_sum(gradient)

    def core_send(ref, n, tp):
        remote(ref.at[tp, 1 - c], core_land.at[n % 6], ks.at[n], kr.at[n], C).start()

    def core_add(ref, n, tp):
        wait_recv(core_land.at[n % 6], kr.at[n])
        ref[tp, c] = ref[tp, c] + core_land[n % 6]

    def free():
        pl.semaphore_signal(credit, inc=1, device_id=C, device_id_type=MESH)

    def wait_free():
        pl.semaphore_wait(credit, 1)

    def xy1_send(ref, part, rows, lands, lp, g):
        a = ref.at[part, c, :, 1 - x, 0, rows]
        b = ref.at[part, c, 1 - y, :, 1, rows]
        remote(a, lands[0].at[lp], rs.at[g, 0], rr.at[g, 0], X).start()
        remote(b, lands[1].at[lp], rs.at[g, 1], rr.at[g, 1], Y).start()

    def xy1_add(ref, part, rows, lands, lp, g):
        wait_recv(lands[0].at[lp], rr.at[g, 0])
        ref[part, c, :, x, 0, rows] = ref[part, c, :, x, 0, rows] + lands[0][lp]
        remote(ref.at[part, c, 1 - y, x, 0, rows], lands[3].at[lp], rs.at[g, 3], rr.at[g, 3], Y).start()
        wait_recv(lands[1].at[lp], rr.at[g, 1])
        ref[part, c, y, :, 1, rows] = ref[part, c, y, :, 1, rows] + lands[1][lp]
        remote(ref.at[part, c, y, 1 - x, 1, rows], lands[2].at[lp], rs.at[g, 2], rr.at[g, 2], X).start()

    def xy2_add(ref, part, rows, lands, lp, g):
        wait_recv(lands[3].at[lp], rr.at[g, 3])
        ref[part, c, y, x, 0, rows] = ref[part, c, y, x, 0, rows] + lands[3][lp]
        wait_recv(lands[2].at[lp], rr.at[g, 2])
        ref[part, c, y, x, 1, rows] = ref[part, c, y, x, 1, rows] + lands[2][lp]

    def xy_rs_drain(lands, lp, g):
        for k in range(4):
            wait_send(lands[k].at[lp], rs.at[g, k])

    def z_send(ref, rows, land, g):
        for j in range(1, 4):
            k = (t + j) % 4
            remote(ref.at[k, c, y, x, :, rows], land.at[j - 1], zs.at[g, j - 1], zr.at[g, j - 1], (d, k)).start()

    def zk_send(ref, rows, land, g, k):
        @pl.when(t != k)
        def _():
            slot = (k - t + 3) % 4
            remote(ref.at[k, c, y, x, :, rows], land.at[slot], zs.at[g, slot], zr.at[g, slot], (d, k)).start()

    def z_sum(ref, rows, land, g):
        for j in range(3):
            wait_recv(land.at[j], zr.at[g, j])
        value = ref[t, c, y, x, :, rows].astype(f32)
        for j in range(3):
            value = value + land[j].astype(f32)
        ref[t, c, y, x, :, rows] = value.astype(bf16)

    def z_drain_sum(land, g):
        for j in range(3):
            wait_send(land.at[j], zs.at[g, j])

    def zf_send(ref, rows, land, g, k):
        @pl.when(t != k)
        def _():
            slot = (k - t + 3) % 4
            remote(ref.at[k, c, :, :, :, rows], land.at[slot], zs.at[g, slot], zr.at[g, slot], (d, k)).start()

    def zf_sum(ref, rows, land, g):
        for j in range(3):
            wait_recv(land.at[j], zr.at[g, j])
        value = ref[t, c, :, :, :, rows].astype(f32)
        for j in range(3):
            value = value + land[j].astype(f32)
        ref[t, c, :, :, :, rows] = value.astype(bf16)

    def across(ref, land, g):
        for i, peer in enumerate(extras):
            copy = remote(ref, land.at[i], es.at[g, i], er.at[g, i], peer)
            copy.start()
            copy.wait()
            ref[...] = ref[...] + land[i]

    g1 = W.at[2]
    g0 = W.at[1]
    low, high, every = pl.ds(0, 2), pl.ds(2, 2), pl.ds(0, 4)
    rows_x, rows_f, rows, rows_t = pl.ds(0, XR), pl.ds(XR, FR), pl.ds(0, R), pl.ds(0, RT)
    tables = [act.at[pl.ds(0, 4)], act.at[pl.ds(4, 4)]]
    b2_low, b2_high = (G2, low, rows_x, lands2, low, 0), (G2, high, rows_x, lands2, high, 1)
    b1_low, b1_high = (g1, low, rows, lands1, low, 2), (g1, high, rows, lands1, high, 3)
    b0_low = (g0, low, rows, lands0, low, 4)
    b0_q2, b0_q3 = (g0, pl.ds(2, 1), rows, lands0, pl.ds(2, 1), 5), (g0, pl.ds(3, 1), rows, lands0, pl.ds(3, 1), 6)
    table1 = (tables[1], every, rows_t, lands_t, every, 8)
    f2, ft = (G2, t, rows_f, lands_f, 0, 9), (tables[0], t, rows_t, lands_ft, 0, 7)
    z0, z1, z2 = (g0, rows, zl0, 0), (g1, rows, zl1, 1), (G2, rows_x, zl2, 2)
    zt1 = (tables[1], rows_t, zlt, 4)
    zf2, zft = (G2, rows_f, zlf, 7), (tables[0], rows_t, zlft, 3)

    def span(i):
        return pl.ds(pl.multiple_of(i * 512, 512), 512)

    def down_grad(i):
        activated = act[pl.ds(2 * i, 2)].reshape(512, 768)
        G2[i] = dot(activated, bgrad[...], 0, 0).astype(bf16).reshape(2, 2, 2, 2, R, 768)
        core_send(G2, i, i)

    def down_act(i):
        grad = dot(bgrad[...], W[2, i].reshape(768, 768), 1, 1).astype(bf16)
        pre_grad = (grad.astype(f32) * gp[i].astype(f32)).astype(bf16)
        pre[span(i), :] = pre_grad
        vec[pl.ds(6 + i, 1), :] = row_sum(pre_grad.astype(f32))

    def down_add(i):
        core_add(G2, i, i)
        free()
        zf_send(*zf2, i)

    def up_grad(i):
        g1[i] = dot(midb[...], pre[span(i), :], 0, 0).astype(bf16).reshape(2, 2, 2, 2, R, 768)

        @pl.when(i >= 2)
        def _():
            wait_free()

        core_send(g1, 4 + i, i)

    def up_act(i):
        res[...] += dot(pre[span(i), :], W[1, i].reshape(768, 768), 1, 1)

    def up_add(i):
        core_add(g1, 4 + i, i)
        if i < 2:
            free()

    def norm_back():
        normed = n1[...]
        gradient = res[...]
        residual_grad = normalize_back(gradient, normed, r1[...], gain[0:1])
        res[...] = residual_grad
        bgrad[...] = residual_grad.astype(bf16)
        vec[0:1, :] = row_sum(bgrad[...].astype(f32))
        vec[2:3, :] = row_sum(gradient * normed)
        vec[4:5, :] = row_sum(gradient)

    def heads_back(i):
        context_grad = dot(bgrad[...], W[0, i, 1, 1].reshape(192, 768), 1, 1).astype(bf16)
        for j in range(3):
            q = qkv[i, :, j * 64 : (j + 1) * 64]
            k = qkv[i, :, 192 + j * 64 : 192 + (j + 1) * 64]
            v = qkv[i, :, 384 + j * 64 : 384 + (j + 1) * 64]
            dc = context_grad[:, j * 64 : (j + 1) * 64]
            scores = jnp.where(visible, dot(k, q, 1, 1) * scaling, -1e30)
            attend = jnp.exp(scores - lse[i, j : j + 1, :])
            prob_grad = dot(v, dc, 1, 1)
            inner = jnp.sum(prob_grad * attend, axis=0, keepdims=True)
            score_grad = (attend * (prob_grad - inner)).astype(bf16)
            value_grad = dot(attend.astype(bf16), dc, 1, 0)
            key_grad = dot(score_grad, q, 1, 0) * scaling
            query_grad = dot(score_grad, k, 0, 0) * scaling
            qkv[i, :, j * 64 : (j + 1) * 64] = query_grad.astype(bf16)
            qkv[i, :, 192 + j * 64 : 192 + (j + 1) * 64] = key_grad.astype(bf16)
            qkv[i, :, 384 + j * 64 : 384 + (j + 1) * 64] = value_grad.astype(bf16)
        grads = qkv[i]
        res[...] += dot(grads, W[0, i].reshape(768, 768)[0:576], 1, 0)
        vec[pl.ds(10 + i, 1), 0:576] = row_sum(grads.astype(f32))

    def in_grad(i):
        made = dot(qkv[i], resb[...], 0, 0).astype(bf16)
        g0[i, 0] = made[0:384].reshape(2, 2, 2, R, 768)
        g0[i, 1, 0] = made[384:576].reshape(2, 2, R, 768)
        g0[i, 1, 1] = dot(ctx[i], bgrad[...], 0, 0).astype(bf16).reshape(2, 2, R, 768)
        wait_free()
        core_send(g0, 8 + i, i)

    def in_add(i):
        core_add(g0, 8 + i, i)

    def table_grad(h):
        if h == 0:
            hid[...] = res[...].astype(bf16)
        hot = one_hot(boxes[h : h + 1], boxes[h + 2 : h + 3], levels)
        made = dot(hot, hid[...], 1, 0).astype(bf16)
        act[4 * h : 4 * h + 4] = made.reshape(4, 2, 2, 2, 2, RT, 768)
        if h == 0:
            act[3, 1, 1, 1, 1] = vec[...].astype(bf16)
        remote(tables[h].at[:, 1 - c], core_land_t.at[h], ks.at[12 + h], kr.at[12 + h], C).start()

    def table_add(h):
        wait_recv(core_land_t.at[h], kr.at[12 + h])
        tables[h][:, c] = tables[h][:, c] + core_land_t[h]
        if h == 0:
            for k in range(4):
                zf_send(*zft, k)

    F = [g0.at[t, c, y, x], g1.at[t, c, y, x], G2.at[t, c, y, x]]
    F += [ref.at[t, c, y, x] for ref in tables]
    back = [G.at[0], G.at[1], G.at[2], GT.at[0, t], GT.at[1, t]]
    item = [9, 10, 11, 12, 16]
    kept = [pltpu.make_async_copy(F[b], back[b].at[c, y, x], loc.at[10 + b]) for b in range(5)]

    def ag_own(b):
        across(F[b], extra_t if b >= 3 else extra, b)
        kept[b].start()
        xy_own(F[b], back[b], item[b])

    def ag_relay(b):
        xy_relay(back[b], item[b])

    def ag_finish(b):
        kept[b].wait()
        xy_finish(back[b], item[b])

    def table_out(h):
        ag_own(3 + h)
        for j in range(1, 4):
            send, recv = zs.at[5 + h, j - 1], zr.at[5 + h, j - 1]
            remote(F[3 + h], GT.at[h, t, c, y, x], send, recv, (d, (t + j) % 4)).start()

    def table_in(h, j):
        ref = GT.at[h, (t + 4 - j) % 4]
        wait_recv(ref.at[c, y, x], zr.at[5 + h, j - 1])
        xy_own(ref.at[c, y, x], ref, 12 + 4 * h + j)

    def table_relay(h, j):
        xy_relay(GT.at[h, (t + 4 - j) % 4], 12 + 4 * h + j)

    def table_finish(h, j):
        if j == 0:
            kept[3 + h].wait()
        xy_finish(GT.at[h, (t + 4 - j) % 4], 12 + 4 * h + j)

    def first_grads(i, _):
        down_grad(i)
        events(i, [], [], [(down_add, 0)], [(down_add, 1), (xy1_send, *b2_low)])
        return 0

    def second_grads(i, _):
        @pl.when(i < 4)
        def _():
            @pl.when(i == 3)
            def _():
                out_copy.wait()

            down_act(i)

        events(
            i,
            [(down_add, 2)],
            [(down_add, 3), (xy1_send, *b2_high), (drain_late,)],
            [],
            [(xy1_add, *b2_low), (up_add, 0)],
            [(up_add, 1), (xy1_send, *b1_low)],
        )

        @pl.when(i >= 1)
        def _():
            up_grad(i - 1)

        return 0

    def third_grads(i, _):
        up_act(i)
        events(
            i,
            [(xy1_add, *b2_high), (up_add, 2)],
            [(up_add, 3), (xy2_add, *b2_low)],
            [],
            [(xy1_send, *b1_high)],
        )
        return 0

    def fourth_grads(i, _):
        heads_back(i)
        events(
            i,
            [(xy1_add, *b1_low), (xy2_add, *b2_high), (z_send, *z2)],
            [(in_add, 0)],
            [(xy2_add, *b1_high), (zk_send, *z1, 2), (zk_send, *z1, 3), (zf_sum, *zf2), (xy1_send, *f2)],
        )

        @pl.when(i < 3)
        def _():
            in_grad(i)

        events(
            i,
            [],
            [
                (xy1_add, *b1_high),
                (xy2_add, *b1_low),
                (zk_send, *z1, 0),
                (zk_send, *z1, 1),
                (in_add, 1),
                (xy1_send, *b0_low),
            ],
        )
        return 0

    lax.fori_loop(0, 4, first_grads, 0)
    lax.fori_loop(0, 5, second_grads, 0)
    lax.fori_loop(0, 4, third_grads, 0)
    norm_back()
    lax.fori_loop(0, 4, fourth_grads, 0)
    hidden_copy = pltpu.make_async_copy(res, grad_hidden, loc.at[9])
    hidden_copy.start()
    xy1_add(*b0_low)
    xy1_add(*f2)
    in_add(2)
    table_grad(0)
    table_grad(1)
    table_add(0)
    in_grad(3)
    table_add(1)
    xy1_send(*table1)
    xy2_add(*b0_low)
    xy2_add(*f2)
    in_add(3)
    z_sum(*z2)
    xy1_add(*table1)
    xy1_send(*b0_q2)
    z_sum(*z1)
    xy2_add(*table1)
    z_send(*zt1)
    xy1_send(*b0_q3)
    ag_own(2)
    xy1_add(*b0_q2)
    ag_own(1)
    zf_sum(*zft)
    xy1_send(*ft)
    z_sum(*zt1)
    table_out(1)
    ag_relay(2)
    xy1_add(*ft)
    xy1_add(*b0_q3)
    xy2_add(*b0_q2)
    xy2_add(*ft)
    table_out(0)
    for k in range(3):
        zk_send(*z0, k)
    ag_relay(1)
    xy2_add(*b0_q3)
    zk_send(*z0, 3)
    table_in(1, 1)
    table_relay(1, 0)
    table_in(1, 2)
    table_in(1, 3)
    table_in(0, 1)
    table_relay(0, 0)
    table_in(0, 2)
    table_in(0, 3)
    ag_finish(2)
    table_relay(1, 1)
    table_relay(1, 2)
    table_relay(1, 3)
    ag_finish(1)
    table_relay(0, 1)
    table_relay(0, 2)
    table_relay(0, 3)
    table_finish(1, 0)
    table_finish(1, 1)
    z_sum(*z0)
    ag_own(0)
    table_finish(1, 2)
    table_finish(1, 3)
    table_finish(0, 0)
    table_finish(0, 1)
    table_finish(0, 2)
    table_finish(0, 3)
    ag_relay(0)
    ag_finish(0)

    hidden_copy.wait()
    for j in range(3):
        wait_send(bias.at[0], bs.at[j])
    for n in range(12):
        wait_send(core_land.at[0], ks.at[n])
    for h in range(2):
        wait_send(core_land_t.at[h], ks.at[12 + h])
    for group in (b2_low, b2_high, b1_low, b1_high, b0_low, b0_q2, b0_q3, table1, f2, ft):
        xy_rs_drain(*group[3:])
    for group in (z0, z1, z2, zt1):
        z_drain_sum(*group[2:])
    z_drain_sum(zlf, 7)
    z_drain_sum(zlft, 3)
    z_drain_sum(zlt, 5)
    z_drain_sum(zlt, 6)
    for b in range(3):
        xy_drain(back[b], 9 + b)
        xy_done(back[b], 9 + b)
    for h in range(2):
        for j in range(4):
            ref = GT.at[h, (t + 4 - j) % 4]
            xy_drain(ref, 12 + 4 * h + j)
            xy_done(ref, 12 + 4 * h + j)


def finish(
    G,
    GT,
    table_x,
    table_y,
    in_w,
    out_w,
    up_w,
    down_w,
    in_b,
    out_b,
    up_b,
    down_b,
    gain,
    nbias,
    wide_w,
    wide_t,
    full_w,
    full_t,
    sem_in,
    sem_out,
):
    t = lax.axis_index("tensor")
    places = [in_w.at[0], in_w.at[1], in_w.at[2], out_w]
    places += [ref.at[pl.ds(192 * i, 192)] for ref in (up_w, down_w) for i in range(4)]
    tables = [ref.at[pl.ds(256 * i, 256)] for ref in (table_x, table_y) for i in range(4)]
    ins = [pltpu.make_async_copy(GT.at[i], wide_t.at[i], sem_in.at[12 + i]) for i in range(8)]
    ins = [pltpu.make_async_copy(G.at[i], wide_w.at[i], sem_in.at[i]) for i in range(12)] + ins
    outs = [pltpu.make_async_copy(full_w.at[i], places[i], sem_out.at[i]) for i in range(12)]
    outs += [pltpu.make_async_copy(full_t.at[i], tables[i], sem_out.at[12 + i]) for i in range(8)]
    for copy in ins:
        copy.start()
    for i in range(12):
        ins[i].wait()
        full_w[i] = wide_w[i].astype(f32)
        outs[i].start()
    for i in range(8):
        ins[12 + i].wait()
        full_t[i] = wide_t[i].astype(f32)
        if i == 3:
            small = wide_t[3, 240:256].astype(f32)
            full_t[3, 240:256, :] = jnp.zeros((16, 768), f32)
            gain[...] = small[2:4]
            nbias[...] = small[4:6]
            out_b[...] = small[0]
            down_b[...] = small[1]
            level = lax.broadcasted_iota(jnp.int32, (16, 1), 0)
            up_b[...] = jnp.sum(jnp.where(level == 6 + t, small, 0.0), axis=0)
            row = jnp.sum(jnp.where(level == 10 + t, small, 0.0), axis=0, keepdims=True)
            in_b[0:1, :] = row[:, 0:192]
            in_b[1:2, :] = row[:, 384:576]
        outs[12 + i].start()
    for copy in outs:
        copy.wait()


def on_device(
    dp,
    hidden,
    page_boxes,
    lengths,
    table_x,
    table_y,
    in_weight,
    in_bias,
    out_weight,
    out_bias,
    up_weight,
    up_bias,
    down_weight,
    down_bias,
    norm_gain,
    norm_bias,
    cotangent,
):
    blocks = (2, 2, 2, 2)
    vmem = pl.BlockSpec(memory_space=pltpu.VMEM)
    anywhere = pl.BlockSpec(memory_space=pl.ANY)
    dma = pltpu.SemaphoreType.DMA
    count = max(1, (dp // 8).bit_length() - 1)
    V = pltpu.VMEM

    def lands(quarters, rows):
        first, second = V((quarters, 2, rows, 768), bf16), V((quarters, rows, 768), bf16)
        return [first, first, second, second]

    scratch = [
        V((3, 4, *blocks, R, 768), bf16),
        V((4, *blocks, R, 768), bf16),
        V((2048, 768), bf16),
        V((8, *blocks, RT, 768), bf16),
        V((4, 512, 768), bf16),
        V((4, 512, 576), bf16),
        V((4, 512, 192), bf16),
        V((4, 8, 512), f32),
        V((512, 768), bf16),
        V((512, 768), bf16),
        V((512, 768), bf16),
        V((512, 768), bf16),
        V((512, 768), f32),
        V((512, 768), f32),
        V((512, 768), f32),
        V((512, 1), f32),
        V((4, 8, 768), f32),
        V((16, 768), f32),
        V((6, 2, 2, 2, R, 768), bf16),
        V((2, 4, 2, 2, 2, RT, 768), bf16),
        lands(4, R),
        lands(4, R),
        lands(4, XR),
        lands(4, RT),
        lands(1, FR),
        lands(1, RT),
        V((3, 2, R, 768), bf16),
        V((3, 2, R, 768), bf16),
        V((3, 2, XR, 768), bf16),
        V((3, 2, RT, 768), bf16),
        V((3, 2, 2, 2, FR, 768), bf16),
        V((3, 2, 2, 2, RT, 768), bf16),
        V((count, 2, R, 768) if dp > 8 else (8, 128), bf16),
        V((count, 2, RT, 768) if dp > 8 else (8, 128), bf16),
        dma((15,)),
        dma((3,)),
        dma((3,)),
        dma((3, 5, 2)),
        dma((3, 4, 2)),
        dma((2, 5)),
        dma((2, 4)),
        dma((20, 6)),
        dma((20, 6)),
        dma((20,)),
        dma((20,)),
        dma((14,)),
        dma((14,)),
        pltpu.SemaphoreType.REGULAR,
        dma((10, 4)),
        dma((10, 4)),
        dma((8, 3)),
        dma((8, 3)),
        dma((5, count)),
        dma((5, count)),
    ]
    shape = jax.ShapeDtypeStruct
    made_out, made_hidden, G, GT = pl.pallas_call(
        partial(kernel, dp),
        out_shape=(
            shape((512, 768), bf16),
            shape((512, 768), f32),
            shape((3, *blocks, R, 768), bf16),
            shape((2, 4, *blocks, RT, 768), bf16),
        ),
        in_specs=[
            anywhere,
            vmem,
            pl.BlockSpec(memory_space=pltpu.SMEM),
            anywhere,
            anywhere,
            anywhere,
            vmem,
            anywhere,
            vmem,
            anywhere,
            vmem,
            anywhere,
            vmem,
            vmem,
            vmem,
            anywhere,
        ],
        out_specs=(anywhere,) * 4,
        scratch_shapes=scratch,
        compiler_params=pltpu.CompilerParams(
            collective_id=0, has_side_effects=True, vmem_limit_bytes=61 * 2**20
        ),
    )(
        hidden,
        page_boxes.T,
        lengths,
        table_x,
        table_y,
        in_weight.transpose(0, 2, 1).reshape(3, 2, 2, R, 768),
        in_bias,
        out_weight.reshape(2, 2, R, 768),
        out_bias,
        up_weight.reshape(*blocks, R, 768),
        up_bias,
        down_weight.reshape(*blocks, R, 768),
        down_bias,
        norm_gain,
        norm_bias,
        cotangent,
    )
    outs = pl.pallas_call(
        finish,
        out_shape=(
            shape((1024, 768), f32),
            shape((1024, 768), f32),
            shape((3, 192, 768), f32),
            shape((192, 768), f32),
            shape((768, 768), f32),
            shape((768, 768), f32),
            shape((2, 192), f32),
            shape((768,), f32),
            shape((768,), f32),
            shape((768,), f32),
            shape((2, 768), f32),
            shape((2, 768), f32),
        ),
        in_specs=[pl.BlockSpec(memory_space=pltpu.HBM)] * 2,
        out_specs=(anywhere,) * 6 + (vmem,) * 6,
        scratch_shapes=[
            V((12, 192, 768), bf16),
            V((8, 256, 768), bf16),
            V((12, 192, 768), f32),
            V((8, 256, 768), f32),
            dma((20,)),
            dma((20,)),
        ],
        compiler_params=pltpu.CompilerParams(vmem_limit_bytes=62 * 2**20),
    )(G.reshape(12, 192, 768), GT.reshape(8, 256, 768))
    out, hidden_grad, outs = lax.optimization_barrier((made_out, made_hidden, outs))
    tx, ty, in_w, out_w, up_w, down_w, in_b, out_b, up_b, down_b, gains, biases = outs
    in_w = in_w.transpose(0, 2, 1)
    return out, hidden_grad, tx, ty, in_w, in_b, out_w, out_b, up_w, up_b, down_w, down_b, gains, biases


def solution(mesh):
    both = ("dp", "tensor")
    in_specs = (
        P(both, None),
        P(both, None),
        P("dp"),
        P(),
        P(),
        P(None, None, "tensor"),
        P(None, "tensor"),
        P("tensor", None),
        P(),
        P(None, "tensor"),
        P("tensor"),
        P("tensor", None),
        P(),
        P(),
        P(),
        P(both, None),
    )
    out_specs = (
        P(both, None),
        P(both, None),
        P(),
        P(),
        P(None, None, "tensor"),
        P(None, "tensor"),
        P("tensor", None),
        P(),
        P(None, "tensor"),
        P("tensor"),
        P("tensor", None),
        P(),
        P(),
        P(),
    )
    return jax.shard_map(
        partial(on_device, mesh.shape["dp"]),
        mesh=mesh,
        in_specs=in_specs,
        out_specs=out_specs,
        check_vma=False,
    )
```

```python
from functools import partial

import jax
import jax.numpy as jnp
from jax import lax
from jax.experimental import pallas as pl
from jax.experimental.pallas import tpu as pltpu
from jax.sharding import PartitionSpec as P

HEAD = 64
EPS = 1e-12
MESH = pl.DeviceIdType.MESH
f32 = jnp.float32
bf16 = jnp.bfloat16

R = 48
RT = 16
FR = 16
XR = R - FR
ZR = 16


def dot(a, b, ca, cb):
    return lax.dot_general(a, b, (((ca,), (cb,)), ((), ())), preferred_element_type=f32)


def kernel(
    dp,
    hidden,
    boxes,
    lengths,
    tables_x,
    tables_y,
    in_w,
    in_b,
    out_w,
    out_b,
    up_w,
    up_b,
    down_w,
    down_b,
    gain,
    nbias,
    cotangent,
    layer_out,
    grad_hidden,
    G,
    GT,
    W,
    G2,
    pre,
    act,
    gp,
    qkv,
    ctx,
    lse,
    resb,
    midb,
    bgrad,
    hid,
    res,
    total,
    n1,
    r1,
    bias,
    vec,
    core_land,
    core_land_t,
    lands0,
    lands1,
    lands2,
    lands_t,
    lands_f,
    lands_ft,
    zl0,
    zl1,
    zl2,
    zlt,
    zlf,
    zlft,
    extra,
    extra_t,
    loc,
    bs,
    br,
    gzs,
    gzr,
    gds,
    gdr,
    xs,
    xr,
    cs,
    cr,
    ks,
    kr,
    credit,
    rs,
    rr,
    zs,
    zr,
    es,
    er,
):
    d = lax.axis_index("dp")
    t = lax.axis_index("tensor")
    c = d % 2
    x = (d // 2) % 2
    y = (d // 4) % 2
    X = (d + 2 - 4 * x, t)
    Y = (d + 4 - 8 * y, t)
    C = (d + 1 - 2 * c, t)
    extras = []
    step = 8
    while step < dp:
        extras.append((d + step - 2 * step * ((d // step) % 2), t))
        step *= 2

    def remote(src, dst, send, recv, dev):
        return pltpu.make_async_remote_copy(
            src_ref=src, dst_ref=dst, send_sem=send, recv_sem=recv, device_id=dev, device_id_type=MESH
        )

    def wait_recv(ref, sem):
        remote(ref, ref, sem, sem, C).wait_recv()

    def wait_send(ref, sem):
        remote(ref, ref, sem, sem, C).wait_send()

    barrier = pltpu.get_barrier_semaphore()
    zpeers = [(d, (t + j) % 4) for j in range(1, 4)]
    peers = [X, Y, C] + zpeers + extras
    for peer in peers:
        pl.semaphore_signal(barrier, inc=1, device_id=peer, device_id_type=MESH)

    local = [
        pltpu.make_async_copy(in_w.at[pl.ds(0, 2)], W.at[0, t, 0], loc.at[0]),
        pltpu.make_async_copy(tables_x, pre.at[pl.ds(0, 1024)], loc.at[1]),
        pltpu.make_async_copy(tables_y, pre.at[pl.ds(1024, 1024)], loc.at[2]),
        pltpu.make_async_copy(hidden, hid, loc.at[3]),
        pltpu.make_async_copy(out_w, W.at[0, t, 1, 1], loc.at[4]),
        pltpu.make_async_copy(up_w, W.at[1, t], loc.at[5]),
        pltpu.make_async_copy(down_w, W.at[2, t], loc.at[6]),
        pltpu.make_async_copy(in_w.at[2], W.at[0, t, 1, 0], loc.at[7]),
    ]
    for i in (0, 7, 4, 1, 2, 3, 5, 6):
        local[i].start()
    bias[t] = jnp.zeros((8, 768), f32)
    bias[t, 0:1, :] = up_b[...].reshape(1, 768)
    bias[t, 1:2, 0:192] = in_b[0:1, :]
    bias[t, 1:2, 384:576] = in_b[1:2, :]
    def entry_local():
        local[0].wait()
        local[4].wait()
        local[7].wait()

    def entry_barrier():
        pl.semaphore_wait(barrier, len(peers))

    entry_barrier()
    entry_local()

    half = t // 2
    near = t * (1 - half) + (3 - t) * half

    def other(j):
        base = j + 1 - near * ((3 - j) // 3)
        return base * (1 - half) + (3 - base) * half

    def z_own(src, dst, ss, rsem):
        @pl.when(t > 0)
        def _():
            remote(src, dst, ss(0), rsem, (d, t - 1)).start()

        @pl.when(t < 3)
        def _():
            remote(src, dst, ss(1), rsem, (d, t + 1)).start()

    def z_arrive(ref, tp, send, recv):
        wait_recv(ref, recv)

        @pl.when(jnp.logical_and(tp < t, t < 3))
        def _():
            remote(ref, ref, send, recv, (d, t + 1)).start()

        @pl.when(jnp.logical_and(tp > t, t > 0))
        def _():
            remote(ref, ref, send, recv, (d, t - 1)).start()

    def z_drain(ref, ss):
        @pl.when(t > 0)
        def _():
            wait_send(ref, ss(0))

        @pl.when(t < 3)
        def _():
            wait_send(ref, ss(1))

    def z_arrive_drain(ref, tp, send):
        @pl.when(jnp.logical_or(jnp.logical_and(tp < t, t < 3), jnp.logical_and(tp > t, t > 0)))
        def _():
            wait_send(ref, send)

    def xy_own(src, dst, i):
        a, b = src.at[0], src.at[1]
        da, db = dst.at[c, y, x, 0], dst.at[c, y, x, 1]
        remote(a, da, xs.at[i, 0], xr.at[i, 0], X).start()
        remote(b, db, xs.at[i, 2], xr.at[i, 2], Y).start()
        remote(a, da, xs.at[i, 1], xr.at[i, 1], Y).start()
        remote(b, db, xs.at[i, 3], xr.at[i, 3], X).start()

    def xy_relay(ref, i, ra=slice(None), rb=slice(None)):
        a, b = ref.at[c, y, 1 - x, 0, ra], ref.at[c, 1 - y, x, 1, rb]
        wait_recv(a, xr.at[i, 0])
        remote(a, a, xs.at[i, 4], xr.at[i, 4], Y).start()
        wait_recv(b, xr.at[i, 2])
        remote(b, b, xs.at[i, 5], xr.at[i, 5], X).start()

    def xy_finish(ref, i, ra=slice(None), rb=slice(None)):
        wait_recv(ref.at[c, 1 - y, x, 0, ra], xr.at[i, 1])
        wait_recv(ref.at[c, y, 1 - x, 1, rb], xr.at[i, 3])
        wait_recv(ref.at[c, 1 - y, 1 - x, 0, ra], xr.at[i, 4])
        wait_recv(ref.at[c, 1 - y, 1 - x, 1, rb], xr.at[i, 5])
        remote(ref.at[c], ref.at[c], cs.at[i], cr.at[i], C).start()

    def xy_done(ref, i):
        wait_recv(ref.at[1 - c], cr.at[i])

    def xy_drain(ref, i, ra=slice(None), rb=slice(None)):
        for k in range(6):
            wait_send(ref.at[c, 0, 0, 0, ra if k in (0, 1, 4) else rb], xs.at[i, k])
        wait_send(ref.at[c], cs.at[i])

    def rows_of(b, h):
        return pl.ds(0, R - ZR) if b + h == 2 else pl.ds(0, R)

    def both(b):
        return rows_of(b, 0), rows_of(b, 1)

    def whole(b, tp):
        return W.at[b, tp, c, :, :, 2 - b, pl.ds(R - ZR, ZR)]

    def whole_own(b):
        z_own(whole(b, t), whole(b, t), lambda k: gds.at[b - 1, k], gdr.at[b - 1, t])

    def whole_in(i):
        b, j = i // 3, i % 3
        z_arrive(whole(b, other(j)), other(j), gds.at[b - 1, 2 + j], gdr.at[b - 1, other(j)])

    def gz_own(b):
        for h in range(2):
            ref = W.at[b, t, c, y, x, h, rows_of(b, h)]
            z_own(ref, ref, lambda k: gzs.at[b, k, h], gzr.at[b, t, h])

    def gz_end(b):
        @pl.when(jnp.logical_or(t == 0, t == 3))
        def _():
            gz_own(b)

    def gz_middle(b):
        @pl.when(jnp.logical_and(t > 0, t < 3))
        def _():
            gz_own(b)

    def e1(i):
        b, j = i // 3, i % 3
        tp = other(j)
        for h in range(2):
            ref = W.at[b, tp, c, y, x, h, rows_of(b, h)]
            z_arrive(ref, tp, gzs.at[b, 2 + j, h], gzr.at[b, tp, h])
            for dev, k in ((X, 0), (Y, 1)) if h == 0 else ((Y, 2), (X, 3)):
                remote(ref, ref, xs.at[i, k], xr.at[i, k], dev).start()

    def e2(i):
        xy_relay(W.at[i // 3, other(i % 3)], i, *both(i // 3))

    def e3(i):
        xy_finish(W.at[i // 3, other(i % 3)], i, *both(i // 3))

    def e4(i):
        xy_done(W.at[i // 3, other(i % 3)], i)

    gz_own(0)
    for j in range(3):
        remote(bias.at[t], bias.at[t], bs.at[j], br.at[2 - j], zpeers[j]).start()

    def one_hot(first, second, levels):
        return ((first == levels).astype(f32) + (second == levels).astype(f32)).astype(bf16)

    levels = lax.broadcasted_iota(jnp.int32, (1024, 1), 0)

    def embed():
        for i in (1, 2, 3):
            local[i].wait()
        horizontal = one_hot(boxes[0:1], boxes[2:3], levels)
        vertical = one_hot(boxes[1:2], boxes[3:4], levels)
        residual = (
            hid[...].astype(f32)
            + dot(horizontal, pre[0:1024, :], 0, 0)
            + dot(vertical, pre[1024:2048, :], 0, 0)
        )
        res[...] = residual
        resb[...] = residual.astype(bf16)
        total[...] = jnp.zeros_like(total)

    embed()
    local[5].wait()
    local[6].wait()
    cot_copy = pltpu.make_async_copy(cotangent, hid, loc.at[3])
    cot_copy.start()

    def biases():
        for j in range(3):
            tz = (t + 3 - j) % 4
            wait_recv(bias.at[tz], br.at[2 - j])

    length = lengths[t]
    visible = lax.broadcasted_iota(jnp.int32, (512, 1), 0) < length
    scaling = HEAD**-0.5

    def project(tp):
        weight = W[0, tp].reshape(768, 768)
        qkv[tp] = (dot(resb[...], weight[0:576], 1, 1) + bias[tp, 1:2, 0:576]).astype(bf16)

    def heads(tp):
        for j in range(3):
            q = qkv[tp, :, j * 64 : (j + 1) * 64]
            k = qkv[tp, :, 192 + j * 64 : 192 + (j + 1) * 64]
            v = qkv[tp, :, 384 + j * 64 : 384 + (j + 1) * 64]
            scores = jnp.where(visible, dot(k, q, 1, 1) * scaling, -1e30)
            top = jnp.max(scores, axis=0, keepdims=True)
            exponent = jnp.exp(scores - top)
            sums = jnp.sum(exponent, axis=0, keepdims=True)
            attend = (exponent * (1.0 / sums)).astype(bf16)
            ctx[tp, :, j * 64 : (j + 1) * 64] = dot(attend, v, 0, 0).astype(bf16)
            lse[tp, j : j + 1, :] = top + jnp.log(sums)
        total[...] += dot(ctx[tp], W[0, tp, 1, 1].reshape(192, 768), 1, 0)

    def up(tp):
        hidden_pre = dot(midb[...], W[1, tp].reshape(768, 768), 1, 0) + bias[tp, 0:1, :]
        cdf = 0.5 * (1.0 + lax.erf(hidden_pre * 0.7071067811865476))
        act[pl.ds(2 * tp, 2)] = (hidden_pre * cdf).astype(bf16).reshape(2, 2, 2, 2, 2, RT, 768)
        slope = cdf + hidden_pre * jnp.exp(-0.5 * hidden_pre * hidden_pre) * 0.3989422804014327
        gp[tp] = slope.astype(bf16)

    def down(tp):
        total[...] += dot(act[pl.ds(2 * tp, 2)].reshape(512, 768), W[2, tp].reshape(768, 768), 1, 0)

    def normalize(value):
        average = jnp.mean(value, axis=-1, keepdims=True)
        centered = value - average
        inverse = lax.rsqrt(jnp.mean(centered * centered, axis=-1, keepdims=True) + EPS)
        return centered * inverse, inverse

    def normalize_back(gradient, normed, inverse, gain_row):
        scaled = gradient * gain_row
        inner = (
            scaled
            - jnp.mean(scaled, axis=-1, keepdims=True)
            - normed * jnp.mean(scaled * normed, axis=-1, keepdims=True)
        )
        return inverse * inner

    def row_sum(value):
        return jnp.sum(value, axis=0, keepdims=True)

    def out_norm():
        normed, inverse = normalize(res[...] + total[...] + out_b[...].reshape(1, 768))
        n1[...] = normed
        r1[...] = inverse
        middle = normed * gain[0:1] + nbias[0:1]
        res[...] = middle
        midb[...] = middle.astype(bf16)
        total[...] = jnp.zeros_like(total)

    def drain_items(b):
        def one(j, _):
            xy_drain(W.at[0, 0], 3 * b + j, *both(b))
            return 0

        lax.fori_loop(0, 3, one, 0)

    def drain_z(b):
        for h in range(2):
            ref = W.at[0, 0, 0, 0, 0, 0, rows_of(b, h)]
            z_drain(ref, lambda k: gzs.at[b, k, h])
            for j in range(3):
                z_arrive_drain(ref, other(j), gzs.at[b, 2 + j, h])

    def drain_whole(b):
        z_drain(whole(b, 0), lambda k: gds.at[b - 1, k])
        for j in range(3):
            z_arrive_drain(whole(b, 0), other(j), gds.at[b - 1, 2 + j])

    def events(k, *turns):
        for turn, calls in enumerate(turns):
            if calls:

                @pl.when(k == turn)
                def _(calls=calls):
                    for call, *given in calls:
                        call(*given)

    def quarter(k):
        own = (3 - k) // 3
        return own * t + (1 - own) * other(k - 1)

    e1(0)
    e1(1)
    gz_end(1)
    e2(0)
    e1(2)
    gz_middle(1)
    e2(1)
    biases()

    def attend(k, _):
        tp = quarter(k)
        project(tp)
        events(
            k,
            [(e2, 2)],
            [(e1, 4), (whole_own, 1), (gz_end, 2), (e3, 1)],
            [(e3, 2)],
            [(e1, 7), (e2, 5), (whole_in, 3)],
        )
        heads(tp)
        events(
            k,
            [(e3, 0), (e1, 3), (e4, 0)],
            [(e1, 5), (gz_middle, 2), (e2, 3), (e4, 1)],
            [(e2, 4), (e1, 6), (e4, 2)],
            [(e1, 8), (whole_own, 2), (e3, 3)],
        )
        return 0

    def widen(k, _):
        up(quarter(k))
        events(
            k,
            [(e4, 3), (whole_in, 4), (e3, 4)],
            [(e2, 7), (whole_in, 5), (e3, 5), (e4, 4), (whole_in, 6)],
            [(e2, 8), (whole_in, 7), (e3, 6), (e4, 5)],
        )
        return 0

    def drain_early():
        drain_items(0)
        drain_items(1)
        for b in range(3):
            drain_z(b)
        drain_whole(1)

    def drain_late():
        drain_items(2)
        drain_whole(2)

    def narrow(k, _):
        down(quarter(k))
        events(k, [(e3, 7), (whole_in, 8), (drain_early,), (e4, 6)], [(e3, 8), (e4, 7)], [(e4, 8)])
        return 0

    lax.fori_loop(0, 4, attend, 0)
    out_norm()
    e2(6)
    lax.fori_loop(0, 4, widen, 0)
    lax.fori_loop(0, 4, narrow, 0)

    normed, inverse = normalize(res[...] + total[...] + down_b[...].reshape(1, 768))
    pre[1536:2048, :] = (normed * gain[1:2] + nbias[1:2]).astype(bf16)
    out_copy = pltpu.make_async_copy(pre.at[pl.ds(1536, 512)], layer_out, loc.at[8])
    out_copy.start()
    cot_copy.wait()
    gradient = hid[...].astype(f32)
    final_grad = normalize_back(gradient, normed, inverse, gain[1:2])
    res[...] = final_grad
    bgrad[...] = final_grad.astype(bf16)
    vec[...] = jnp.zeros_like(vec)
    vec[1:2, :] = row_sum(bgrad[...].astype(f32))
    vec[3:4, :] = row_sum(gradient * normed)
    vec[5:6, :] = row_sum(gradient)

    def core_send(ref, n, tp):
        remote(ref.at[tp, 1 - c], core_land.at[n % 6], ks.at[n], kr.at[n], C).start()

    def core_add(ref, n, tp):
        wait_recv(core_land.at[n % 6], kr.at[n])
        ref[tp, c] = ref[tp, c] + core_land[n % 6]

    def free():
        pl.semaphore_signal(credit, inc=1, device_id=C, device_id_type=MESH)

    def wait_free():
        pl.semaphore_wait(credit, 1)

    def xy1_send(ref, part, rows, lands, lp, g):
        a = ref.at[part, c, :, 1 - x, 0, rows]
        b = ref.at[part, c, 1 - y, :, 1, rows]
        remote(a, lands[0].at[lp], rs.at[g, 0], rr.at[g, 0], X).start()
        remote(b, lands[1].at[lp], rs.at[g, 1], rr.at[g, 1], Y).start()

    def xy1_add(ref, part, rows, lands, lp, g):
        wait_recv(lands[0].at[lp], rr.at[g, 0])
        ref[part, c, :, x, 0, rows] = ref[part, c, :, x, 0, rows] + lands[0][lp]
        remote(ref.at[part, c, 1 - y, x, 0, rows], lands[3].at[lp], rs.at[g, 3], rr.at[g, 3], Y).start()
        wait_recv(lands[1].at[lp], rr.at[g, 1])
        ref[part, c, y, :, 1, rows] = ref[part, c, y, :, 1, rows] + lands[1][lp]
        remote(ref.at[part, c, y, 1 - x, 1, rows], lands[2].at[lp], rs.at[g, 2], rr.at[g, 2], X).start()

    def xy2_add(ref, part, rows, lands, lp, g):
        wait_recv(lands[3].at[lp], rr.at[g, 3])
        ref[part, c, y, x, 0, rows] = ref[part, c, y, x, 0, rows] + lands[3][lp]
        wait_recv(lands[2].at[lp], rr.at[g, 2])
        ref[part, c, y, x, 1, rows] = ref[part, c, y, x, 1, rows] + lands[2][lp]

    def xy_rs_drain(lands, lp, g):
        for k in range(4):
            wait_send(lands[k].at[lp], rs.at[g, k])

    def z_send(ref, rows, land, g):
        for j in range(1, 4):
            k = (t + j) % 4
            remote(ref.at[k, c, y, x, :, rows], land.at[j - 1], zs.at[g, j - 1], zr.at[g, j - 1], (d, k)).start()

    def zk_send(ref, rows, land, g, k):
        @pl.when(t != k)
        def _():
            slot = (k - t + 3) % 4
            remote(ref.at[k, c, y, x, :, rows], land.at[slot], zs.at[g, slot], zr.at[g, slot], (d, k)).start()

    def z_sum(ref, rows, land, g):
        for j in range(3):
            wait_recv(land.at[j], zr.at[g, j])
        value = ref[t, c, y, x, :, rows].astype(f32)
        for j in range(3):
            value = value + land[j].astype(f32)
        ref[t, c, y, x, :, rows] = value.astype(bf16)

    def z_drain_sum(land, g):
        for j in range(3):
            wait_send(land.at[j], zs.at[g, j])

    def zf_send(ref, rows, land, g, k):
        @pl.when(t != k)
        def _():
            slot = (k - t + 3) % 4
            remote(ref.at[k, c, :, :, :, rows], land.at[slot], zs.at[g, slot], zr.at[g, slot], (d, k)).start()

    def zf_sum(ref, rows, land, g):
        for j in range(3):
            wait_recv(land.at[j], zr.at[g, j])
        value = ref[t, c, :, :, :, rows].astype(f32)
        for j in range(3):
            value = value + land[j].astype(f32)
        ref[t, c, :, :, :, rows] = value.astype(bf16)

    def across(ref, land, g):
        for i, peer in enumerate(extras):
            copy = remote(ref, land.at[i], es.at[g, i], er.at[g, i], peer)
            copy.start()
            copy.wait()
            ref[...] = ref[...] + land[i]

    g1 = W.at[2]
    g0 = W.at[1]
    low, high, every = pl.ds(0, 2), pl.ds(2, 2), pl.ds(0, 4)
    rows_x, rows_f, rows, rows_t = pl.ds(0, XR), pl.ds(XR, FR), pl.ds(0, R), pl.ds(0, RT)
    tables = [act.at[pl.ds(0, 4)], act.at[pl.ds(4, 4)]]
    b2_low, b2_high = (G2, low, rows_x, lands2, low, 0), (G2, high, rows_x, lands2, high, 1)
    b1_low, b1_high = (g1, low, rows, lands1, low, 2), (g1, high, rows, lands1, high, 3)
    b0_low = (g0, low, rows, lands0, low, 4)
    b0_q2, b0_q3 = (g0, pl.ds(2, 1), rows, lands0, pl.ds(2, 1), 5), (g0, pl.ds(3, 1), rows, lands0, pl.ds(3, 1), 6)
    table1 = (tables[1], every, rows_t, lands_t, every, 8)
    f2, ft = (G2, t, rows_f, lands_f, 0, 9), (tables[0], t, rows_t, lands_ft, 0, 7)
    z0, z1, z2 = (g0, rows, zl0, 0), (g1, rows, zl1, 1), (G2, rows_x, zl2, 2)
    zt1 = (tables[1], rows_t, zlt, 4)
    zf2, zft = (G2, rows_f, zlf, 7), (tables[0], rows_t, zlft, 3)

    def span(i):
        return pl.ds(pl.multiple_of(i * 512, 512), 512)

    def down_grad(i):
        activated = act[pl.ds(2 * i, 2)].reshape(512, 768)
        G2[i] = dot(activated, bgrad[...], 0, 0).astype(bf16).reshape(2, 2, 2, 2, R, 768)
        core_send(G2, i, i)

    def down_act(i):
        grad = dot(bgrad[...], W[2, i].reshape(768, 768), 1, 1).astype(bf16)
        pre_grad = (grad.astype(f32) * gp[i].astype(f32)).astype(bf16)
        pre[span(i), :] = pre_grad
        vec[pl.ds(6 + i, 1), :] = row_sum(pre_grad.astype(f32))

    def down_add(i):
        core_add(G2, i, i)
        free()
        zf_send(*zf2, i)

    def up_grad(i):
        g1[i] = dot(midb[...], pre[span(i), :], 0, 0).astype(bf16).reshape(2, 2, 2, 2, R, 768)

        @pl.when(i >= 2)
        def _():
            wait_free()

        core_send(g1, 4 + i, i)

    def up_act(i):
        res[...] += dot(pre[span(i), :], W[1, i].reshape(768, 768), 1, 1)

    def up_add(i):
        core_add(g1, 4 + i, i)
        if i < 2:
            free()

    def norm_back():
        normed = n1[...]
        gradient = res[...]
        residual_grad = normalize_back(gradient, normed, r1[...], gain[0:1])
        res[...] = residual_grad
        bgrad[...] = residual_grad.astype(bf16)
        vec[0:1, :] = row_sum(bgrad[...].astype(f32))
        vec[2:3, :] = row_sum(gradient * normed)
        vec[4:5, :] = row_sum(gradient)

    def heads_back(i):
        context_grad = dot(bgrad[...], W[0, i, 1, 1].reshape(192, 768), 1, 1).astype(bf16)
        for j in range(3):
            q = qkv[i, :, j * 64 : (j + 1) * 64]
            k = qkv[i, :, 192 + j * 64 : 192 + (j + 1) * 64]
            v = qkv[i, :, 384 + j * 64 : 384 + (j + 1) * 64]
            dc = context_grad[:, j * 64 : (j + 1) * 64]
            scores = jnp.where(visible, dot(k, q, 1, 1) * scaling, -1e30)
            attend = jnp.exp(scores - lse[i, j : j + 1, :])
            prob_grad = dot(v, dc, 1, 1)
            inner = jnp.sum(prob_grad * attend, axis=0, keepdims=True)
            score_grad = (attend * (prob_grad - inner)).astype(bf16)
            value_grad = dot(attend.astype(bf16), dc, 1, 0)
            key_grad = dot(score_grad, q, 1, 0) * scaling
            query_grad = dot(score_grad, k, 0, 0) * scaling
            qkv[i, :, j * 64 : (j + 1) * 64] = query_grad.astype(bf16)
            qkv[i, :, 192 + j * 64 : 192 + (j + 1) * 64] = key_grad.astype(bf16)
            qkv[i, :, 384 + j * 64 : 384 + (j + 1) * 64] = value_grad.astype(bf16)
        grads = qkv[i]
        res[...] += dot(grads, W[0, i].reshape(768, 768)[0:576], 1, 0)
        vec[pl.ds(10 + i, 1), 0:576] = row_sum(grads.astype(f32))

    def in_grad(i):
        made = dot(qkv[i], resb[...], 0, 0).astype(bf16)
        g0[i, 0] = made[0:384].reshape(2, 2, 2, R, 768)
        g0[i, 1, 0] = made[384:576].reshape(2, 2, R, 768)
        g0[i, 1, 1] = dot(ctx[i], bgrad[...], 0, 0).astype(bf16).reshape(2, 2, R, 768)
        wait_free()
        core_send(g0, 8 + i, i)

    def in_add(i):
        core_add(g0, 8 + i, i)

    def table_grad(h):
        if h == 0:
            hid[...] = res[...].astype(bf16)
        hot = one_hot(boxes[h : h + 1], boxes[h + 2 : h + 3], levels)
        made = dot(hot, hid[...], 1, 0).astype(bf16)
        act[4 * h : 4 * h + 4] = made.reshape(4, 2, 2, 2, 2, RT, 768)
        if h == 0:
            act[3, 1, 1, 1, 1] = vec[...].astype(bf16)
        remote(tables[h].at[:, 1 - c], core_land_t.at[h], ks.at[12 + h], kr.at[12 + h], C).start()

    def table_add(h):
        wait_recv(core_land_t.at[h], kr.at[12 + h])
        tables[h][:, c] = tables[h][:, c] + core_land_t[h]
        if h == 0:
            for k in range(4):
                zf_send(*zft, k)

    F = [g0.at[t, c, y, x], g1.at[t, c, y, x], G2.at[t, c, y, x]]
    F += [ref.at[t, c, y, x] for ref in tables]
    back = [G.at[0], G.at[1], G.at[2], GT.at[0, t], GT.at[1, t]]
    item = [9, 10, 11, 12, 16]
    kept = [pltpu.make_async_copy(F[b], back[b].at[c, y, x], loc.at[10 + b]) for b in range(5)]

    def ag_own(b):
        across(F[b], extra_t if b >= 3 else extra, b)
        kept[b].start()
        xy_own(F[b], back[b], item[b])

    def ag_relay(b):
        xy_relay(back[b], item[b])

    def ag_finish(b):
        kept[b].wait()
        xy_finish(back[b], item[b])

    def table_out(h):
        ag_own(3 + h)
        for j in range(1, 4):
            send, recv = zs.at[5 + h, j - 1], zr.at[5 + h, j - 1]
            remote(F[3 + h], GT.at[h, t, c, y, x], send, recv, (d, (t + j) % 4)).start()

    def table_in(h, j):
        ref = GT.at[h, (t + 4 - j) % 4]
        wait_recv(ref.at[c, y, x], zr.at[5 + h, j - 1])
        xy_own(ref.at[c, y, x], ref, 12 + 4 * h + j)

    def table_relay(h, j):
        xy_relay(GT.at[h, (t + 4 - j) % 4], 12 + 4 * h + j)

    def table_finish(h, j):
        if j == 0:
            kept[3 + h].wait()
        xy_finish(GT.at[h, (t + 4 - j) % 4], 12 + 4 * h + j)

    def drain_first():
        for j in range(3):
            wait_send(bias.at[0], bs.at[j])
        for n in range(12):
            wait_send(core_land.at[0], ks.at[n])
        for h in range(2):
            wait_send(core_land_t.at[h], ks.at[12 + h])
        for group in (b2_low, b2_high, b1_low, b1_high, b0_low, f2, table1):
            xy_rs_drain(*group[3:])
        for group in (z1, z2):
            z_drain_sum(*group[2:])
        z_drain_sum(zlf, 7)

    def drain_second():
        hidden_copy.wait()
        for group in (b0_q2, b0_q3, ft):
            xy_rs_drain(*group[3:])
        z_drain_sum(zlt, 4)
        z_drain_sum(zlft, 3)

    def drain_third():
        z_drain_sum(zlt, 5)
        z_drain_sum(zlt, 6)
        z_drain_sum(*z0[2:])
        for b in (1, 2):
            xy_drain(back[b], 9 + b)
            xy_done(back[b], 9 + b)

    def drain_tables(h):
        for j in range(4):
            xy_drain(GT.at[h, (t + 4 - j) % 4], 12 + 4 * h + j)
            xy_done(GT.at[h, (t + 4 - j) % 4], 12 + 4 * h + j)

    def drain_back():
        drain_tables(0)
        xy_drain(back[0], 9)
        xy_done(back[0], 9)

    def first_grads(i, _):
        down_grad(i)
        events(i, [], [], [(down_add, 0)], [(down_add, 1), (xy1_send, *b2_low)])
        return 0

    def second_grads(i, _):
        @pl.when(i < 4)
        def _():
            @pl.when(i == 3)
            def _():
                out_copy.wait()

            down_act(i)

        events(
            i,
            [(down_add, 2)],
            [(down_add, 3), (xy1_send, *b2_high), (drain_late,)],
            [],
            [(xy1_add, *b2_low), (up_add, 0)],
            [(up_add, 1), (xy1_send, *b1_low)],
        )

        @pl.when(i >= 1)
        def _():
            up_grad(i - 1)

        return 0

    def third_grads(i, _):
        up_act(i)
        events(
            i,
            [(xy1_add, *b2_high), (up_add, 2)],
            [(up_add, 3), (xy2_add, *b2_low)],
            [],
            [(xy1_send, *b1_high)],
        )
        return 0

    def fourth_grads(i, _):
        heads_back(i)
        events(
            i,
            [(xy1_add, *b1_low), (xy2_add, *b2_high), (z_send, *z2)],
            [(in_add, 0)],
            [(xy2_add, *b1_high), (zk_send, *z1, 2), (zk_send, *z1, 3), (zf_sum, *zf2), (xy1_send, *f2)],
        )

        @pl.when(i < 3)
        def _():
            in_grad(i)

        events(
            i,
            [],
            [
                (xy1_add, *b1_high),
                (xy2_add, *b1_low),
                (zk_send, *z1, 0),
                (zk_send, *z1, 1),
                (in_add, 1),
                (xy1_send, *b0_low),
            ],
        )
        return 0

    lax.fori_loop(0, 4, first_grads, 0)
    lax.fori_loop(0, 5, second_grads, 0)
    lax.fori_loop(0, 4, third_grads, 0)
    norm_back()
    lax.fori_loop(0, 4, fourth_grads, 0)
    hidden_copy = pltpu.make_async_copy(res, grad_hidden, loc.at[9])
    hidden_copy.start()
    xy1_add(*b0_low)
    xy1_add(*f2)
    in_add(2)
    table_grad(0)
    table_grad(1)
    table_add(0)
    in_grad(3)
    table_add(1)
    xy1_send(*table1)
    xy2_add(*b0_low)
    xy2_add(*f2)
    in_add(3)
    z_sum(*z2)
    xy1_add(*table1)
    xy1_send(*b0_q2)
    z_sum(*z1)
    xy2_add(*table1)
    z_send(*zt1)
    xy1_send(*b0_q3)
    ag_own(2)
    xy1_add(*b0_q2)
    zf_sum(*zft)
    xy1_send(*ft)
    z_sum(*zt1)
    table_out(1)
    ag_relay(2)
    drain_first()
    xy1_add(*ft)
    ag_own(1)
    xy1_add(*b0_q3)
    xy2_add(*b0_q2)
    xy2_add(*ft)
    table_out(0)
    for k in range(3):
        zk_send(*z0, k)
    ag_relay(1)
    xy2_add(*b0_q3)
    zk_send(*z0, 3)
    table_in(1, 1)
    table_relay(1, 0)
    table_in(1, 2)
    table_in(1, 3)
    table_in(0, 1)
    table_relay(0, 0)
    table_in(0, 2)
    table_in(0, 3)
    ag_finish(2)
    drain_second()
    table_relay(1, 1)
    table_relay(1, 2)
    table_relay(1, 3)
    ag_finish(1)
    table_relay(0, 1)
    table_relay(0, 2)
    table_relay(0, 3)
    table_finish(1, 0)
    table_finish(1, 1)
    z_sum(*z0)
    ag_own(0)
    table_finish(1, 2)
    table_finish(1, 3)
    table_finish(0, 0)
    table_finish(0, 1)
    table_finish(0, 2)
    table_finish(0, 3)
    ag_relay(0)
    drain_third()
    drain_tables(1)
    ag_finish(0)

    drain_back()


def finish(
    G,
    GT,
    made_out,
    made_hidden,
    layer_out,
    grad_hidden,
    table_x,
    table_y,
    in_w,
    out_w,
    up_w,
    down_w,
    in_b,
    out_b,
    up_b,
    down_b,
    gain,
    nbias,
    wide_w,
    wide_t,
    full_w,
    full_t,
    held_out,
    held_hidden,
    sem_in,
    sem_out,
):
    t = lax.axis_index("tensor")
    places = [in_w.at[0], in_w.at[1], in_w.at[2], out_w]
    places += [ref.at[pl.ds(192 * i, 192)] for ref in (up_w, down_w) for i in range(4)]
    tables = [ref.at[pl.ds(256 * i, 256)] for ref in (table_x, table_y) for i in range(4)]
    ins = [pltpu.make_async_copy(GT.at[i], wide_t.at[i], sem_in.at[12 + i]) for i in range(8)]
    ins = [pltpu.make_async_copy(G.at[i], wide_w.at[i], sem_in.at[i]) for i in range(12)] + ins
    outs = [pltpu.make_async_copy(full_w.at[i], places[i], sem_out.at[i]) for i in range(12)]
    outs += [pltpu.make_async_copy(full_t.at[i], tables[i], sem_out.at[12 + i]) for i in range(8)]
    ins += [
        pltpu.make_async_copy(made_hidden, held_hidden, sem_in.at[20]),
        pltpu.make_async_copy(made_out, held_out, sem_in.at[21]),
    ]
    outs += [
        pltpu.make_async_copy(held_hidden, grad_hidden, sem_out.at[20]),
        pltpu.make_async_copy(held_out, layer_out, sem_out.at[21]),
    ]
    for copy in ins:
        copy.start()
    for i in range(12):
        ins[i].wait()
        full_w[i] = wide_w[i].astype(f32)
        outs[i].start()
    for i in range(8):
        ins[12 + i].wait()
        full_t[i] = wide_t[i].astype(f32)
        if i == 3:
            small = wide_t[3, 240:256].astype(f32)
            full_t[3, 240:256, :] = jnp.zeros((16, 768), f32)
            gain[...] = small[2:4]
            nbias[...] = small[4:6]
            out_b[...] = small[0]
            down_b[...] = small[1]
            level = lax.broadcasted_iota(jnp.int32, (16, 1), 0)
            up_b[...] = jnp.sum(jnp.where(level == 6 + t, small, 0.0), axis=0)
            row = jnp.sum(jnp.where(level == 10 + t, small, 0.0), axis=0, keepdims=True)
            in_b[0:1, :] = row[:, 0:192]
            in_b[1:2, :] = row[:, 384:576]
        outs[12 + i].start()
    for i in (20, 21):
        ins[i].wait()
        outs[i].start()
    for copy in outs:
        copy.wait()


def on_device(
    dp,
    hidden,
    page_boxes,
    lengths,
    table_x,
    table_y,
    in_weight,
    in_bias,
    out_weight,
    out_bias,
    up_weight,
    up_bias,
    down_weight,
    down_bias,
    norm_gain,
    norm_bias,
    cotangent,
):
    blocks = (2, 2, 2, 2)
    vmem = pl.BlockSpec(memory_space=pltpu.VMEM)
    anywhere = pl.BlockSpec(memory_space=pl.ANY)
    dma = pltpu.SemaphoreType.DMA
    count = max(1, (dp // 8).bit_length() - 1)
    V = pltpu.VMEM

    def lands(quarters, rows):
        first, second = V((quarters, 2, rows, 768), bf16), V((quarters, rows, 768), bf16)
        return [first, first, second, second]

    scratch = [
        V((3, 4, *blocks, R, 768), bf16),
        V((4, *blocks, R, 768), bf16),
        V((2048, 768), bf16),
        V((8, *blocks, RT, 768), bf16),
        V((4, 512, 768), bf16),
        V((4, 512, 576), bf16),
        V((4, 512, 192), bf16),
        V((4, 8, 512), f32),
        V((512, 768), bf16),
        V((512, 768), bf16),
        V((512, 768), bf16),
        V((512, 768), bf16),
        V((512, 768), f32),
        V((512, 768), f32),
        V((512, 768), f32),
        V((512, 1), f32),
        V((4, 8, 768), f32),
        V((16, 768), f32),
        V((6, 2, 2, 2, R, 768), bf16),
        V((2, 4, 2, 2, 2, RT, 768), bf16),
        lands(4, R),
        lands(4, R),
        lands(4, XR),
        lands(4, RT),
        lands(1, FR),
        lands(1, RT),
        V((3, 2, R, 768), bf16),
        V((3, 2, R, 768), bf16),
        V((3, 2, XR, 768), bf16),
        V((3, 2, RT, 768), bf16),
        V((3, 2, 2, 2, FR, 768), bf16),
        V((3, 2, 2, 2, RT, 768), bf16),
        V((count, 2, R, 768) if dp > 8 else (8, 128), bf16),
        V((count, 2, RT, 768) if dp > 8 else (8, 128), bf16),
        dma((15,)),
        dma((3,)),
        dma((3,)),
        dma((3, 5, 2)),
        dma((3, 4, 2)),
        dma((2, 5)),
        dma((2, 4)),
        dma((20, 6)),
        dma((20, 6)),
        dma((20,)),
        dma((20,)),
        dma((14,)),
        dma((14,)),
        pltpu.SemaphoreType.REGULAR,
        dma((10, 4)),
        dma((10, 4)),
        dma((8, 3)),
        dma((8, 3)),
        dma((5, count)),
        dma((5, count)),
    ]
    shape = jax.ShapeDtypeStruct
    made_out, made_hidden, G, GT = pl.pallas_call(
        partial(kernel, dp),
        out_shape=(
            shape((512, 768), bf16),
            shape((512, 768), f32),
            shape((3, *blocks, R, 768), bf16),
            shape((2, 4, *blocks, RT, 768), bf16),
        ),
        in_specs=[
            anywhere,
            vmem,
            pl.BlockSpec(memory_space=pltpu.SMEM),
            anywhere,
            anywhere,
            anywhere,
            vmem,
            anywhere,
            vmem,
            anywhere,
            vmem,
            anywhere,
            vmem,
            vmem,
            vmem,
            anywhere,
        ],
        out_specs=(anywhere,) * 4,
        scratch_shapes=scratch,
        compiler_params=pltpu.CompilerParams(
            collective_id=0, has_side_effects=True, vmem_limit_bytes=61 * 2**20
        ),
    )(
        hidden,
        page_boxes.T,
        lengths,
        table_x,
        table_y,
        in_weight.transpose(0, 2, 1).reshape(3, 2, 2, R, 768),
        in_bias,
        out_weight.reshape(2, 2, R, 768),
        out_bias,
        up_weight.reshape(*blocks, R, 768),
        up_bias,
        down_weight.reshape(*blocks, R, 768),
        down_bias,
        norm_gain,
        norm_bias,
        cotangent,
    )
    outs = pl.pallas_call(
        finish,
        out_shape=(
            shape((512, 768), bf16),
            shape((512, 768), f32),
            shape((1024, 768), f32),
            shape((1024, 768), f32),
            shape((3, 192, 768), f32),
            shape((192, 768), f32),
            shape((768, 768), f32),
            shape((768, 768), f32),
            shape((2, 192), f32),
            shape((768,), f32),
            shape((768,), f32),
            shape((768,), f32),
            shape((2, 768), f32),
            shape((2, 768), f32),
        ),
        in_specs=[pl.BlockSpec(memory_space=pltpu.HBM)] * 4,
        out_specs=(anywhere,) * 8 + (vmem,) * 6,
        scratch_shapes=[
            V((12, 192, 768), bf16),
            V((8, 256, 768), bf16),
            V((12, 192, 768), f32),
            V((8, 256, 768), f32),
            V((512, 768), bf16),
            V((512, 768), f32),
            dma((22,)),
            dma((22,)),
        ],
        compiler_params=pltpu.CompilerParams(vmem_limit_bytes=62 * 2**20),
    )(G.reshape(12, 192, 768), GT.reshape(8, 256, 768), made_out, made_hidden)
    out, hidden_grad, tx, ty, in_w, out_w, up_w, down_w, in_b, out_b, up_b, down_b, gains, biases = outs
    in_w = in_w.transpose(0, 2, 1)
    return out, hidden_grad, tx, ty, in_w, in_b, out_w, out_b, up_w, up_b, down_w, down_b, gains, biases


def solution(mesh):
    both = ("dp", "tensor")
    in_specs = (
        P(both, None),
        P(both, None),
        P("dp"),
        P(),
        P(),
        P(None, None, "tensor"),
        P(None, "tensor"),
        P("tensor", None),
        P(),
        P(None, "tensor"),
        P("tensor"),
        P("tensor", None),
        P(),
        P(),
        P(),
        P(both, None),
    )
    out_specs = (
        P(both, None),
        P(both, None),
        P(),
        P(),
        P(None, None, "tensor"),
        P(None, "tensor"),
        P("tensor", None),
        P(),
        P(None, "tensor"),
        P("tensor"),
        P("tensor", None),
        P(),
        P(),
        P(),
    )
    return jax.shard_map(
        partial(on_device, mesh.shape["dp"]),
        mesh=mesh,
        in_specs=in_specs,
        out_specs=out_specs,
        check_vma=False,
    )
```

```python
from functools import partial

import jax
import jax.numpy as jnp
from jax import lax
from jax.experimental import pallas as pl
from jax.experimental.pallas import tpu as pltpu
from jax.sharding import PartitionSpec as P

HEAD = 64
EPS = 1e-12
MESH = pl.DeviceIdType.MESH
f32 = jnp.float32
bf16 = jnp.bfloat16

R = 48
RT = 16
FR = 16
XR = R - FR
ZR = 16


def dot(a, b, ca, cb):
    return lax.dot_general(a, b, (((ca,), (cb,)), ((), ())), preferred_element_type=f32)


def kernel(
    dp,
    hidden,
    boxes,
    lengths,
    tables_x,
    tables_y,
    in_w,
    in_b,
    out_w,
    out_b,
    up_w,
    up_b,
    down_w,
    down_b,
    gain,
    nbias,
    cotangent,
    layer_out,
    grad_hidden,
    G,
    GT,
    W,
    G2,
    pre,
    act,
    gp,
    qkv,
    ctx,
    lse,
    resb,
    midb,
    bgrad,
    hid,
    res,
    total,
    n1,
    r1,
    bias,
    vec,
    core_land,
    core_land_t,
    lands0,
    lands1,
    lands2,
    lands_t,
    lands_f,
    lands_ft,
    zl0,
    zl1,
    zl2,
    zlt,
    zlf,
    zlft,
    extra,
    extra_t,
    loc,
    bs,
    br,
    gzs,
    gzr,
    gds,
    gdr,
    xs,
    xr,
    cs,
    cr,
    ks,
    kr,
    credit,
    rs,
    rr,
    zs,
    zr,
    es,
    er,
):
    d = lax.axis_index("dp")
    t = lax.axis_index("tensor")
    c = d % 2
    x = (d // 2) % 2
    y = (d // 4) % 2
    X = (d + 2 - 4 * x, t)
    Y = (d + 4 - 8 * y, t)
    C = (d + 1 - 2 * c, t)
    extras = []
    step = 8
    while step < dp:
        extras.append((d + step - 2 * step * ((d // step) % 2), t))
        step *= 2

    def remote(src, dst, send, recv, dev):
        return pltpu.make_async_remote_copy(
            src_ref=src, dst_ref=dst, send_sem=send, recv_sem=recv, device_id=dev, device_id_type=MESH
        )

    def wait_recv(ref, sem):
        remote(ref, ref, sem, sem, C).wait_recv()

    def wait_send(ref, sem):
        remote(ref, ref, sem, sem, C).wait_send()

    barrier = pltpu.get_barrier_semaphore()
    zpeers = [(d, (t + j) % 4) for j in range(1, 4)]
    peers = [X, Y, C] + zpeers + extras
    for peer in peers:
        pl.semaphore_signal(barrier, inc=1, device_id=peer, device_id_type=MESH)

    local = [
        pltpu.make_async_copy(in_w.at[pl.ds(0, 2)], W.at[0, t, 0], loc.at[0]),
        pltpu.make_async_copy(tables_x, pre.at[pl.ds(0, 1024)], loc.at[1]),
        pltpu.make_async_copy(tables_y, pre.at[pl.ds(1024, 1024)], loc.at[2]),
        pltpu.make_async_copy(hidden, hid, loc.at[3]),
        pltpu.make_async_copy(out_w, W.at[0, t, 1, 1], loc.at[4]),
        pltpu.make_async_copy(up_w, W.at[1, t], loc.at[5]),
        pltpu.make_async_copy(down_w, W.at[2, t], loc.at[6]),
        pltpu.make_async_copy(in_w.at[2], W.at[0, t, 1, 0], loc.at[7]),
    ]
    for i in (0, 7, 4, 1, 2, 3, 5, 6):
        local[i].start()
    bias[t] = jnp.zeros((8, 768), f32)
    bias[t, 0:1, :] = up_b[...].reshape(1, 768)
    bias[t, 1:2, 0:192] = in_b[0:1, :]
    bias[t, 1:2, 384:576] = in_b[1:2, :]
    def entry_local():
        local[0].wait()
        local[4].wait()
        local[7].wait()

    def entry_barrier():
        pl.semaphore_wait(barrier, len(peers))

    entry_barrier()
    entry_local()

    half = t // 2
    near = t * (1 - half) + (3 - t) * half

    def other(j):
        base = j + 1 - near * ((3 - j) // 3)
        return base * (1 - half) + (3 - base) * half

    def z_own(src, dst, ss, rsem):
        @pl.when(t > 0)
        def _():
            remote(src, dst, ss(0), rsem, (d, t - 1)).start()

        @pl.when(t < 3)
        def _():
            remote(src, dst, ss(1), rsem, (d, t + 1)).start()

    def z_arrive(ref, tp, send, recv):
        wait_recv(ref, recv)

        @pl.when(jnp.logical_and(tp < t, t < 3))
        def _():
            remote(ref, ref, send, recv, (d, t + 1)).start()

        @pl.when(jnp.logical_and(tp > t, t > 0))
        def _():
            remote(ref, ref, send, recv, (d, t - 1)).start()

    def z_drain(ref, ss):
        @pl.when(t > 0)
        def _():
            wait_send(ref, ss(0))

        @pl.when(t < 3)
        def _():
            wait_send(ref, ss(1))

    def z_arrive_drain(ref, tp, send):
        @pl.when(jnp.logical_or(jnp.logical_and(tp < t, t < 3), jnp.logical_and(tp > t, t > 0)))
        def _():
            wait_send(ref, send)

    def xy_own(src, dst, i):
        a, b = src.at[0], src.at[1]
        da, db = dst.at[c, y, x, 0], dst.at[c, y, x, 1]
        remote(a, da, xs.at[i, 0], xr.at[i, 0], X).start()
        remote(b, db, xs.at[i, 1], xr.at[i, 2], Y).start()
        remote(a, da, xs.at[i, 0], xr.at[i, 1], Y).start()
        remote(b, db, xs.at[i, 1], xr.at[i, 3], X).start()

    def xy_relay(ref, i, ra=slice(None), rb=slice(None)):
        a, b = ref.at[c, y, 1 - x, 0, ra], ref.at[c, 1 - y, x, 1, rb]
        wait_recv(a, xr.at[i, 0])
        remote(a, a, xs.at[i, 0], xr.at[i, 4], Y).start()
        wait_recv(b, xr.at[i, 2])
        remote(b, b, xs.at[i, 1], xr.at[i, 5], X).start()

    def xy_finish(ref, i, ra=slice(None), rb=slice(None)):
        wait_recv(ref.at[c, 1 - y, x, 0, ra], xr.at[i, 1])
        wait_recv(ref.at[c, y, 1 - x, 1, rb], xr.at[i, 3])
        wait_recv(ref.at[c, 1 - y, 1 - x, 0, ra], xr.at[i, 4])
        wait_recv(ref.at[c, 1 - y, 1 - x, 1, rb], xr.at[i, 5])
        remote(ref.at[c], ref.at[c], cs.at[i], cr.at[i], C).start()

    def xy_done(ref, i):
        wait_recv(ref.at[1 - c], cr.at[i])

    def xy_drain(ref, i, rows_a, rows_b):
        for h, count in enumerate((rows_a, rows_b)):
            wait_send(pre.at[pl.ds(0, 3 * count)], xs.at[i, h])
        wait_send(ref.at[c], cs.at[i])

    def rows_of(b, h):
        return pl.ds(0, R - ZR) if b + h == 2 else pl.ds(0, R)

    def both(b):
        return rows_of(b, 0), rows_of(b, 1)

    def whole(b, tp):
        return W.at[b, tp, c, :, :, 2 - b, pl.ds(R - ZR, ZR)]

    def whole_own(b):
        z_own(whole(b, t), whole(b, t), lambda k: gds.at[b - 1, k], gdr.at[b - 1, t])

    def whole_in(i):
        b, j = i // 3, i % 3
        z_arrive(whole(b, other(j)), other(j), gds.at[b - 1, 2 + j], gdr.at[b - 1, other(j)])

    def gz_own(b):
        for h in range(2):
            ref = W.at[b, t, c, y, x, h, rows_of(b, h)]
            z_own(ref, ref, lambda k: gzs.at[b, k, h], gzr.at[b, t, h])

    def gz_end(b):
        @pl.when(jnp.logical_or(t == 0, t == 3))
        def _():
            gz_own(b)

    def gz_middle(b):
        @pl.when(jnp.logical_and(t > 0, t < 3))
        def _():
            gz_own(b)

    def e1(i):
        b, j = i // 3, i % 3
        tp = other(j)
        for h in range(2):
            ref = W.at[b, tp, c, y, x, h, rows_of(b, h)]
            z_arrive(ref, tp, gzs.at[b, 2 + j, h], gzr.at[b, tp, h])
            for dev, k in ((X, 0), (Y, 1)) if h == 0 else ((Y, 2), (X, 3)):
                remote(ref, ref, xs.at[i, h], xr.at[i, k], dev).start()

    def e2(i):
        xy_relay(W.at[i // 3, other(i % 3)], i, *both(i // 3))

    def e3(i):
        xy_finish(W.at[i // 3, other(i % 3)], i, *both(i // 3))

    def e4(i):
        xy_done(W.at[i // 3, other(i % 3)], i)

    gz_own(0)
    for j in range(3):
        remote(bias.at[t], bias.at[t], bs.at[j], br.at[2 - j], zpeers[j]).start()

    def one_hot(first, second, levels):
        return ((first == levels).astype(f32) + (second == levels).astype(f32)).astype(bf16)

    levels = lax.broadcasted_iota(jnp.int32, (1024, 1), 0)

    def embed():
        for i in (1, 2, 3):
            local[i].wait()
        horizontal = one_hot(boxes[0:1], boxes[2:3], levels)
        vertical = one_hot(boxes[1:2], boxes[3:4], levels)
        residual = (
            hid[...].astype(f32)
            + dot(horizontal, pre[0:1024, :], 0, 0)
            + dot(vertical, pre[1024:2048, :], 0, 0)
        )
        res[...] = residual
        resb[...] = residual.astype(bf16)
        total[...] = jnp.zeros_like(total)

    embed()
    local[5].wait()
    local[6].wait()
    cot_copy = pltpu.make_async_copy(cotangent, hid, loc.at[3])
    cot_copy.start()

    def biases():
        for j in range(3):
            tz = (t + 3 - j) % 4
            wait_recv(bias.at[tz], br.at[2 - j])

    length = lengths[t]
    visible = lax.broadcasted_iota(jnp.int32, (512, 1), 0) < length
    scaling = HEAD**-0.5

    def project(tp):
        weight = W[0, tp].reshape(768, 768)
        qkv[tp] = (dot(resb[...], weight[0:576], 1, 1) + bias[tp, 1:2, 0:576]).astype(bf16)

    def heads(tp):
        for j in range(3):
            q = qkv[tp, :, j * 64 : (j + 1) * 64]
            k = qkv[tp, :, 192 + j * 64 : 192 + (j + 1) * 64]
            v = qkv[tp, :, 384 + j * 64 : 384 + (j + 1) * 64]
            scores = jnp.where(visible, dot(k, q, 1, 1) * scaling, -1e30)
            top = jnp.max(scores, axis=0, keepdims=True)
            exponent = jnp.exp(scores - top)
            sums = jnp.sum(exponent, axis=0, keepdims=True)
            attend = (exponent * (1.0 / sums)).astype(bf16)
            ctx[tp, :, j * 64 : (j + 1) * 64] = dot(attend, v, 0, 0).astype(bf16)
            lse[tp, j : j + 1, :] = top + jnp.log(sums)
        total[...] += dot(ctx[tp], W[0, tp, 1, 1].reshape(192, 768), 1, 0)

    def up(tp):
        hidden_pre = dot(midb[...], W[1, tp].reshape(768, 768), 1, 0) + bias[tp, 0:1, :]
        cdf = 0.5 * (1.0 + lax.erf(hidden_pre * 0.7071067811865476))
        act[pl.ds(2 * tp, 2)] = (hidden_pre * cdf).astype(bf16).reshape(2, 2, 2, 2, 2, RT, 768)
        slope = cdf + hidden_pre * jnp.exp(-0.5 * hidden_pre * hidden_pre) * 0.3989422804014327
        gp[tp] = slope.astype(bf16)

    def down(tp):
        total[...] += dot(act[pl.ds(2 * tp, 2)].reshape(512, 768), W[2, tp].reshape(768, 768), 1, 0)

    def normalize(value):
        average = jnp.mean(value, axis=-1, keepdims=True)
        centered = value - average
        inverse = lax.rsqrt(jnp.mean(centered * centered, axis=-1, keepdims=True) + EPS)
        return centered * inverse, inverse

    def normalize_back(gradient, normed, inverse, gain_row):
        scaled = gradient * gain_row
        inner = (
            scaled
            - jnp.mean(scaled, axis=-1, keepdims=True)
            - normed * jnp.mean(scaled * normed, axis=-1, keepdims=True)
        )
        return inverse * inner

    def row_sum(value):
        return jnp.sum(value, axis=0, keepdims=True)

    def out_norm():
        normed, inverse = normalize(res[...] + total[...] + out_b[...].reshape(1, 768))
        n1[...] = normed
        r1[...] = inverse
        middle = normed * gain[0:1] + nbias[0:1]
        res[...] = middle
        midb[...] = middle.astype(bf16)
        total[...] = jnp.zeros_like(total)

    def drain_items(b):
        def one(j, _):
            xy_drain(W.at[0, 0], 3 * b + j, *(r.size for r in both(b)))
            return 0

        lax.fori_loop(0, 3, one, 0)

    def drain_z(b):
        for h in range(2):
            ref = W.at[0, 0, 0, 0, 0, 0, rows_of(b, h)]
            z_drain(ref, lambda k: gzs.at[b, k, h])
            for j in range(3):
                z_arrive_drain(ref, other(j), gzs.at[b, 2 + j, h])

    def drain_whole(b):
        z_drain(whole(b, 0), lambda k: gds.at[b - 1, k])
        for j in range(3):
            z_arrive_drain(whole(b, 0), other(j), gds.at[b - 1, 2 + j])

    def events(k, *turns):
        for turn, calls in enumerate(turns):
            if calls:

                @pl.when(k == turn)
                def _(calls=calls):
                    for call, *given in calls:
                        call(*given)

    def quarter(k):
        own = (3 - k) // 3
        return own * t + (1 - own) * other(k - 1)

    e1(0)
    e1(1)
    gz_end(1)
    e2(0)
    e1(2)
    gz_middle(1)
    e2(1)
    biases()

    def attend(k, _):
        tp = quarter(k)
        project(tp)
        events(
            k,
            [(e2, 2)],
            [(e1, 4), (whole_own, 1), (gz_end, 2), (e3, 1)],
            [(e3, 2)],
            [(e1, 7), (e2, 5), (whole_in, 3)],
        )
        heads(tp)
        events(
            k,
            [(e3, 0), (e1, 3), (e4, 0)],
            [(e1, 5), (gz_middle, 2), (e2, 3), (e4, 1)],
            [(e2, 4), (e1, 6), (e4, 2)],
            [(e1, 8), (whole_own, 2), (e3, 3)],
        )
        return 0

    def widen(k, _):
        up(quarter(k))
        events(
            k,
            [(e4, 3), (whole_in, 4), (e3, 4)],
            [(e2, 7), (whole_in, 5), (e3, 5), (e4, 4), (whole_in, 6)],
            [(e2, 8), (whole_in, 7), (e3, 6), (e4, 5)],
        )
        return 0

    def drain_early():
        drain_items(0)
        drain_items(1)
        for b in range(3):
            drain_z(b)
        drain_whole(1)

    def drain_late():
        drain_items(2)
        drain_whole(2)

    def narrow(k, _):
        down(quarter(k))
        events(k, [(e3, 7), (whole_in, 8), (drain_early,), (e4, 6)], [(e3, 8), (e4, 7)], [(e4, 8)])
        return 0

    lax.fori_loop(0, 4, attend, 0)
    out_norm()
    e2(6)
    lax.fori_loop(0, 4, widen, 0)
    lax.fori_loop(0, 4, narrow, 0)

    normed, inverse = normalize(res[...] + total[...] + down_b[...].reshape(1, 768))
    pre[1536:2048, :] = (normed * gain[1:2] + nbias[1:2]).astype(bf16)
    out_copy = pltpu.make_async_copy(pre.at[pl.ds(1536, 512)], layer_out, loc.at[8])
    out_copy.start()
    cot_copy.wait()
    gradient = hid[...].astype(f32)
    final_grad = normalize_back(gradient, normed, inverse, gain[1:2])
    res[...] = final_grad
    bgrad[...] = final_grad.astype(bf16)
    vec[...] = jnp.zeros_like(vec)
    vec[1:2, :] = row_sum(bgrad[...].astype(f32))
    vec[3:4, :] = row_sum(gradient * normed)
    vec[5:6, :] = row_sum(gradient)

    def core_send(ref, n, tp):
        remote(ref.at[tp, 1 - c], core_land.at[n % 6], ks.at[n], kr.at[n], C).start()

    def core_add(ref, n, tp):
        wait_recv(core_land.at[n % 6], kr.at[n])
        ref[tp, c] = ref[tp, c] + core_land[n % 6]

    def free():
        pl.semaphore_signal(credit, inc=1, device_id=C, device_id_type=MESH)

    def wait_free():
        pl.semaphore_wait(credit, 1)

    def xy1_send(ref, part, rows, lands, lp, g):
        a = ref.at[part, c, :, 1 - x, 0, rows]
        b = ref.at[part, c, 1 - y, :, 1, rows]
        remote(a, lands[0].at[lp], rs.at[g, 0], rr.at[g, 0], X).start()
        remote(b, lands[1].at[lp], rs.at[g, 1], rr.at[g, 1], Y).start()

    def xy1_add(ref, part, rows, lands, lp, g):
        wait_recv(lands[0].at[lp], rr.at[g, 0])
        ref[part, c, :, x, 0, rows] = ref[part, c, :, x, 0, rows] + lands[0][lp]
        remote(ref.at[part, c, 1 - y, x, 0, rows], lands[3].at[lp], rs.at[g, 3], rr.at[g, 3], Y).start()
        wait_recv(lands[1].at[lp], rr.at[g, 1])
        ref[part, c, y, :, 1, rows] = ref[part, c, y, :, 1, rows] + lands[1][lp]
        remote(ref.at[part, c, y, 1 - x, 1, rows], lands[2].at[lp], rs.at[g, 2], rr.at[g, 2], X).start()

    def xy2_add(ref, part, rows, lands, lp, g):
        wait_recv(lands[3].at[lp], rr.at[g, 3])
        ref[part, c, y, x, 0, rows] = ref[part, c, y, x, 0, rows] + lands[3][lp]
        wait_recv(lands[2].at[lp], rr.at[g, 2])
        ref[part, c, y, x, 1, rows] = ref[part, c, y, x, 1, rows] + lands[2][lp]

    def xy_rs_drain(lands, lp, g):
        for k in range(4):
            wait_send(lands[k].at[lp], rs.at[g, k])

    def z_send(ref, rows, land, g):
        for j in range(1, 4):
            k = (t + j) % 4
            remote(ref.at[k, c, y, x, :, rows], land.at[j - 1], zs.at[g, j - 1], zr.at[g, j - 1], (d, k)).start()

    def zk_send(ref, rows, land, g, k):
        @pl.when(t != k)
        def _():
            slot = (k - t + 3) % 4
            remote(ref.at[k, c, y, x, :, rows], land.at[slot], zs.at[g, slot], zr.at[g, slot], (d, k)).start()

    def z_sum(ref, rows, land, g):
        for j in range(3):
            wait_recv(land.at[j], zr.at[g, j])
        value = ref[t, c, y, x, :, rows].astype(f32)
        for j in range(3):
            value = value + land[j].astype(f32)
        ref[t, c, y, x, :, rows] = value.astype(bf16)

    def z_drain_sum(land, g):
        for j in range(3):
            wait_send(land.at[j], zs.at[g, j])

    def zf_send(ref, rows, land, g, k):
        @pl.when(t != k)
        def _():
            slot = (k - t + 3) % 4
            remote(ref.at[k, c, :, :, :, rows], land.at[slot], zs.at[g, slot], zr.at[g, slot], (d, k)).start()

    def zf_sum(ref, rows, land, g):
        for j in range(3):
            wait_recv(land.at[j], zr.at[g, j])
        value = ref[t, c, :, :, :, rows].astype(f32)
        for j in range(3):
            value = value + land[j].astype(f32)
        ref[t, c, :, :, :, rows] = value.astype(bf16)

    def across(ref, land, g):
        for i, peer in enumerate(extras):
            copy = remote(ref, land.at[i], es.at[g, i], er.at[g, i], peer)
            copy.start()
            copy.wait()
            ref[...] = ref[...] + land[i]

    g1 = W.at[2]
    g0 = W.at[1]
    low, high, every = pl.ds(0, 2), pl.ds(2, 2), pl.ds(0, 4)
    rows_x, rows_f, rows, rows_t = pl.ds(0, XR), pl.ds(XR, FR), pl.ds(0, R), pl.ds(0, RT)
    tables = [act.at[pl.ds(0, 4)], act.at[pl.ds(4, 4)]]
    b2_low, b2_high = (G2, low, rows_x, lands2, low, 0), (G2, high, rows_x, lands2, high, 1)
    b1_low, b1_high = (g1, low, rows, lands1, low, 2), (g1, high, rows, lands1, high, 3)
    b0_low = (g0, low, rows, lands0, low, 4)
    b0_q2, b0_q3 = (g0, pl.ds(2, 1), rows, lands0, pl.ds(2, 1), 5), (g0, pl.ds(3, 1), rows, lands0, pl.ds(3, 1), 6)
    table1 = (tables[1], every, rows_t, lands_t, every, 8)
    f2, ft = (G2, t, rows_f, lands_f, 0, 9), (tables[0], t, rows_t, lands_ft, 0, 7)
    z0, z1, z2 = (g0, rows, zl0, 0), (g1, rows, zl1, 1), (G2, rows_x, zl2, 2)
    zt1 = (tables[1], rows_t, zlt, 4)
    zf2, zft = (G2, rows_f, zlf, 7), (tables[0], rows_t, zlft, 3)

    def span(i):
        return pl.ds(pl.multiple_of(i * 512, 512), 512)

    def down_grad(i):
        activated = act[pl.ds(2 * i, 2)].reshape(512, 768)
        G2[i] = dot(activated, bgrad[...], 0, 0).astype(bf16).reshape(2, 2, 2, 2, R, 768)
        core_send(G2, i, i)

    def down_act(i):
        grad = dot(bgrad[...], W[2, i].reshape(768, 768), 1, 1).astype(bf16)
        pre_grad = (grad.astype(f32) * gp[i].astype(f32)).astype(bf16)
        pre[span(i), :] = pre_grad
        vec[pl.ds(6 + i, 1), :] = row_sum(pre_grad.astype(f32))

    def down_add(i):
        core_add(G2, i, i)
        free()
        zf_send(*zf2, i)

    def up_grad(i):
        g1[i] = dot(midb[...], pre[span(i), :], 0, 0).astype(bf16).reshape(2, 2, 2, 2, R, 768)

        @pl.when(i >= 2)
        def _():
            wait_free()

        core_send(g1, 4 + i, i)

    def up_act(i):
        res[...] += dot(pre[span(i), :], W[1, i].reshape(768, 768), 1, 1)

    def up_add(i):
        core_add(g1, 4 + i, i)
        if i < 2:
            free()

    def norm_back():
        normed = n1[...]
        gradient = res[...]
        residual_grad = normalize_back(gradient, normed, r1[...], gain[0:1])
        res[...] = residual_grad
        bgrad[...] = residual_grad.astype(bf16)
        vec[0:1, :] = row_sum(bgrad[...].astype(f32))
        vec[2:3, :] = row_sum(gradient * normed)
        vec[4:5, :] = row_sum(gradient)

    def heads_back(i):
        context_grad = dot(bgrad[...], W[0, i, 1, 1].reshape(192, 768), 1, 1).astype(bf16)
        for j in range(3):
            q = qkv[i, :, j * 64 : (j + 1) * 64]
            k = qkv[i, :, 192 + j * 64 : 192 + (j + 1) * 64]
            v = qkv[i, :, 384 + j * 64 : 384 + (j + 1) * 64]
            dc = context_grad[:, j * 64 : (j + 1) * 64]
            scores = jnp.where(visible, dot(k, q, 1, 1) * scaling, -1e30)
            attend = jnp.exp(scores - lse[i, j : j + 1, :])
            prob_grad = dot(v, dc, 1, 1)
            inner = jnp.sum(prob_grad * attend, axis=0, keepdims=True)
            score_grad = (attend * (prob_grad - inner)).astype(bf16)
            value_grad = dot(attend.astype(bf16), dc, 1, 0)
            key_grad = dot(score_grad, q, 1, 0) * scaling
            query_grad = dot(score_grad, k, 0, 0) * scaling
            qkv[i, :, j * 64 : (j + 1) * 64] = query_grad.astype(bf16)
            qkv[i, :, 192 + j * 64 : 192 + (j + 1) * 64] = key_grad.astype(bf16)
            qkv[i, :, 384 + j * 64 : 384 + (j + 1) * 64] = value_grad.astype(bf16)
        grads = qkv[i]
        res[...] += dot(grads, W[0, i].reshape(768, 768)[0:576], 1, 0)
        vec[pl.ds(10 + i, 1), 0:576] = row_sum(grads.astype(f32))

    def in_grad(i):
        made = dot(qkv[i], resb[...], 0, 0).astype(bf16)
        g0[i, 0] = made[0:384].reshape(2, 2, 2, R, 768)
        g0[i, 1, 0] = made[384:576].reshape(2, 2, R, 768)
        g0[i, 1, 1] = dot(ctx[i], bgrad[...], 0, 0).astype(bf16).reshape(2, 2, R, 768)
        wait_free()
        core_send(g0, 8 + i, i)

    def in_add(i):
        core_add(g0, 8 + i, i)

    def table_grad(h):
        if h == 0:
            hid[...] = res[...].astype(bf16)
        hot = one_hot(boxes[h : h + 1], boxes[h + 2 : h + 3], levels)
        made = dot(hot, hid[...], 1, 0).astype(bf16)
        act[4 * h : 4 * h + 4] = made.reshape(4, 2, 2, 2, 2, RT, 768)
        if h == 0:
            act[3, 1, 1, 1, 1] = vec[...].astype(bf16)
        remote(tables[h].at[:, 1 - c], core_land_t.at[h], ks.at[12 + h], kr.at[12 + h], C).start()

    def table_add(h):
        wait_recv(core_land_t.at[h], kr.at[12 + h])
        tables[h][:, c] = tables[h][:, c] + core_land_t[h]
        if h == 0:
            for k in range(4):
                zf_send(*zft, k)

    F = [g0.at[t, c, y, x], g1.at[t, c, y, x], G2.at[t, c, y, x]]
    F += [ref.at[t, c, y, x] for ref in tables]
    back = [G.at[0], G.at[1], G.at[2], GT.at[0, t], GT.at[1, t]]
    item = [9, 10, 11, 12, 16]
    kept = [pltpu.make_async_copy(F[b], back[b].at[c, y, x], loc.at[10 + b]) for b in range(5)]

    def ag_own(b):
        across(F[b], extra_t if b >= 3 else extra, b)
        kept[b].start()
        xy_own(F[b], back[b], item[b])

    def ag_relay(b):
        xy_relay(back[b], item[b])

    def ag_finish(b):
        kept[b].wait()
        xy_finish(back[b], item[b])

    def table_out(h):
        ag_own(3 + h)
        for j in range(1, 4):
            send, recv = zs.at[5 + h, j - 1], zr.at[5 + h, j - 1]
            remote(F[3 + h], GT.at[h, t, c, y, x], send, recv, (d, (t + j) % 4)).start()

    def table_in(h, j):
        ref = GT.at[h, (t + 4 - j) % 4]
        wait_recv(ref.at[c, y, x], zr.at[5 + h, j - 1])
        xy_own(ref.at[c, y, x], ref, 12 + 4 * h + j)

    def table_relay(h, j):
        xy_relay(GT.at[h, (t + 4 - j) % 4], 12 + 4 * h + j)

    def table_finish(h, j):
        if j == 0:
            kept[3 + h].wait()
        xy_finish(GT.at[h, (t + 4 - j) % 4], 12 + 4 * h + j)

    def drain_first():
        for j in range(3):
            wait_send(bias.at[0], bs.at[j])
        for n in range(12):
            wait_send(core_land.at[0], ks.at[n])
        for h in range(2):
            wait_send(core_land_t.at[h], ks.at[12 + h])
        for group in (b2_low, b2_high, b1_low, b1_high, b0_low, f2, table1):
            xy_rs_drain(*group[3:])
        for group in (z1, z2):
            z_drain_sum(*group[2:])
        z_drain_sum(zlf, 7)

    def drain_second():
        hidden_copy.wait()
        for group in (b0_q2, b0_q3, ft):
            xy_rs_drain(*group[3:])
        z_drain_sum(zlt, 4)
        z_drain_sum(zlft, 3)

    def drain_third():
        z_drain_sum(zlt, 5)
        z_drain_sum(zlt, 6)
        z_drain_sum(*z0[2:])
        for b in (1, 2):
            xy_drain(back[b], 9 + b, R, R)
            xy_done(back[b], 9 + b)

    def drain_tables(h):
        for j in range(4):
            xy_drain(GT.at[h, (t + 4 - j) % 4], 12 + 4 * h + j, RT, RT)
            xy_done(GT.at[h, (t + 4 - j) % 4], 12 + 4 * h + j)

    def drain_back():
        drain_tables(0)
        xy_drain(back[0], 9, R, R)
        xy_done(back[0], 9)

    def first_grads(i, _):
        down_grad(i)
        events(i, [], [], [(down_add, 0)], [(down_add, 1), (xy1_send, *b2_low)])
        return 0

    def second_grads(i, _):
        @pl.when(i < 4)
        def _():
            @pl.when(i == 3)
            def _():
                out_copy.wait()

            down_act(i)

        events(
            i,
            [(down_add, 2)],
            [(down_add, 3), (xy1_send, *b2_high), (drain_late,)],
            [],
            [(xy1_add, *b2_low), (up_add, 0)],
            [(up_add, 1), (xy1_send, *b1_low)],
        )

        @pl.when(i >= 1)
        def _():
            up_grad(i - 1)

        return 0

    def third_grads(i, _):
        up_act(i)
        events(
            i,
            [(xy1_add, *b2_high), (up_add, 2)],
            [(up_add, 3), (xy2_add, *b2_low)],
            [],
            [(xy1_send, *b1_high)],
        )
        return 0

    def fourth_grads(i, _):
        heads_back(i)
        events(
            i,
            [(xy1_add, *b1_low), (xy2_add, *b2_high), (z_send, *z2)],
            [(in_add, 0)],
            [(xy2_add, *b1_high), (zk_send, *z1, 2), (zk_send, *z1, 3), (zf_sum, *zf2), (xy1_send, *f2)],
        )

        @pl.when(i < 3)
        def _():
            in_grad(i)

        events(
            i,
            [],
            [
                (xy1_add, *b1_high),
                (xy2_add, *b1_low),
                (zk_send, *z1, 0),
                (zk_send, *z1, 1),
                (in_add, 1),
                (xy1_send, *b0_low),
            ],
        )
        return 0

    lax.fori_loop(0, 4, first_grads, 0)
    lax.fori_loop(0, 5, second_grads, 0)
    lax.fori_loop(0, 4, third_grads, 0)
    norm_back()
    lax.fori_loop(0, 4, fourth_grads, 0)
    hidden_copy = pltpu.make_async_copy(res, grad_hidden, loc.at[9])
    hidden_copy.start()
    xy1_add(*b0_low)
    xy1_add(*f2)
    in_add(2)
    table_grad(0)
    table_grad(1)
    table_add(0)
    in_grad(3)
    table_add(1)
    xy1_send(*table1)
    xy2_add(*b0_low)
    xy2_add(*f2)
    in_add(3)
    z_sum(*z2)
    xy1_add(*table1)
    xy1_send(*b0_q2)
    z_sum(*z1)
    xy2_add(*table1)
    z_send(*zt1)
    xy1_send(*b0_q3)
    ag_own(2)
    xy1_add(*b0_q2)
    zf_sum(*zft)
    xy1_send(*ft)
    z_sum(*zt1)
    table_out(1)
    ag_relay(2)
    drain_first()
    xy1_add(*ft)
    ag_own(1)
    xy1_add(*b0_q3)
    xy2_add(*b0_q2)
    xy2_add(*ft)
    table_out(0)
    for k in range(3):
        zk_send(*z0, k)
    ag_relay(1)
    xy2_add(*b0_q3)
    zk_send(*z0, 3)
    table_in(1, 1)
    table_relay(1, 0)
    table_in(1, 2)
    table_in(1, 3)
    table_in(0, 1)
    table_relay(0, 0)
    table_in(0, 2)
    table_in(0, 3)
    ag_finish(2)
    drain_second()
    table_relay(1, 1)
    table_relay(1, 2)
    table_relay(1, 3)
    ag_finish(1)
    table_relay(0, 1)
    table_relay(0, 2)
    table_relay(0, 3)
    table_finish(1, 0)
    table_finish(1, 1)
    z_sum(*z0)
    ag_own(0)
    table_finish(1, 2)
    table_finish(1, 3)
    table_finish(0, 0)
    table_finish(0, 1)
    table_finish(0, 2)
    table_finish(0, 3)
    ag_relay(0)
    drain_third()
    drain_tables(1)
    ag_finish(0)

    drain_back()


def finish(
    G,
    GT,
    made_out,
    made_hidden,
    layer_out,
    grad_hidden,
    table_x,
    table_y,
    in_w,
    out_w,
    up_w,
    down_w,
    in_b,
    out_b,
    up_b,
    down_b,
    gain,
    nbias,
    wide_w,
    wide_t,
    full_w,
    full_t,
    held_out,
    held_hidden,
    sem_in,
    sem_out,
):
    t = lax.axis_index("tensor")
    places = [in_w.at[0], in_w.at[1], in_w.at[2], out_w]
    places += [ref.at[pl.ds(192 * i, 192)] for ref in (up_w, down_w) for i in range(4)]
    tables = [ref.at[pl.ds(256 * i, 256)] for ref in (table_x, table_y) for i in range(4)]
    ins = [pltpu.make_async_copy(GT.at[i], wide_t.at[i], sem_in.at[12 + i]) for i in range(8)]
    ins = [pltpu.make_async_copy(G.at[i], wide_w.at[i], sem_in.at[i]) for i in range(12)] + ins
    outs = [pltpu.make_async_copy(full_w.at[i], places[i], sem_out.at[i]) for i in range(12)]
    outs += [pltpu.make_async_copy(full_t.at[i], tables[i], sem_out.at[12 + i]) for i in range(8)]
    ins += [
        pltpu.make_async_copy(made_hidden, held_hidden, sem_in.at[20]),
        pltpu.make_async_copy(made_out, held_out, sem_in.at[21]),
    ]
    outs += [
        pltpu.make_async_copy(held_hidden, grad_hidden, sem_out.at[20]),
        pltpu.make_async_copy(held_out, layer_out, sem_out.at[21]),
    ]
    for copy in ins:
        copy.start()
    for i in range(12):
        ins[i].wait()
        full_w[i] = wide_w[i].astype(f32)
        outs[i].start()
    for i in range(8):
        ins[12 + i].wait()
        full_t[i] = wide_t[i].astype(f32)
        if i == 3:
            small = wide_t[3, 240:256].astype(f32)
            full_t[3, 240:256, :] = jnp.zeros((16, 768), f32)
            gain[...] = small[2:4]
            nbias[...] = small[4:6]
            out_b[...] = small[0]
            down_b[...] = small[1]
            level = lax.broadcasted_iota(jnp.int32, (16, 1), 0)
            up_b[...] = jnp.sum(jnp.where(level == 6 + t, small, 0.0), axis=0)
            row = jnp.sum(jnp.where(level == 10 + t, small, 0.0), axis=0, keepdims=True)
            in_b[0:1, :] = row[:, 0:192]
            in_b[1:2, :] = row[:, 384:576]
        outs[12 + i].start()
    for i in (20, 21):
        ins[i].wait()
        outs[i].start()
    for copy in outs:
        copy.wait()


def on_device(
    dp,
    hidden,
    page_boxes,
    lengths,
    table_x,
    table_y,
    in_weight,
    in_bias,
    out_weight,
    out_bias,
    up_weight,
    up_bias,
    down_weight,
    down_bias,
    norm_gain,
    norm_bias,
    cotangent,
):
    blocks = (2, 2, 2, 2)
    vmem = pl.BlockSpec(memory_space=pltpu.VMEM)
    anywhere = pl.BlockSpec(memory_space=pl.ANY)
    dma = pltpu.SemaphoreType.DMA
    count = max(1, (dp // 8).bit_length() - 1)
    V = pltpu.VMEM

    def lands(quarters, rows):
        first, second = V((quarters, 2, rows, 768), bf16), V((quarters, rows, 768), bf16)
        return [first, first, second, second]

    scratch = [
        V((3, 4, *blocks, R, 768), bf16),
        V((4, *blocks, R, 768), bf16),
        V((2048, 768), bf16),
        V((8, *blocks, RT, 768), bf16),
        V((4, 512, 768), bf16),
        V((4, 512, 576), bf16),
        V((4, 512, 192), bf16),
        V((4, 8, 512), f32),
        V((512, 768), bf16),
        V((512, 768), bf16),
        V((512, 768), bf16),
        V((512, 768), bf16),
        V((512, 768), f32),
        V((512, 768), f32),
        V((512, 768), f32),
        V((512, 1), f32),
        V((4, 8, 768), f32),
        V((16, 768), f32),
        V((6, 2, 2, 2, R, 768), bf16),
        V((2, 4, 2, 2, 2, RT, 768), bf16),
        lands(4, R),
        lands(4, R),
        lands(4, XR),
        lands(4, RT),
        lands(1, FR),
        lands(1, RT),
        V((3, 2, R, 768), bf16),
        V((3, 2, R, 768), bf16),
        V((3, 2, XR, 768), bf16),
        V((3, 2, RT, 768), bf16),
        V((3, 2, 2, 2, FR, 768), bf16),
        V((3, 2, 2, 2, RT, 768), bf16),
        V((count, 2, R, 768) if dp > 8 else (8, 128), bf16),
        V((count, 2, RT, 768) if dp > 8 else (8, 128), bf16),
        dma((15,)),
        dma((3,)),
        dma((3,)),
        dma((3, 5, 2)),
        dma((3, 4, 2)),
        dma((2, 5)),
        dma((2, 4)),
        dma((20, 2)),
        dma((20, 6)),
        dma((20,)),
        dma((20,)),
        dma((14,)),
        dma((14,)),
        pltpu.SemaphoreType.REGULAR,
        dma((10, 4)),
        dma((10, 4)),
        dma((8, 3)),
        dma((8, 3)),
        dma((5, count)),
        dma((5, count)),
    ]
    shape = jax.ShapeDtypeStruct
    made_out, made_hidden, G, GT = pl.pallas_call(
        partial(kernel, dp),
        out_shape=(
            shape((512, 768), bf16),
            shape((512, 768), f32),
            shape((3, *blocks, R, 768), bf16),
            shape((2, 4, *blocks, RT, 768), bf16),
        ),
        in_specs=[
            anywhere,
            vmem,
            pl.BlockSpec(memory_space=pltpu.SMEM),
            anywhere,
            anywhere,
            anywhere,
            vmem,
            anywhere,
            vmem,
            anywhere,
            vmem,
            anywhere,
            vmem,
            vmem,
            vmem,
            anywhere,
        ],
        out_specs=(anywhere,) * 4,
        scratch_shapes=scratch,
        compiler_params=pltpu.CompilerParams(
            collective_id=0, has_side_effects=True, vmem_limit_bytes=61 * 2**20
        ),
    )(
        hidden,
        page_boxes.T,
        lengths,
        table_x,
        table_y,
        in_weight.transpose(0, 2, 1).reshape(3, 2, 2, R, 768),
        in_bias,
        out_weight.reshape(2, 2, R, 768),
        out_bias,
        up_weight.reshape(*blocks, R, 768),
        up_bias,
        down_weight.reshape(*blocks, R, 768),
        down_bias,
        norm_gain,
        norm_bias,
        cotangent,
    )
    outs = pl.pallas_call(
        finish,
        out_shape=(
            shape((512, 768), bf16),
            shape((512, 768), f32),
            shape((1024, 768), f32),
            shape((1024, 768), f32),
            shape((3, 192, 768), f32),
            shape((192, 768), f32),
            shape((768, 768), f32),
            shape((768, 768), f32),
            shape((2, 192), f32),
            shape((768,), f32),
            shape((768,), f32),
            shape((768,), f32),
            shape((2, 768), f32),
            shape((2, 768), f32),
        ),
        in_specs=[pl.BlockSpec(memory_space=pltpu.HBM)] * 4,
        out_specs=(anywhere,) * 8 + (vmem,) * 6,
        scratch_shapes=[
            V((12, 192, 768), bf16),
            V((8, 256, 768), bf16),
            V((12, 192, 768), f32),
            V((8, 256, 768), f32),
            V((512, 768), bf16),
            V((512, 768), f32),
            dma((22,)),
            dma((22,)),
        ],
        compiler_params=pltpu.CompilerParams(vmem_limit_bytes=62 * 2**20),
    )(G.reshape(12, 192, 768), GT.reshape(8, 256, 768), made_out, made_hidden)
    out, hidden_grad, tx, ty, in_w, out_w, up_w, down_w, in_b, out_b, up_b, down_b, gains, biases = outs
    in_w = in_w.transpose(0, 2, 1)
    return out, hidden_grad, tx, ty, in_w, in_b, out_w, out_b, up_w, up_b, down_w, down_b, gains, biases


def solution(mesh):
    both = ("dp", "tensor")
    in_specs = (
        P(both, None),
        P(both, None),
        P("dp"),
        P(),
        P(),
        P(None, None, "tensor"),
        P(None, "tensor"),
        P("tensor", None),
        P(),
        P(None, "tensor"),
        P("tensor"),
        P("tensor", None),
        P(),
        P(),
        P(),
        P(both, None),
    )
    out_specs = (
        P(both, None),
        P(both, None),
        P(),
        P(),
        P(None, None, "tensor"),
        P(None, "tensor"),
        P("tensor", None),
        P(),
        P(None, "tensor"),
        P("tensor"),
        P("tensor", None),
        P(),
        P(),
        P(),
    )
    return jax.shard_map(
        partial(on_device, mesh.shape["dp"]),
        mesh=mesh,
        in_specs=in_specs,
        out_specs=out_specs,
        check_vma=False,
    )
```

```python
from functools import partial

import jax
import jax.numpy as jnp
from jax import lax
from jax.experimental import pallas as pl
from jax.experimental.pallas import tpu as pltpu
from jax.sharding import PartitionSpec as P

HEAD = 64
EPS = 1e-12
MESH = pl.DeviceIdType.MESH
f32 = jnp.float32
bf16 = jnp.bfloat16

R = 48
RT = 16
FR = 16
XR = R - FR
ZR = 16


def dot(a, b, ca, cb):
    return lax.dot_general(a, b, (((ca,), (cb,)), ((), ())), preferred_element_type=f32)


def kernel(
    dp,
    hidden,
    boxes,
    lengths,
    tables_x,
    tables_y,
    in_w,
    in_b,
    out_w,
    out_b,
    up_w,
    up_b,
    down_w,
    down_b,
    gain,
    nbias,
    cotangent,
    layer_out,
    grad_hidden,
    G,
    GT,
    W,
    G2,
    pre,
    act,
    gp,
    qkv,
    ctx,
    lse,
    resb,
    midb,
    bgrad,
    hid,
    res,
    total,
    n1,
    r1,
    bias,
    vec,
    core_land,
    core_land_t,
    lands0,
    lands1,
    lands2,
    lands_t,
    lands_f,
    lands_ft,
    zl0,
    zl1,
    zl2,
    zlt,
    zlf,
    zlft,
    extra,
    extra_t,
    loc,
    bs,
    br,
    gzs,
    gzr,
    gds,
    gdr,
    xs,
    xr,
    cs,
    cr,
    ks,
    kr,
    credit,
    rs,
    rr,
    zs,
    zr,
    es,
    er,
):
    d = lax.axis_index("dp")
    t = lax.axis_index("tensor")
    c = d % 2
    x = (d // 2) % 2
    y = (d // 4) % 2
    X = (d + 2 - 4 * x, t)
    Y = (d + 4 - 8 * y, t)
    C = (d + 1 - 2 * c, t)
    extras = []
    step = 8
    while step < dp:
        extras.append((d + step - 2 * step * ((d // step) % 2), t))
        step *= 2

    def remote(src, dst, send, recv, dev):
        return pltpu.make_async_remote_copy(
            src_ref=src, dst_ref=dst, send_sem=send, recv_sem=recv, device_id=dev, device_id_type=MESH
        )

    def wait_recv(ref, sem):
        remote(ref, ref, sem, sem, C).wait_recv()

    def wait_send(ref, sem):
        remote(ref, ref, sem, sem, C).wait_send()

    barrier = pltpu.get_barrier_semaphore()
    zpeers = [(d, (t + j) % 4) for j in range(1, 4)]
    peers = [X, Y, C] + zpeers + extras
    for peer in peers:
        pl.semaphore_signal(barrier, inc=1, device_id=peer, device_id_type=MESH)

    local = [
        pltpu.make_async_copy(in_w.at[pl.ds(0, 2)], W.at[0, t, 0], loc.at[0]),
        pltpu.make_async_copy(tables_x, pre.at[pl.ds(0, 1024)], loc.at[1]),
        pltpu.make_async_copy(tables_y, pre.at[pl.ds(1024, 1024)], loc.at[2]),
        pltpu.make_async_copy(hidden, hid, loc.at[3]),
        pltpu.make_async_copy(out_w, W.at[0, t, 1, 1], loc.at[4]),
        pltpu.make_async_copy(up_w, W.at[1, t], loc.at[5]),
        pltpu.make_async_copy(down_w, W.at[2, t], loc.at[6]),
        pltpu.make_async_copy(in_w.at[2], W.at[0, t, 1, 0], loc.at[7]),
    ]
    for i in (0, 7, 4, 1, 2, 3, 5, 6):
        local[i].start()
    bias[t] = jnp.zeros((8, 768), f32)
    bias[t, 0:1, :] = up_b[...].reshape(1, 768)
    bias[t, 1:2, 0:192] = in_b[0:1, :]
    bias[t, 1:2, 384:576] = in_b[1:2, :]
    def entry_local():
        local[0].wait()
        local[4].wait()
        local[7].wait()

    def entry_barrier():
        pl.semaphore_wait(barrier, len(peers))

    entry_barrier()
    entry_local()

    half = t // 2
    near = t * (1 - half) + (3 - t) * half

    def other(j):
        base = j + 1 - near * ((3 - j) // 3)
        return base * (1 - half) + (3 - base) * half

    def z_own(src, dst, ss, rsem):
        @pl.when(t > 0)
        def _():
            remote(src, dst, ss(0), rsem, (d, t - 1)).start()

        @pl.when(t < 3)
        def _():
            remote(src, dst, ss(1), rsem, (d, t + 1)).start()

    def z_arrive(ref, tp, send, recv):
        wait_recv(ref, recv)

        @pl.when(jnp.logical_and(tp < t, t < 3))
        def _():
            remote(ref, ref, send, recv, (d, t + 1)).start()

        @pl.when(jnp.logical_and(tp > t, t > 0))
        def _():
            remote(ref, ref, send, recv, (d, t - 1)).start()

    def z_drain(ref, ss):
        @pl.when(t > 0)
        def _():
            wait_send(ref, ss(0))

        @pl.when(t < 3)
        def _():
            wait_send(ref, ss(1))

    def z_arrive_drain(ref, tp, send):
        @pl.when(jnp.logical_or(jnp.logical_and(tp < t, t < 3), jnp.logical_and(tp > t, t > 0)))
        def _():
            wait_send(ref, send)

    def xy_own(src, dst, i):
        a, b = src.at[0], src.at[1]
        da, db = dst.at[c, y, x, 0], dst.at[c, y, x, 1]
        remote(a, da, xs.at[i, 0], xr.at[i, 0], X).start()
        remote(b, db, xs.at[i, 1], xr.at[i, 2], Y).start()
        remote(a, da, xs.at[i, 0], xr.at[i, 1], Y).start()
        remote(b, db, xs.at[i, 1], xr.at[i, 3], X).start()

    def xy_relay(ref, i, ra=slice(None), rb=slice(None)):
        a, b = ref.at[c, y, 1 - x, 0, ra], ref.at[c, 1 - y, x, 1, rb]
        wait_recv(a, xr.at[i, 0])
        remote(a, a, xs.at[i, 0], xr.at[i, 4], Y).start()
        wait_recv(b, xr.at[i, 2])
        remote(b, b, xs.at[i, 1], xr.at[i, 5], X).start()

    def xy_finish(ref, i, ra=slice(None), rb=slice(None)):
        wait_recv(ref.at[c, 1 - y, x, 0, ra], xr.at[i, 1])
        wait_recv(ref.at[c, y, 1 - x, 1, rb], xr.at[i, 3])
        wait_recv(ref.at[c, 1 - y, 1 - x, 0, ra], xr.at[i, 4])
        wait_recv(ref.at[c, 1 - y, 1 - x, 1, rb], xr.at[i, 5])
        remote(ref.at[c], ref.at[c], cs.at[i], cr.at[i], C).start()

    def xy_done(ref, i):
        wait_recv(ref.at[1 - c], cr.at[i])

    def xy_drain(ref, i, rows_a, rows_b):
        for h, count in enumerate((rows_a, rows_b)):
            wait_send(pre.at[pl.ds(0, 3 * count)], xs.at[i, h])
        wait_send(ref.at[c], cs.at[i])

    def rows_of(b, h):
        return pl.ds(0, R - ZR) if b + h == 2 else pl.ds(0, R)

    def both(b):
        return rows_of(b, 0), rows_of(b, 1)

    def whole(b, tp):
        return W.at[b, tp, c, :, :, 2 - b, pl.ds(R - ZR, ZR)]

    def whole_own(b):
        z_own(whole(b, t), whole(b, t), lambda k: gds.at[b - 1, k], gdr.at[b - 1, t])

    def whole_in(i):
        b, j = i // 3, i % 3
        z_arrive(whole(b, other(j)), other(j), gds.at[b - 1, 2 + j], gdr.at[b - 1, other(j)])

    def gz_own(b):
        for h in range(2):
            ref = W.at[b, t, c, y, x, h, rows_of(b, h)]
            z_own(ref, ref, lambda k: gzs.at[b, k, h], gzr.at[b, t, h])

    def gz_end(b):
        @pl.when(jnp.logical_or(t == 0, t == 3))
        def _():
            gz_own(b)

    def gz_middle(b):
        @pl.when(jnp.logical_and(t > 0, t < 3))
        def _():
            gz_own(b)

    def e1(i):
        b, j = i // 3, i % 3
        tp = other(j)
        for h in range(2):
            ref = W.at[b, tp, c, y, x, h, rows_of(b, h)]
            z_arrive(ref, tp, gzs.at[b, 2 + j, h], gzr.at[b, tp, h])
            for dev, k in ((X, 0), (Y, 1)) if h == 0 else ((Y, 2), (X, 3)):
                remote(ref, ref, xs.at[i, h], xr.at[i, k], dev).start()

    def e2(i):
        xy_relay(W.at[i // 3, other(i % 3)], i, *both(i // 3))

    def e3(i):
        xy_finish(W.at[i // 3, other(i % 3)], i, *both(i // 3))

    def e4(i):
        xy_done(W.at[i // 3, other(i % 3)], i)

    gz_own(0)
    for j in range(3):
        remote(bias.at[t], bias.at[t], bs.at[j], br.at[2 - j], zpeers[j]).start()

    def one_hot(first, second, levels):
        return ((first == levels).astype(f32) + (second == levels).astype(f32)).astype(bf16)

    levels = lax.broadcasted_iota(jnp.int32, (1024, 1), 0)

    def embed():
        for i in (1, 2, 3):
            local[i].wait()
        horizontal = one_hot(boxes[0:1], boxes[2:3], levels)
        vertical = one_hot(boxes[1:2], boxes[3:4], levels)
        residual = (
            hid[...].astype(f32)
            + dot(horizontal, pre[0:1024, :], 0, 0)
            + dot(vertical, pre[1024:2048, :], 0, 0)
        )
        res[...] = residual
        resb[...] = residual.astype(bf16)
        total[...] = jnp.zeros_like(total)

    embed()
    local[5].wait()
    local[6].wait()
    cot_copy = pltpu.make_async_copy(cotangent, hid, loc.at[3])
    cot_copy.start()

    def biases():
        for j in range(3):
            tz = (t + 3 - j) % 4
            wait_recv(bias.at[tz], br.at[2 - j])

    length = lengths[t]
    visible = lax.broadcasted_iota(jnp.int32, (512, 1), 0) < length
    scaling = HEAD**-0.5

    def project(tp):
        weight = W[0, tp].reshape(768, 768)
        qkv[tp] = (dot(resb[...], weight[0:576], 1, 1) + bias[tp, 1:2, 0:576]).astype(bf16)

    def heads(tp):
        for j in range(3):
            q = qkv[tp, :, j * 64 : (j + 1) * 64]
            k = qkv[tp, :, 192 + j * 64 : 192 + (j + 1) * 64]
            v = qkv[tp, :, 384 + j * 64 : 384 + (j + 1) * 64]
            scores = jnp.where(visible, dot(k, q, 1, 1) * scaling, -1e30)
            top = jnp.max(scores, axis=0, keepdims=True)
            exponent = jnp.exp(scores - top)
            sums = jnp.sum(exponent, axis=0, keepdims=True)
            attend = (exponent * (1.0 / sums)).astype(bf16)
            ctx[tp, :, j * 64 : (j + 1) * 64] = dot(attend, v, 0, 0).astype(bf16)
            lse[tp, j : j + 1, :] = top + jnp.log(sums)
        total[...] += dot(ctx[tp], W[0, tp, 1, 1].reshape(192, 768), 1, 0)

    def up(tp):
        hidden_pre = dot(midb[...], W[1, tp].reshape(768, 768), 1, 0) + bias[tp, 0:1, :]
        cdf = 0.5 * (1.0 + lax.erf(hidden_pre * 0.7071067811865476))
        act[pl.ds(2 * tp, 2)] = (hidden_pre * cdf).astype(bf16).reshape(2, 2, 2, 2, 2, RT, 768)
        slope = cdf + hidden_pre * jnp.exp(-0.5 * hidden_pre * hidden_pre) * 0.3989422804014327
        gp[tp] = slope.astype(bf16)

    def down(tp):
        total[...] += dot(act[pl.ds(2 * tp, 2)].reshape(512, 768), W[2, tp].reshape(768, 768), 1, 0)

    def normalize(value):
        average = jnp.mean(value, axis=-1, keepdims=True)
        centered = value - average
        inverse = lax.rsqrt(jnp.mean(centered * centered, axis=-1, keepdims=True) + EPS)
        return centered * inverse, inverse

    def normalize_back(gradient, normed, inverse, gain_row):
        scaled = gradient * gain_row
        inner = (
            scaled
            - jnp.mean(scaled, axis=-1, keepdims=True)
            - normed * jnp.mean(scaled * normed, axis=-1, keepdims=True)
        )
        return inverse * inner

    def row_sum(value):
        return jnp.sum(value, axis=0, keepdims=True)

    def out_norm():
        normed, inverse = normalize(res[...] + total[...] + out_b[...].reshape(1, 768))
        n1[...] = normed
        r1[...] = inverse
        middle = normed * gain[0:1] + nbias[0:1]
        res[...] = middle
        midb[...] = middle.astype(bf16)
        total[...] = jnp.zeros_like(total)

    def drain_items(b):
        def one(j, _):
            xy_drain(W.at[0, 0], 3 * b + j, *(r.size for r in both(b)))
            return 0

        lax.fori_loop(0, 3, one, 0)

    def drain_z(b):
        for h in range(2):
            ref = W.at[0, 0, 0, 0, 0, 0, rows_of(b, h)]
            z_drain(ref, lambda k: gzs.at[b, k, h])
            for j in range(3):
                z_arrive_drain(ref, other(j), gzs.at[b, 2 + j, h])

    def drain_whole(b):
        z_drain(whole(b, 0), lambda k: gds.at[b - 1, k])
        for j in range(3):
            z_arrive_drain(whole(b, 0), other(j), gds.at[b - 1, 2 + j])

    def events(k, *turns):
        for turn, calls in enumerate(turns):
            if calls:

                @pl.when(k == turn)
                def _(calls=calls):
                    for call, *given in calls:
                        call(*given)

    def quarter(k):
        own = (3 - k) // 3
        return own * t + (1 - own) * other(k - 1)

    e1(0)
    e1(1)
    gz_end(1)
    e2(0)
    e1(2)
    gz_middle(1)
    e2(1)
    biases()

    def attend(k, _):
        tp = quarter(k)
        project(tp)
        events(
            k,
            [(e2, 2)],
            [(e1, 4), (whole_own, 1), (gz_end, 2), (e3, 1)],
            [(e3, 2)],
            [(e1, 7), (e2, 5), (whole_in, 3)],
        )
        heads(tp)
        events(
            k,
            [(e3, 0), (e1, 3), (e4, 0)],
            [(e1, 5), (gz_middle, 2), (e2, 3), (e4, 1)],
            [(e2, 4), (e1, 6), (e4, 2)],
            [(e1, 8), (whole_own, 2), (e3, 3)],
        )
        return 0

    def widen(k, _):
        up(quarter(k))
        events(
            k,
            [(e4, 3), (whole_in, 4), (e3, 4)],
            [(e2, 7), (whole_in, 5), (e3, 5), (e4, 4), (whole_in, 6)],
            [(e2, 8), (whole_in, 7), (e3, 6), (e4, 5)],
        )
        return 0

    def drain_early():
        drain_items(0)
        drain_items(1)
        for b in range(3):
            drain_z(b)
        drain_whole(1)

    def drain_late():
        drain_items(2)
        drain_whole(2)

    def narrow(k, _):
        down(quarter(k))
        events(k, [(e3, 7), (whole_in, 8), (drain_early,), (e4, 6)], [(e3, 8), (e4, 7)], [(e4, 8)])
        return 0

    lax.fori_loop(0, 4, attend, 0)
    out_norm()
    e2(6)
    lax.fori_loop(0, 4, widen, 0)
    lax.fori_loop(0, 4, narrow, 0)

    normed, inverse = normalize(res[...] + total[...] + down_b[...].reshape(1, 768))
    pre[1536:2048, :] = (normed * gain[1:2] + nbias[1:2]).astype(bf16)
    out_copy = pltpu.make_async_copy(pre.at[pl.ds(1536, 512)], layer_out, loc.at[8])
    out_copy.start()
    cot_copy.wait()
    gradient = hid[...].astype(f32)
    final_grad = normalize_back(gradient, normed, inverse, gain[1:2])
    res[...] = final_grad
    bgrad[...] = final_grad.astype(bf16)
    vec[...] = jnp.zeros_like(vec)
    vec[1:2, :] = row_sum(bgrad[...].astype(f32))
    vec[3:4, :] = row_sum(gradient * normed)
    vec[5:6, :] = row_sum(gradient)

    def core_send(ref, n, tp):
        remote(ref.at[tp, 1 - c], core_land.at[n % 6], ks.at[n // 4], kr.at[n], C).start()

    def core_add(ref, n, tp):
        wait_recv(core_land.at[n % 6], kr.at[n])
        ref[tp, c] = ref[tp, c] + core_land[n % 6]

    def free():
        pl.semaphore_signal(credit, inc=1, device_id=C, device_id_type=MESH)

    def wait_free():
        pl.semaphore_wait(credit, 1)

    def xy1_send(ref, part, rows, lands, lp, g):
        a = ref.at[part, c, :, 1 - x, 0, rows]
        b = ref.at[part, c, 1 - y, :, 1, rows]
        remote(a, lands[0].at[lp], rs.at[g], rr.at[g, 0], X).start()
        remote(b, lands[1].at[lp], rs.at[g], rr.at[g, 1], Y).start()

    def xy1_add(ref, part, rows, lands, lp, g):
        wait_recv(lands[0].at[lp], rr.at[g, 0])
        ref[part, c, :, x, 0, rows] = ref[part, c, :, x, 0, rows] + lands[0][lp]
        remote(ref.at[part, c, 1 - y, x, 0, rows], lands[3].at[lp], rs.at[g], rr.at[g, 3], Y).start()
        wait_recv(lands[1].at[lp], rr.at[g, 1])
        ref[part, c, y, :, 1, rows] = ref[part, c, y, :, 1, rows] + lands[1][lp]
        remote(ref.at[part, c, y, 1 - x, 1, rows], lands[2].at[lp], rs.at[g], rr.at[g, 2], X).start()

    def xy2_add(ref, part, rows, lands, lp, g):
        wait_recv(lands[3].at[lp], rr.at[g, 3])
        ref[part, c, y, x, 0, rows] = ref[part, c, y, x, 0, rows] + lands[3][lp]
        wait_recv(lands[2].at[lp], rr.at[g, 2])
        ref[part, c, y, x, 1, rows] = ref[part, c, y, x, 1, rows] + lands[2][lp]

    def xy_rs_drain(lands, lp, g):
        count = 1
        for extent in lands[2].at[lp].shape[:-1]:
            count *= extent
        wait_send(pre.at[pl.ds(0, 6 * count)], rs.at[g])

    def z_send(ref, rows, land, g):
        for j in range(1, 4):
            k = (t + j) % 4
            remote(ref.at[k, c, y, x, :, rows], land.at[j - 1], zs.at[g], zr.at[g, j - 1], (d, k)).start()

    def zk_send(ref, rows, land, g, k):
        @pl.when(t != k)
        def _():
            slot = (k - t + 3) % 4
            remote(ref.at[k, c, y, x, :, rows], land.at[slot], zs.at[g], zr.at[g, slot], (d, k)).start()

    def z_sum(ref, rows, land, g):
        for j in range(3):
            wait_recv(land.at[j], zr.at[g, j])
        value = ref[t, c, y, x, :, rows].astype(f32)
        for j in range(3):
            value = value + land[j].astype(f32)
        ref[t, c, y, x, :, rows] = value.astype(bf16)

    def z_drain_sum(land, g):
        wait_send(land, zs.at[g])

    def zf_send(ref, rows, land, g, k):
        @pl.when(t != k)
        def _():
            slot = (k - t + 3) % 4
            remote(ref.at[k, c, :, :, :, rows], land.at[slot], zs.at[g], zr.at[g, slot], (d, k)).start()

    def zf_sum(ref, rows, land, g):
        for j in range(3):
            wait_recv(land.at[j], zr.at[g, j])
        value = ref[t, c, :, :, :, rows].astype(f32)
        for j in range(3):
            value = value + land[j].astype(f32)
        ref[t, c, :, :, :, rows] = value.astype(bf16)

    def across(ref, land, g):
        for i, peer in enumerate(extras):
            copy = remote(ref, land.at[i], es.at[g, i], er.at[g, i], peer)
            copy.start()
            copy.wait()
            ref[...] = ref[...] + land[i]

    g1 = W.at[2]
    g0 = W.at[1]
    low, high, every = pl.ds(0, 2), pl.ds(2, 2), pl.ds(0, 4)
    rows_x, rows_f, rows, rows_t = pl.ds(0, XR), pl.ds(XR, FR), pl.ds(0, R), pl.ds(0, RT)
    tables = [act.at[pl.ds(0, 4)], act.at[pl.ds(4, 4)]]
    b2_low, b2_high = (G2, low, rows_x, lands2, low, 0), (G2, high, rows_x, lands2, high, 1)
    b1_low, b1_high = (g1, low, rows, lands1, low, 2), (g1, high, rows, lands1, high, 3)
    b0_low = (g0, low, rows, lands0, low, 4)
    b0_q2, b0_q3 = (g0, pl.ds(2, 1), rows, lands0, pl.ds(2, 1), 5), (g0, pl.ds(3, 1), rows, lands0, pl.ds(3, 1), 6)
    table1 = (tables[1], every, rows_t, lands_t, every, 8)
    f2, ft = (G2, t, rows_f, lands_f, 0, 9), (tables[0], t, rows_t, lands_ft, 0, 7)
    z0, z1, z2 = (g0, rows, zl0, 0), (g1, rows, zl1, 1), (G2, rows_x, zl2, 2)
    zt1 = (tables[1], rows_t, zlt, 4)
    zf2, zft = (G2, rows_f, zlf, 7), (tables[0], rows_t, zlft, 3)

    def span(i):
        return pl.ds(pl.multiple_of(i * 512, 512), 512)

    def down_grad(i):
        activated = act[pl.ds(2 * i, 2)].reshape(512, 768)
        G2[i] = dot(activated, bgrad[...], 0, 0).astype(bf16).reshape(2, 2, 2, 2, R, 768)
        core_send(G2, i, i)

    def down_act(i):
        grad = dot(bgrad[...], W[2, i].reshape(768, 768), 1, 1).astype(bf16)
        pre_grad = (grad.astype(f32) * gp[i].astype(f32)).astype(bf16)
        pre[span(i), :] = pre_grad
        vec[pl.ds(6 + i, 1), :] = row_sum(pre_grad.astype(f32))

    def down_add(i):
        core_add(G2, i, i)
        free()
        zf_send(*zf2, i)

    def up_grad(i):
        g1[i] = dot(midb[...], pre[span(i), :], 0, 0).astype(bf16).reshape(2, 2, 2, 2, R, 768)

        @pl.when(i >= 2)
        def _():
            wait_free()

        core_send(g1, 4 + i, i)

    def up_act(i):
        res[...] += dot(pre[span(i), :], W[1, i].reshape(768, 768), 1, 1)

    def up_add(i):
        core_add(g1, 4 + i, i)
        if i < 2:
            free()

    def norm_back():
        normed = n1[...]
        gradient = res[...]
        residual_grad = normalize_back(gradient, normed, r1[...], gain[0:1])
        res[...] = residual_grad
        bgrad[...] = residual_grad.astype(bf16)
        vec[0:1, :] = row_sum(bgrad[...].astype(f32))
        vec[2:3, :] = row_sum(gradient * normed)
        vec[4:5, :] = row_sum(gradient)

    def heads_back(i):
        context_grad = dot(bgrad[...], W[0, i, 1, 1].reshape(192, 768), 1, 1).astype(bf16)
        for j in range(3):
            q = qkv[i, :, j * 64 : (j + 1) * 64]
            k = qkv[i, :, 192 + j * 64 : 192 + (j + 1) * 64]
            v = qkv[i, :, 384 + j * 64 : 384 + (j + 1) * 64]
            dc = context_grad[:, j * 64 : (j + 1) * 64]
            scores = jnp.where(visible, dot(k, q, 1, 1) * scaling, -1e30)
            attend = jnp.exp(scores - lse[i, j : j + 1, :])
            prob_grad = dot(v, dc, 1, 1)
            inner = jnp.sum(prob_grad * attend, axis=0, keepdims=True)
            score_grad = (attend * (prob_grad - inner)).astype(bf16)
            value_grad = dot(attend.astype(bf16), dc, 1, 0)
            key_grad = dot(score_grad, q, 1, 0) * scaling
            query_grad = dot(score_grad, k, 0, 0) * scaling
            qkv[i, :, j * 64 : (j + 1) * 64] = query_grad.astype(bf16)
            qkv[i, :, 192 + j * 64 : 192 + (j + 1) * 64] = key_grad.astype(bf16)
            qkv[i, :, 384 + j * 64 : 384 + (j + 1) * 64] = value_grad.astype(bf16)
        grads = qkv[i]
        res[...] += dot(grads, W[0, i].reshape(768, 768)[0:576], 1, 0)
        vec[pl.ds(10 + i, 1), 0:576] = row_sum(grads.astype(f32))

    def in_grad(i):
        made = dot(qkv[i], resb[...], 0, 0).astype(bf16)
        g0[i, 0] = made[0:384].reshape(2, 2, 2, R, 768)
        g0[i, 1, 0] = made[384:576].reshape(2, 2, R, 768)
        g0[i, 1, 1] = dot(ctx[i], bgrad[...], 0, 0).astype(bf16).reshape(2, 2, R, 768)
        wait_free()
        core_send(g0, 8 + i, i)

    def in_add(i):
        core_add(g0, 8 + i, i)

    def table_grad(h):
        if h == 0:
            hid[...] = res[...].astype(bf16)
        hot = one_hot(boxes[h : h + 1], boxes[h + 2 : h + 3], levels)
        made = dot(hot, hid[...], 1, 0).astype(bf16)
        act[4 * h : 4 * h + 4] = made.reshape(4, 2, 2, 2, 2, RT, 768)
        if h == 0:
            act[3, 1, 1, 1, 1] = vec[...].astype(bf16)
        remote(tables[h].at[:, 1 - c], core_land_t.at[h], ks.at[3], kr.at[12 + h], C).start()

    def table_add(h):
        wait_recv(core_land_t.at[h], kr.at[12 + h])
        tables[h][:, c] = tables[h][:, c] + core_land_t[h]
        if h == 0:
            for k in range(4):
                zf_send(*zft, k)

    F = [g0.at[t, c, y, x], g1.at[t, c, y, x], G2.at[t, c, y, x]]
    F += [ref.at[t, c, y, x] for ref in tables]
    back = [G.at[0], G.at[1], G.at[2], GT.at[0, t], GT.at[1, t]]
    item = [9, 10, 11, 12, 16]
    kept = [pltpu.make_async_copy(F[b], back[b].at[c, y, x], loc.at[10 + b]) for b in range(5)]

    def ag_own(b):
        across(F[b], extra_t if b >= 3 else extra, b)
        kept[b].start()
        xy_own(F[b], back[b], item[b])

    def ag_relay(b):
        xy_relay(back[b], item[b])

    def ag_finish(b):
        kept[b].wait()
        xy_finish(back[b], item[b])

    def table_out(h):
        ag_own(3 + h)
        for j in range(1, 4):
            send, recv = zs.at[5 + h], zr.at[5 + h, j - 1]
            remote(F[3 + h], GT.at[h, t, c, y, x], send, recv, (d, (t + j) % 4)).start()

    def table_in(h, j):
        ref = GT.at[h, (t + 4 - j) % 4]
        wait_recv(ref.at[c, y, x], zr.at[5 + h, j - 1])
        xy_own(ref.at[c, y, x], ref, 12 + 4 * h + j)

    def table_relay(h, j):
        xy_relay(GT.at[h, (t + 4 - j) % 4], 12 + 4 * h + j)

    def table_finish(h, j):
        if j == 0:
            kept[3 + h].wait()
        xy_finish(GT.at[h, (t + 4 - j) % 4], 12 + 4 * h + j)

    def drain_first():
        for j in range(3):
            wait_send(bias.at[0], bs.at[j])
        for n in range(3):
            wait_send(pre.at[pl.ds(0, 1536)], ks.at[n])
        wait_send(core_land_t, ks.at[3])
        for group in (b2_low, b2_high, b1_low, b1_high, b0_low, f2, table1):
            xy_rs_drain(*group[3:])
        for group in (z1, z2):
            z_drain_sum(*group[2:])
        z_drain_sum(zlf, 7)

    def drain_second():
        hidden_copy.wait()
        for group in (b0_q2, b0_q3, ft):
            xy_rs_drain(*group[3:])
        z_drain_sum(zlt, 4)
        z_drain_sum(zlft, 3)

    def drain_third():
        z_drain_sum(zlt, 5)
        z_drain_sum(zlt, 6)
        z_drain_sum(*z0[2:])
        for b in (1, 2):
            xy_drain(back[b], 9 + b, R, R)
            xy_done(back[b], 9 + b)

    def drain_tables(h):
        for j in range(4):
            xy_drain(GT.at[h, (t + 4 - j) % 4], 12 + 4 * h + j, RT, RT)
            xy_done(GT.at[h, (t + 4 - j) % 4], 12 + 4 * h + j)

    def drain_back():
        drain_tables(0)
        xy_drain(back[0], 9, R, R)
        xy_done(back[0], 9)

    def first_grads(i, _):
        down_grad(i)
        events(i, [], [], [(down_add, 0)], [(down_add, 1), (xy1_send, *b2_low)])
        return 0

    def second_grads(i, _):
        @pl.when(i < 4)
        def _():
            @pl.when(i == 3)
            def _():
                out_copy.wait()

            down_act(i)

        events(
            i,
            [(down_add, 2)],
            [(down_add, 3), (xy1_send, *b2_high), (drain_late,)],
            [],
            [(xy1_add, *b2_low), (up_add, 0)],
            [(up_add, 1), (xy1_send, *b1_low)],
        )

        @pl.when(i >= 1)
        def _():
            up_grad(i - 1)

        return 0

    def third_grads(i, _):
        up_act(i)
        events(
            i,
            [(xy1_add, *b2_high), (up_add, 2)],
            [(up_add, 3), (xy2_add, *b2_low)],
            [],
            [(xy1_send, *b1_high)],
        )
        return 0

    def fourth_grads(i, _):
        heads_back(i)
        events(
            i,
            [(xy1_add, *b1_low), (xy2_add, *b2_high), (z_send, *z2)],
            [(in_add, 0)],
            [(xy2_add, *b1_high), (zk_send, *z1, 2), (zk_send, *z1, 3), (zf_sum, *zf2), (xy1_send, *f2)],
        )

        @pl.when(i < 3)
        def _():
            in_grad(i)

        events(
            i,
            [],
            [
                (xy1_add, *b1_high),
                (xy2_add, *b1_low),
                (zk_send, *z1, 0),
                (zk_send, *z1, 1),
                (in_add, 1),
                (xy1_send, *b0_low),
            ],
        )
        return 0

    lax.fori_loop(0, 4, first_grads, 0)
    lax.fori_loop(0, 5, second_grads, 0)
    lax.fori_loop(0, 4, third_grads, 0)
    norm_back()
    lax.fori_loop(0, 4, fourth_grads, 0)
    hidden_copy = pltpu.make_async_copy(res, grad_hidden, loc.at[9])
    hidden_copy.start()
    xy1_add(*b0_low)
    xy1_add(*f2)
    in_add(2)
    table_grad(0)
    table_grad(1)
    table_add(0)
    in_grad(3)
    table_add(1)
    xy1_send(*table1)
    xy2_add(*b0_low)
    xy2_add(*f2)
    in_add(3)
    z_sum(*z2)
    xy1_add(*table1)
    xy1_send(*b0_q2)
    z_sum(*z1)
    xy2_add(*table1)
    z_send(*zt1)
    xy1_send(*b0_q3)
    ag_own(2)
    xy1_add(*b0_q2)
    zf_sum(*zft)
    xy1_send(*ft)
    z_sum(*zt1)
    table_out(1)
    ag_relay(2)
    drain_first()
    xy1_add(*ft)
    ag_own(1)
    xy1_add(*b0_q3)
    xy2_add(*b0_q2)
    xy2_add(*ft)
    table_out(0)
    for k in range(3):
        zk_send(*z0, k)
    ag_relay(1)
    xy2_add(*b0_q3)
    zk_send(*z0, 3)
    table_in(1, 1)
    table_relay(1, 0)
    table_in(1, 2)
    table_in(1, 3)
    table_in(0, 1)
    table_relay(0, 0)
    table_in(0, 2)
    table_in(0, 3)
    ag_finish(2)
    drain_second()
    table_relay(1, 1)
    table_relay(1, 2)
    table_relay(1, 3)
    ag_finish(1)
    table_relay(0, 1)
    table_relay(0, 2)
    table_relay(0, 3)
    table_finish(1, 0)
    table_finish(1, 1)
    z_sum(*z0)
    ag_own(0)
    table_finish(1, 2)
    table_finish(1, 3)
    table_finish(0, 0)
    table_finish(0, 1)
    table_finish(0, 2)
    table_finish(0, 3)
    ag_relay(0)
    drain_third()
    drain_tables(1)
    ag_finish(0)

    drain_back()


def finish(
    G,
    GT,
    made_out,
    made_hidden,
    layer_out,
    grad_hidden,
    table_x,
    table_y,
    in_w,
    out_w,
    up_w,
    down_w,
    in_b,
    out_b,
    up_b,
    down_b,
    gain,
    nbias,
    wide_w,
    wide_t,
    full_w,
    full_t,
    held_out,
    held_hidden,
    sem_in,
    sem_out,
):
    t = lax.axis_index("tensor")
    places = [in_w.at[0], in_w.at[1], in_w.at[2], out_w]
    places += [ref.at[pl.ds(192 * i, 192)] for ref in (up_w, down_w) for i in range(4)]
    tables = [ref.at[pl.ds(256 * i, 256)] for ref in (table_x, table_y) for i in range(4)]
    ins = [pltpu.make_async_copy(GT.at[i], wide_t.at[i], sem_in.at[12 + i]) for i in range(8)]
    ins = [pltpu.make_async_copy(G.at[i], wide_w.at[i], sem_in.at[i]) for i in range(12)] + ins
    outs = [pltpu.make_async_copy(full_w.at[i], places[i], sem_out.at[i]) for i in range(12)]
    outs += [pltpu.make_async_copy(full_t.at[i], tables[i], sem_out.at[12 + i]) for i in range(8)]
    ins += [
        pltpu.make_async_copy(made_hidden, held_hidden, sem_in.at[20]),
        pltpu.make_async_copy(made_out, held_out, sem_in.at[21]),
    ]
    outs += [
        pltpu.make_async_copy(held_hidden, grad_hidden, sem_out.at[20]),
        pltpu.make_async_copy(held_out, layer_out, sem_out.at[21]),
    ]
    for copy in ins:
        copy.start()
    for i in range(12):
        ins[i].wait()
        full_w[i] = wide_w[i].astype(f32)
        outs[i].start()
    for i in range(8):
        ins[12 + i].wait()
        full_t[i] = wide_t[i].astype(f32)
        if i == 3:
            small = wide_t[3, 240:256].astype(f32)
            full_t[3, 240:256, :] = jnp.zeros((16, 768), f32)
            gain[...] = small[2:4]
            nbias[...] = small[4:6]
            out_b[...] = small[0]
            down_b[...] = small[1]
            level = lax.broadcasted_iota(jnp.int32, (16, 1), 0)
            up_b[...] = jnp.sum(jnp.where(level == 6 + t, small, 0.0), axis=0)
            row = jnp.sum(jnp.where(level == 10 + t, small, 0.0), axis=0, keepdims=True)
            in_b[0:1, :] = row[:, 0:192]
            in_b[1:2, :] = row[:, 384:576]
        outs[12 + i].start()
    for i in (20, 21):
        ins[i].wait()
        outs[i].start()
    for copy in outs:
        copy.wait()


def on_device(
    dp,
    hidden,
    page_boxes,
    lengths,
    table_x,
    table_y,
    in_weight,
    in_bias,
    out_weight,
    out_bias,
    up_weight,
    up_bias,
    down_weight,
    down_bias,
    norm_gain,
    norm_bias,
    cotangent,
):
    blocks = (2, 2, 2, 2)
    vmem = pl.BlockSpec(memory_space=pltpu.VMEM)
    anywhere = pl.BlockSpec(memory_space=pl.ANY)
    dma = pltpu.SemaphoreType.DMA
    count = max(1, (dp // 8).bit_length() - 1)
    V = pltpu.VMEM

    def lands(quarters, rows):
        first, second = V((quarters, 2, rows, 768), bf16), V((quarters, rows, 768), bf16)
        return [first, first, second, second]

    scratch = [
        V((3, 4, *blocks, R, 768), bf16),
        V((4, *blocks, R, 768), bf16),
        V((2048, 768), bf16),
        V((8, *blocks, RT, 768), bf16),
        V((4, 512, 768), bf16),
        V((4, 512, 576), bf16),
        V((4, 512, 192), bf16),
        V((4, 8, 512), f32),
        V((512, 768), bf16),
        V((512, 768), bf16),
        V((512, 768), bf16),
        V((512, 768), bf16),
        V((512, 768), f32),
        V((512, 768), f32),
        V((512, 768), f32),
        V((512, 1), f32),
        V((4, 8, 768), f32),
        V((16, 768), f32),
        V((6, 2, 2, 2, R, 768), bf16),
        V((2, 4, 2, 2, 2, RT, 768), bf16),
        lands(4, R),
        lands(4, R),
        lands(4, XR),
        lands(4, RT),
        lands(1, FR),
        lands(1, RT),
        V((3, 2, R, 768), bf16),
        V((3, 2, R, 768), bf16),
        V((3, 2, XR, 768), bf16),
        V((3, 2, RT, 768), bf16),
        V((3, 2, 2, 2, FR, 768), bf16),
        V((3, 2, 2, 2, RT, 768), bf16),
        V((count, 2, R, 768) if dp > 8 else (8, 128), bf16),
        V((count, 2, RT, 768) if dp > 8 else (8, 128), bf16),
        dma((15,)),
        dma((3,)),
        dma((3,)),
        dma((3, 5, 2)),
        dma((3, 4, 2)),
        dma((2, 5)),
        dma((2, 4)),
        dma((20, 2)),
        dma((20, 6)),
        dma((20,)),
        dma((20,)),
        dma((4,)),
        dma((14,)),
        pltpu.SemaphoreType.REGULAR,
        dma((10,)),
        dma((10, 4)),
        dma((8,)),
        dma((8, 3)),
        dma((5, count)),
        dma((5, count)),
    ]
    shape = jax.ShapeDtypeStruct
    made_out, made_hidden, G, GT = pl.pallas_call(
        partial(kernel, dp),
        out_shape=(
            shape((512, 768), bf16),
            shape((512, 768), f32),
            shape((3, *blocks, R, 768), bf16),
            shape((2, 4, *blocks, RT, 768), bf16),
        ),
        in_specs=[
            anywhere,
            vmem,
            pl.BlockSpec(memory_space=pltpu.SMEM),
            anywhere,
            anywhere,
            anywhere,
            vmem,
            anywhere,
            vmem,
            anywhere,
            vmem,
            anywhere,
            vmem,
            vmem,
            vmem,
            anywhere,
        ],
        out_specs=(anywhere,) * 4,
        scratch_shapes=scratch,
        compiler_params=pltpu.CompilerParams(
            collective_id=0, has_side_effects=True, vmem_limit_bytes=61 * 2**20
        ),
    )(
        hidden,
        page_boxes.T,
        lengths,
        table_x,
        table_y,
        in_weight.transpose(0, 2, 1).reshape(3, 2, 2, R, 768),
        in_bias,
        out_weight.reshape(2, 2, R, 768),
        out_bias,
        up_weight.reshape(*blocks, R, 768),
        up_bias,
        down_weight.reshape(*blocks, R, 768),
        down_bias,
        norm_gain,
        norm_bias,
        cotangent,
    )
    outs = pl.pallas_call(
        finish,
        out_shape=(
            shape((512, 768), bf16),
            shape((512, 768), f32),
            shape((1024, 768), f32),
            shape((1024, 768), f32),
            shape((3, 192, 768), f32),
            shape((192, 768), f32),
            shape((768, 768), f32),
            shape((768, 768), f32),
            shape((2, 192), f32),
            shape((768,), f32),
            shape((768,), f32),
            shape((768,), f32),
            shape((2, 768), f32),
            shape((2, 768), f32),
        ),
        in_specs=[pl.BlockSpec(memory_space=pltpu.HBM)] * 4,
        out_specs=(anywhere,) * 8 + (vmem,) * 6,
        scratch_shapes=[
            V((12, 192, 768), bf16),
            V((8, 256, 768), bf16),
            V((12, 192, 768), f32),
            V((8, 256, 768), f32),
            V((512, 768), bf16),
            V((512, 768), f32),
            dma((22,)),
            dma((22,)),
        ],
        compiler_params=pltpu.CompilerParams(vmem_limit_bytes=62 * 2**20),
    )(G.reshape(12, 192, 768), GT.reshape(8, 256, 768), made_out, made_hidden)
    out, hidden_grad, tx, ty, in_w, out_w, up_w, down_w, in_b, out_b, up_b, down_b, gains, biases = outs
    in_w = in_w.transpose(0, 2, 1)
    return out, hidden_grad, tx, ty, in_w, in_b, out_w, out_b, up_w, up_b, down_w, down_b, gains, biases


def solution(mesh):
    both = ("dp", "tensor")
    in_specs = (
        P(both, None),
        P(both, None),
        P("dp"),
        P(),
        P(),
        P(None, None, "tensor"),
        P(None, "tensor"),
        P("tensor", None),
        P(),
        P(None, "tensor"),
        P("tensor"),
        P("tensor", None),
        P(),
        P(),
        P(),
        P(both, None),
    )
    out_specs = (
        P(both, None),
        P(both, None),
        P(),
        P(),
        P(None, None, "tensor"),
        P(None, "tensor"),
        P("tensor", None),
        P(),
        P(None, "tensor"),
        P("tensor"),
        P("tensor", None),
        P(),
        P(),
        P(),
    )
    return jax.shard_map(
        partial(on_device, mesh.shape["dp"]),
        mesh=mesh,
        in_specs=in_specs,
        out_specs=out_specs,
        check_vma=False,
    )
```
